256 devices in a mesh: dp: 32 (over x, z), tensor: 8 (over y, core).
Axes of the slice: x: 4, y: 4, z: 8, core: 2. Of those that a mesh axis runs over, the one named last changes fastest.
Arguments:
- q_lat: bfloat16 [1024, 65536], P('dp', 'tensor'), may hold values from -48 to 48
- q_rope: bfloat16 [1024, 8192], P('dp', 'tensor'), may hold values from -6 to 6
- fresh_lat: bfloat16 [1024, 512], P('dp'), may hold values from -4 to 4
- fresh_rope: bfloat16 [1024, 64], P('dp'), may hold values from -6 to 6
- cache_lat: bfloat16 [2048, 128, 512], P('dp'), may hold values from -6 to 6
- cache_rope: bfloat16 [2048, 64, 128], P('dp'), may hold values from -6 to 6
- page_table: int32 [32, 2, 32], P('dp'), may hold values from 0 to 63, as said below
- hit_len: int32 [32, 2], P('dp'), may hold values from 1 to 4096, as said below
- fresh_len: int32 [32, 2], P('dp'), may hold values from 1 to 24, 32 in all within a row
- w_uv: bfloat16 [128, 512, 128], P('tensor'), may hold values from -0.25 to 0.25
- w_o: bfloat16 [16384, 7168], P('tensor', 'dp'), may hold values from -0.046875 to 0.046875
- resid: bfloat16 [1024, 7168], P('tensor', 'dp'), may hold values from -5 to 5
- norm_gain: bfloat16 [7168], P('dp'), may hold values from 0.099609375 to 1.8984375
- w_gate: bfloat16 [7168, 18432], P('dp', 'tensor'), may hold values from -0.0625 to 0.0625
- w_up: bfloat16 [7168, 18432], P('dp', 'tensor'), may hold values from -0.0625 to 0.0625
- w_down: bfloat16 [18432, 7168], P('tensor', 'dp'), may hold values from -0.046875 to 0.046875
Outputs:
- mixed: bfloat16 [1024, 7168], P('tensor', 'dp')
The draws below stay inside these ranges and needn't reach their ends.
Inputs may be any that keep to these rules, and one draw needn't show every extreme that they name: `page_table`: each group's row of the table lists every number from 0 to 63 once. `hit_len`: some request of some group has the full 32 * 128 cached tokens. `fresh_len`: each group's counts sum to 32.
All inputs are finite; a program needn't handle non-finite values.
Results may differ from the reference program's by a relative error of at most 0.025.
Values may be sent and summed in bfloat16 or wider, within the bound.
A program may use at most 128 MiB of HBM per device.

```python
import math
import jax
import jax.numpy as jnp
import numpy as np
from jax import lax

D = 7168
H = 128
LAT = 512
ROPE = 64
VDIM = 128
FF = 18432
PAGE = 128
REQ = 2
PAGES_DEV = 64
PAGES_REQ = 32
GROUP_ROWS = 32
DP_BLOCKS = 32
ROWS = 1024
POOL = 2048
D_BLOCK = 224


def shared_latent(key):
    return jnp.clip(jax.random.normal(key, (ROWS, LAT), jnp.float32), -4.0, 4.0)


def draw_fresh_lat(key, part):
    common = shared_latent(key)
    return common.astype(jnp.bfloat16)


def draw_q_lat(key, part):
    key = jax.random.fold_in(key, 5)
    first = jax.random.fold_in(key, 0)
    values = jnp.clip(jax.random.normal(first, (ROWS, H, LAT), jnp.float32), -6.0, 6.0)
    return values.reshape(ROWS, H * LAT).astype(jnp.bfloat16)


def draw_resid(key, part):
    key = jax.random.fold_in(key, 7)
    first = jax.random.fold_in(key, 0)
    columns = 0.3 + 0.7 * jnp.arange(D, dtype=jnp.float32) / (D - 1)
    return (jnp.clip(jax.random.normal(first, (ROWS, D), jnp.float32), -5.0, 5.0) * columns[None, :]).astype(jnp.bfloat16)


def draw_page_table(key, part):
    key = jax.random.fold_in(key, 11)
    group_keys = jax.random.split(key, DP_BLOCKS)
    orders = jax.vmap(lambda subkey: jax.random.permutation(subkey, PAGES_DEV))(group_keys)
    return orders.reshape(DP_BLOCKS, REQ, PAGES_REQ).astype(jnp.int32)


def draw_hit_len(key, part):
    key = jax.random.fold_in(key, 13)
    first, second, third = jax.random.split(key, 3)
    longest = PAGES_REQ * PAGE
    lengths = jax.random.randint(first, (DP_BLOCKS, REQ), 1, longest + 1)
    full_group = jax.random.randint(second, (), 0, DP_BLOCKS)
    full_request = jax.random.randint(third, (), 0, REQ)
    chosen = (jnp.arange(DP_BLOCKS)[:, None] == full_group) & (jnp.arange(REQ)[None, :] == full_request)
    return jnp.where(chosen, longest, lengths).astype(jnp.int32)


def block_levels(own_key, extent, cuts, least, top_value):
    loudness = 1.0
    for axis_at, parts in cuts:
        steps = jax.random.uniform(jax.random.fold_in(jax.random.fold_in(own_key, 6), axis_at), (parts,), jnp.float32, least / len(cuts), top_value / len(cuts))
        loudness = loudness * jnp.repeat(jnp.exp(steps), extent[axis_at] // parts).reshape((-1,) + (1,) * (len(extent) - 1 - axis_at))
    return loudness


def split_up(count, total, bound, lean):
    loads = [(1 << 20) // math.isqrt(rank ** lean) + 1 for rank in range(2, count + 1)]
    surplus, holding = total - bound - (count - 1), [1] * (count - 1)
    while surplus > 0:
        candidates = [i for i in range(count - 1) if holding[i] < bound]
        mass, budget = sum([loads[i] for i in candidates]), surplus
        for i in candidates:
            addition = min(bound - holding[i], max(1, budget * loads[i] // mass), surplus)
            holding[i] = holding[i] + addition
            surplus = surplus - addition
    return np.array([bound] + holding)


def ragged(own_key, count, total, bound, lean):
    if count == 2:
        one = jax.random.randint(own_key, (), max(1, total - bound), min(bound, total - 1) + 1)
        return jnp.stack([one, total - one])
    sizes = jnp.asarray(split_up(count, total, bound, lean), jnp.int32)
    pairs = (count - 1) // 2
    giver, taker = sizes[1:1 + 2 * pairs:2], sizes[2:2 + 2 * pairs:2]
    room = jnp.minimum(giver - 1, bound - taker)
    moved = jax.random.randint(jax.random.fold_in(own_key, 1), (pairs,), 0, 1 << 20) % (room + 1)
    sizes = sizes.at[1:1 + 2 * pairs:2].set(giver - moved).at[2:2 + 2 * pairs:2].set(taker + moved)
    return sizes[jax.random.permutation(jax.random.fold_in(own_key, 2), count)]


def centred(own_key, shape, deviation, reach, cuts=(), kind=jnp.bfloat16):
    drawn = deviation * jax.random.normal(own_key, shape, jnp.float32)
    if cuts:
        drawn = drawn * block_levels(own_key, shape, cuts, -0.22, 0.18)
    return jnp.clip(drawn, -reach, reach).astype(kind)


def setup_inputs(seed: int = 0) -> dict:
    key_of = jax.random.split(jax.random.key(seed), 17)
    return {
        "q_lat": draw_q_lat(jax.random.fold_in(key_of[16], 71), 0),
        "q_rope": centred(key_of[1], (ROWS, H * ROPE), 1.0, 6.0, ((0, 32), (1, 8))),
        "fresh_lat": draw_fresh_lat(jax.random.fold_in(key_of[16], 71), 0),
        "fresh_rope": centred(key_of[3], (ROWS, ROPE), 1.0, 6.0, ((0, 32),)),
        "cache_lat": centred(key_of[4], (POOL, PAGE, LAT), 1.0, 6.0, ((0, 32),)),
        "cache_rope": centred(key_of[5], (POOL, ROPE, PAGE), 1.0, 6.0, ((0, 32),)),
        "page_table": draw_page_table(jax.random.fold_in(key_of[16], 71), 0),
        "hit_len": draw_hit_len(jax.random.fold_in(key_of[16], 71), 0),
        "fresh_len": jax.vmap(lambda own: ragged(own, REQ, GROUP_ROWS, GROUP_ROWS - max(1, GROUP_ROWS // 4), 2))(jax.random.split(key_of[8], DP_BLOCKS)).reshape((DP_BLOCKS, REQ)).astype(jnp.int32),
        "w_uv": centred(key_of[9], (H, LAT, VDIM), LAT ** -0.5, 0.25, ((0, 8),)),
        "w_o": centred(key_of[10], (H * VDIM, D), (H * VDIM) ** -0.5, 0.046875, ((0, 8), (1, 32))),
        "resid": draw_resid(jax.random.fold_in(key_of[16], 71), 0),
        "norm_gain": jnp.clip(1.0 + 0.18 * jax.random.normal(key_of[12], (D,), jnp.float32), 0.099609375, 1.8984375).astype(jnp.bfloat16),
        "w_gate": centred(key_of[13], (D, FF), D ** -0.5, 0.0625, ((0, 32), (1, 8))),
        "w_up": centred(key_of[14], (D, FF), D ** -0.5, 0.0625, ((0, 32), (1, 8))),
        "w_down": centred(key_of[15], (FF, D), FF ** -0.5, 0.046875, ((0, 8), (1, 32))),
    }


epsilon = 1e-06

def attend(queries, rope_query, fresh_keys, fresh_rotary, keys_lat, keys_rope, hit, counts):
    row_ids = jnp.arange(fresh_keys.shape[0], dtype=jnp.int32)
    bounds = jnp.cumsum(counts)[:-1]
    row_request = lax.optimization_barrier(jnp.sum((row_ids[:, None] >= bounds[None, :]).astype(jnp.int32), axis=1))
    key_ids = jnp.arange(keys_lat.shape[0], dtype=jnp.int32)
    span_len = keys_lat.shape[0] // counts.shape[0]
    key_request = key_ids // span_len
    key_place = key_ids % span_len
    request_ids = jnp.arange(counts.shape[0], dtype=jnp.int32)
    limits = lax.optimization_barrier(jnp.sum(jnp.where(key_request[:, None] == request_ids[None, :], hit[None, :], 0), axis=1))
    cache_mask = (row_request[:, None] == key_request[None, :]) & (key_place[None, :] < limits[None, :])
    fresh_mask = (row_request[:, None] == row_request[None, :]) & (row_ids[None, :] <= row_ids[:, None])
    factor = (VDIM + ROPE) ** (-0.5)
    query_f = queries.astype(jnp.float32)
    rope_f = rope_query.astype(jnp.float32)
    lat_f = keys_lat.astype(jnp.float32)
    fresh_f = fresh_keys.astype(jnp.float32)
    cache_scores = factor * (jnp.einsum('rhl,kl->rhk', query_f, lat_f) + jnp.einsum('rhe,ek->rhk', rope_f, keys_rope.astype(jnp.float32)))
    fresh_scores = factor * (jnp.einsum('rhl,jl->rhj', query_f, fresh_f) + jnp.einsum('rhe,je->rhj', rope_f, fresh_rotary.astype(jnp.float32)))
    cache_scores = jnp.where(cache_mask[:, None, :], cache_scores, -jnp.inf)
    fresh_scores = jnp.where(fresh_mask[:, None, :], fresh_scores, -jnp.inf)
    peak = jnp.maximum(lax.optimization_barrier(jnp.max(cache_scores, axis=2)), lax.optimization_barrier(jnp.max(fresh_scores, axis=2)))
    cache_exp = jnp.exp(cache_scores - peak[..., None])
    fresh_exp = jnp.exp(fresh_scores - peak[..., None])
    denominator = lax.optimization_barrier(jnp.sum(cache_exp, axis=2)) + lax.optimization_barrier(jnp.sum(fresh_exp, axis=2))
    cache_weights = (cache_exp / denominator[..., None]).astype(jnp.bfloat16)
    fresh_weights = (fresh_exp / denominator[..., None]).astype(jnp.bfloat16)
    latent_out = jnp.einsum('rhk,kl->rhl', cache_weights.astype(jnp.float32), lat_f) + jnp.einsum('rhj,jl->rhl', fresh_weights.astype(jnp.float32), fresh_f)
    return latent_out.astype(jnp.bfloat16)

def reference(q_lat, q_rope, fresh_lat, fresh_rope, cache_lat, cache_rope, page_table, hit_len, fresh_len, w_uv, w_o, resid, norm_gain, w_gate, w_up, w_down):
    grouped = (q_lat.reshape(DP_BLOCKS, GROUP_ROWS, H, LAT), q_rope.reshape(DP_BLOCKS, GROUP_ROWS, H, ROPE), fresh_lat.reshape(DP_BLOCKS, GROUP_ROWS, LAT), fresh_rope.reshape(DP_BLOCKS, GROUP_ROWS, ROPE), cache_lat.reshape(DP_BLOCKS, PAGES_DEV, PAGE, LAT), cache_rope.reshape(DP_BLOCKS, PAGES_DEV, ROPE, PAGE), page_table, hit_len, fresh_len)
    uv_f = w_uv.astype(jnp.float32)

    def one_group(pieces):
        queries, rope_query, fresh_keys, fresh_rotary, pool_lat, pool_rope, table, hit, counts = pieces
        order = table.reshape(-1).astype(jnp.int32)
        keys_lat = pool_lat[order].reshape(-1, LAT)
        keys_rope = jnp.transpose(pool_rope[order], (1, 0, 2)).reshape(ROPE, -1)
        latent_out = attend(queries, rope_query, fresh_keys, fresh_rotary, keys_lat, keys_rope, hit, counts)
        values = jnp.einsum('rhl,hlv->rhv', latent_out.astype(jnp.float32), uv_f).astype(jnp.bfloat16)
        return values.reshape(GROUP_ROWS, H * VDIM)
    head_values = lax.map(one_group, grouped).reshape(ROWS, H * VDIM)
    attended = jnp.dot(head_values, w_o, preferred_element_type=jnp.float32)
    stream = resid.astype(jnp.float32) + attended
    mean_square = lax.optimization_barrier(jnp.mean(stream * stream, axis=1, keepdims=True))
    normed = (stream * lax.rsqrt(mean_square + epsilon) * norm_gain.astype(jnp.float32)).astype(jnp.bfloat16)
    normed_blocks = jnp.transpose(normed.reshape(ROWS, DP_BLOCKS, D_BLOCK), (1, 0, 2))
    gate_blocks = w_gate.reshape(DP_BLOCKS, D_BLOCK, FF)
    up_blocks = w_up.reshape(DP_BLOCKS, D_BLOCK, FF)

    def add_block(carry, pieces):
        rows_block, gate_block, up_block = pieces
        gate_part = jnp.dot(rows_block, gate_block, preferred_element_type=jnp.float32).astype(jnp.bfloat16)
        up_part = jnp.dot(rows_block, up_block, preferred_element_type=jnp.float32).astype(jnp.bfloat16)
        gate_part, up_part = lax.optimization_barrier((gate_part, up_part))
        return ((carry[0] + gate_part.astype(jnp.float32), carry[1] + up_part.astype(jnp.float32)), None)
    start_sums = (jnp.zeros((ROWS, FF), jnp.float32), jnp.zeros((ROWS, FF), jnp.float32))
    (gate_pre, up_pre), _ = lax.scan(add_block, start_sums, (normed_blocks, gate_blocks, up_blocks))
    hidden = (jax.nn.silu(gate_pre) * up_pre).astype(jnp.bfloat16)
    return (stream + jnp.dot(hidden, w_down, preferred_element_type=jnp.float32)).astype(jnp.bfloat16)
```

```python
import functools

import jax
import jax.numpy as jnp
from jax import lax
from jax.experimental import pallas as pl
from jax.experimental.pallas import tpu as pltpu
from jax.sharding import PartitionSpec as P

D = 7168
ROPE = 64
VDIM = 128
X, Y, Z = 4, 4, 8
EPS = 1e-06
MESH = pl.DeviceIdType.MESH
F32 = jnp.float32
BF16 = jnp.bfloat16


def attend_local(
    q_lat,
    q_rope,
    fresh_lat,
    fresh_rope,
    cache_lat,
    cache_rope,
    page_table,
    hit_len,
    fresh_len,
    w_uv,
):
    heads, latent_width, value_width = w_uv.shape
    rows_here = fresh_lat.shape[0]
    queries = q_lat.reshape(rows_here, heads, latent_width)
    rope_query = q_rope.reshape(rows_here, heads, fresh_rope.shape[1])
    order = page_table[0].reshape(-1)
    keys_lat = cache_lat[order].reshape(-1, latent_width)
    keys_rope = jnp.transpose(cache_rope[order], (1, 0, 2)).reshape(cache_rope.shape[1], -1)
    counts = fresh_len[0]
    hit = hit_len[0]
    row_ids = jnp.arange(rows_here, dtype=jnp.int32)
    bounds = jnp.cumsum(counts)[:-1]
    row_request = jnp.sum((row_ids[:, None] >= bounds[None, :]).astype(jnp.int32), axis=1)
    key_ids = jnp.arange(keys_lat.shape[0], dtype=jnp.int32)
    span_len = keys_lat.shape[0] // counts.shape[0]
    key_request = key_ids // span_len
    key_place = key_ids % span_len
    request_ids = jnp.arange(counts.shape[0], dtype=jnp.int32)
    limits = jnp.sum(
        jnp.where(key_request[:, None] == request_ids[None, :], hit[None, :], 0), axis=1
    )
    cache_mask = (row_request[:, None] == key_request[None, :]) & (
        key_place[None, :] < limits[None, :]
    )
    fresh_mask = (row_request[:, None] == row_request[None, :]) & (
        row_ids[None, :] <= row_ids[:, None]
    )
    factor = (VDIM + ROPE) ** (-0.5)
    cache_scores = factor * (
        jnp.einsum("rhl,kl->rhk", queries, keys_lat, preferred_element_type=jnp.float32)
        + jnp.einsum("rhe,ek->rhk", rope_query, keys_rope, preferred_element_type=jnp.float32)
    )
    fresh_scores = factor * (
        jnp.einsum("rhl,jl->rhj", queries, fresh_lat, preferred_element_type=jnp.float32)
        + jnp.einsum("rhe,je->rhj", rope_query, fresh_rope, preferred_element_type=jnp.float32)
    )
    cache_scores = jnp.where(cache_mask[:, None, :], cache_scores, -jnp.inf)
    fresh_scores = jnp.where(fresh_mask[:, None, :], fresh_scores, -jnp.inf)
    peak = jnp.maximum(jnp.max(cache_scores, axis=2), jnp.max(fresh_scores, axis=2))
    cache_exp = jnp.exp(cache_scores - peak[..., None])
    fresh_exp = jnp.exp(fresh_scores - peak[..., None])
    denominator = jnp.sum(cache_exp, axis=2) + jnp.sum(fresh_exp, axis=2)
    cache_weights = (cache_exp / denominator[..., None]).astype(jnp.bfloat16)
    fresh_weights = (fresh_exp / denominator[..., None]).astype(jnp.bfloat16)
    latent_out = (
        jnp.einsum("rhk,kl->rhl", cache_weights, keys_lat, preferred_element_type=jnp.float32)
        + jnp.einsum("rhj,jl->rhl", fresh_weights, fresh_lat, preferred_element_type=jnp.float32)
    ).astype(jnp.bfloat16)
    values = jnp.einsum(
        "rhl,hlv->rhv", latent_out, w_uv, preferred_element_type=jnp.float32
    ).astype(jnp.bfloat16)
    return jnp.transpose(values.reshape(rows_here, X, -1), (1, 0, 2))


def layer_kernel(
    hv, resid, gain,
    wgu0, wgu1, wgu2, wgu3, wo0, wo1, wo2, wo3, wd0, wd1, wd2, wd3,
    out,
    heads, normed, wgu, part_o, part_d, sib_o, sib_d,
    a1_o, b1_o, ra_o, rb_o, a2_o, b2_o,
    a1_d, b1_d, ra_d, rb_d, a2_d, b2_d,
    terms, from_left, from_right, hidden, stream,
    ssem, rsem, wsem,
):
    dp, tensor = lax.axis_index("dp"), lax.axis_index("tensor")
    x, z = dp // Z, lax.rem(dp, Z)
    y, c = tensor // 2, lax.rem(tensor, 2)

    def near(dx=0, dy=0, dz=0, dc=0):
        return (
            lax.rem(x + dx, X) * Z + lax.rem(z + dz, Z),
            lax.rem(y + dy, Y) * 2 + lax.rem(c + dc, 2),
        )

    x_of = [near(dx=k) for k in range(X)]
    y_of = [near(dy=k) for k in range(Y)]
    right, left, sibling = near(dz=1), near(dz=Z - 1), near(dc=1)

    loads = []
    for s, block in enumerate((wgu0, wgu1, wgu2, wgu3)):
        row = pl.multiple_of(lax.rem(x - s + X, X) * 256, 256)
        load = pltpu.make_async_copy(block, wgu.at[pl.ds(row, 224), :], wsem.at[s])
        load.start()
        loads.append(load)

    barrier = pltpu.get_barrier_semaphore()
    partners = x_of[1:] + y_of[1:] + [right, left, sibling]
    for device in partners:
        pl.semaphore_signal(barrier, inc=1, device_id=device, device_id_type=MESH)
    pl.semaphore_wait(barrier, len(partners))

    sent = []

    def send(src, dst, device):
        at = len(sent)
        copy = pltpu.make_async_remote_copy(
            src_ref=src, dst_ref=dst, send_sem=ssem.at[at], recv_sem=rsem.at[at],
            device_id=device, device_id_type=MESH,
        )
        copy.start()
        sent.append(copy)
        return copy

    def ring_gather(view, first, arrived):
        got = {}
        for sub in range(4):
            first(sub)
            piece = view(z, sub)
            got["r", 0, sub] = send(piece, piece, right)
            got["l", 0, sub] = send(piece, piece, left)
        for hop in range(1, 4):
            zl, zr = lax.rem(z - hop + Z, Z), lax.rem(z + hop, Z)
            for sub in range(4):
                got["r", hop - 1, sub].wait_recv()
                if hop < 3 or sub < 2:
                    piece = view(zl, sub)
                    got["r", hop, sub] = send(piece, piece, right)
                got["l", hop - 1, sub].wait_recv()
                if hop < 3 or sub >= 2:
                    piece = view(zr, sub)
                    got["l", hop, sub] = send(piece, piece, left)
            arrived(zl)
            arrived(zr)
        for sub in range(4):
            got["r" if sub < 2 else "l", 3, sub].wait_recv()
        arrived(lax.rem(z + 4, Z))

    def reduce_scatter(part, sib, a1, b1, ra, rb, a2, b2):
        swaps = []
        for k in (1, 2, 3, 0):
            yk = lax.rem(y + k, Y)
            swaps.append((k, yk, send(part.at[yk, 1 - c], sib.at[k], sibling)))
        stage_b, stage_a = [], []
        for k, yk, copy in swaps:
            copy.wait_recv()
            part[yk, c] = part[yk, c] + sib[k]
            if k:
                stage_b.append(send(part.at[yk, c, :, pl.ds(64, 64), :], b1.at[k - 1], y_of[k]))
        for k in (1, 2, 3):
            xk = lax.rem(x + k, X)
            stage_a.append(send(part.at[:, c, xk, pl.ds(0, 64), :], a1.at[k - 1], x_of[k]))
        for copy in stage_b:
            copy.wait_recv()
        total = part[y, c, :, 64:128, :].astype(F32)
        for k in range(3):
            total = total + b1[k].astype(F32)
        rb[...] = total.astype(BF16)
        last_b = [
            send(rb.at[lax.rem(x + k, X)], b2.at[k - 1], x_of[k]) for k in (1, 2, 3)
        ]
        for copy in stage_a:
            copy.wait_recv()
        total = part[:, c, x, 0:64, :].astype(F32)
        for k in range(3):
            total = total + a1[k].astype(F32)
        ra[...] = total.astype(BF16)
        last_a = [
            send(ra.at[lax.rem(y + k, Y)], a2.at[k - 1], y_of[k]) for k in (1, 2, 3)
        ]
        for copy in last_a + last_b:
            copy.wait_recv()
        half_a = ra[y].astype(F32)
        half_b = rb[x].astype(F32)
        for k in range(3):
            half_a = half_a + a2[k].astype(F32)
            half_b = half_b + b2[k].astype(F32)
        return half_a[:, :224], half_b[:, :224]

    heads[z, x] = hv[x]
    moved = [None] + [
        send(hv.at[lax.rem(x + k, X)], heads.at[z, x], x_of[k]) for k in (1, 2, 3)
    ]

    def own_heads(sub):
        if sub:
            moved[sub].wait_recv()

    ring_gather(
        lambda zi, sub: heads.at[zi, lax.rem(x - sub + X, X)], own_heads, lambda zi: None
    )

    def project(j, _):
        rows = heads[:, j].reshape(Z * 32, 512)
        for s, w in enumerate((wo0, wo1, wo2, wo3)):
            product = jnp.dot(rows, w[...], preferred_element_type=F32).astype(BF16)
            part_o[j, :, lax.rem(x - s + X, X), :, 0:224] = product.reshape(2, 128, 224)
        return 0

    lax.fori_loop(0, Y, project, 0)

    halves = reduce_scatter(part_o, sib_o, a1_o, b1_o, ra_o, rb_o, a2_o, b2_o)

    width = pl.ds(pl.multiple_of(x * 256, 256), 256)
    for h, attended in enumerate(halves):
        at = pl.ds(64 * h, 64)
        total = resid[at, :].astype(F32) + attended
        stream[at, :] = total
        squares = jnp.sum(total * total, axis=1, keepdims=True)
        high = squares.astype(BF16).astype(F32)
        low = squares - high
        lane = lax.broadcasted_iota(jnp.int32, (64, 32), 1)
        tail = jnp.where(lane == 0, high, jnp.where(lane == 1, low, 0.0))
        scaled = jnp.concatenate([total * gain[...].astype(F32), tail], axis=1)
        normed[y, c, at, width] = scaled.astype(BF16)

    upper, lower = pl.ds(0, 64), pl.ds(64, 64)

    def columns(xk):
        return pl.ds(pl.multiple_of(xk * 256, 256), 256)

    own_a, own_b = normed.at[y, c, upper, width], normed.at[y, c, lower, width]
    a_y = [send(own_a, own_a, y_of[k]) for k in (1, 2, 3)]
    b_x = [send(own_b, own_b, x_of[k]) for k in (1, 2, 3)]
    a_x = [[send(own_a, own_a, x_of[k]) for k in (1, 2, 3)]]
    b_y = [[send(own_b, own_b, y_of[k]) for k in (1, 2, 3)]]
    for k in (1, 2, 3):
        a_y[k - 1].wait_recv()
        piece = normed.at[lax.rem(y - k + Y, Y), c, upper, width]
        a_x.append([send(piece, piece, x_of[j]) for j in (1, 2, 3)])
        b_x[k - 1].wait_recv()
        piece = normed.at[y, c, lower, columns(lax.rem(x - k + X, X))]
        b_y.append([send(piece, piece, y_of[j]) for j in (1, 2, 3)])
    over = []
    piece = normed.at[:, c, upper, width]
    over.append(send(piece, piece, sibling))
    piece = normed.at[y, c, lower, :]
    over.append(send(piece, piece, sibling))
    for k in (1, 2, 3):
        for group in a_x:
            group[k - 1].wait_recv()
        piece = normed.at[:, c, upper, columns(lax.rem(x - k + X, X))]
        over.append(send(piece, piece, sibling))
        for group in b_y:
            group[k - 1].wait_recv()
        piece = normed.at[lax.rem(y - k + Y, Y), c, lower, :]
        over.append(send(piece, piece, sibling))

    for load in loads:
        load.wait()
    row = lax.broadcasted_iota(jnp.int32, (32, 1280), 0)
    lane = lax.broadcasted_iota(jnp.int32, (32, 1280), 1)
    tail = jnp.where((row < 2) & (lane == 576), 1.0, 0.0).astype(BF16)
    for q in range(X):
        wgu[256 * q + 224 : 256 * q + 256, :] = tail
    for copy in over:
        copy.wait_recv()

    def expand(b):
        rows = normed[b // 2, lax.rem(b, 2)]
        terms[b] = jnp.dot(rows, wgu[...], preferred_element_type=F32).astype(BF16)

    def block_at(j):
        far = 4 - (j + 1) // 2
        step = jnp.where(lax.rem(j, 2) == 1, far, Z - far)
        return lax.rem(z + step, Z)

    def expand_range(lo, hi):
        def body(j, _):
            expand(block_at(j))
            return 0

        lax.fori_loop(lo, hi, body, 0)

    def sub_rows(sub):
        return pl.ds(32 * sub, 32)

    got = {}
    expand_range(0, 1)
    far = lax.rem(z + 4, Z)
    for sub in (0, 1):
        got["r", 0, sub] = send(
            terms.at[far, sub_rows(sub)], from_left.at[0, sub_rows(sub)], right
        )
        got["l", 0, sub + 2] = send(
            terms.at[far, sub_rows(sub + 2)], from_right.at[0, sub_rows(sub + 2)], left
        )
    expand_range(1, 3)
    for i in (0, 1):
        got["r", 1, i + 2] = send(
            terms.at[lax.rem(z + 3, Z), sub_rows(i + 2)],
            from_left.at[1, sub_rows(i + 2)],
            right,
        )
        got["l", 1, i] = send(
            terms.at[lax.rem(z + 5, Z), sub_rows(i)], from_right.at[1, sub_rows(i)], left
        )
    expand_range(3, 8)

    def pass_on(step, sub, way):
        buffer, device = (from_left, right) if way == "r" else (from_right, left)
        b = lax.rem(z + (4 - step if way == "r" else 4 + step), Z)
        got[way, step - 1, sub].wait_recv()
        at = sub_rows(sub)
        buffer[step - 1, at] = buffer[step - 1, at] + terms[b, at]
        got[way, step, sub] = send(buffer.at[step - 1, at], buffer.at[step, at], device)

    for i in (0, 1):
        pass_on(1, i, "r")
        pass_on(1, i + 2, "l")
    for step in (2, 3):
        for i in range(4):
            pass_on(step, (i + 2) % 4, "r")
            pass_on(step, i, "l")

    def own_hidden(sub):
        at = sub_rows(sub)
        got["r", 3, sub].wait_recv()
        got["l", 3, sub].wait_recv()
        total = (
            terms[z, at].astype(F32) + from_left[3, at].astype(F32) + from_right[3, at].astype(F32)
        )
        scale = lax.rsqrt(total[:, 576:577] * (1.0 / D) + EPS)
        gate, up = total[:, :640] * scale, total[:, 640:] * scale
        hidden[z, at] = (gate / (1.0 + jnp.exp(-gate)) * up).astype(BF16)

    def contract(b):
        rows = hidden[b, :, 0:576]
        for s, w in enumerate((wd0, wd1, wd2, wd3)):
            product = jnp.dot(rows, w[...], preferred_element_type=F32).astype(BF16)
            part_d[b // 2, lax.rem(b, 2), lax.rem(x - s + X, X), :, 0:224] = product

    ring_gather(lambda zi, sub: hidden.at[zi, sub_rows(sub)], own_hidden, contract)
    contract(z)

    halves = reduce_scatter(part_d, sib_d, a1_d, b1_d, ra_d, rb_d, a2_d, b2_d)
    for h, mlp in enumerate(halves):
        at = pl.ds(64 * h, 64)
        out[at, :] = (stream[at, :] + mlp).astype(BF16)
    for copy in sent:
        copy.wait_send()


COPIES = 176


def layer(hv, resid, gain, wgu, wo, wd):
    vmem = pl.BlockSpec(memory_space=pltpu.VMEM)
    hbm = pl.BlockSpec(memory_space=pl.ANY)
    halves = [
        pltpu.VMEM((3, 4, 64, 256), BF16),
        pltpu.VMEM((3, 4, 64, 256), BF16),
        pltpu.VMEM((4, 64, 256), BF16),
        pltpu.VMEM((4, 64, 256), BF16),
        pltpu.VMEM((3, 64, 256), BF16),
        pltpu.VMEM((3, 64, 256), BF16),
    ]
    return pl.pallas_call(
        layer_kernel,
        out_shape=jax.ShapeDtypeStruct((128, 224), BF16),
        in_specs=[vmem] * 3 + [hbm] * 4 + [vmem] * 8,
        out_specs=vmem,
        scratch_shapes=[
            pltpu.VMEM((Z, X, 32, 512), BF16),
            pltpu.VMEM((Y, 2, 128, X * 256), BF16),
            pltpu.VMEM((X * 256, 1280), BF16),
            pltpu.VMEM((Y, 2, X, 128, 256), BF16),
            pltpu.VMEM((Y, 2, X, 128, 256), BF16),
            pltpu.VMEM((Y, X, 128, 256), BF16),
            pltpu.VMEM((Y, X, 128, 256), BF16),
            *halves,
            *halves,
            pltpu.VMEM((Z, 128, 1280), BF16),
            pltpu.VMEM((4, 128, 1280), BF16),
            pltpu.VMEM((4, 128, 1280), BF16),
            pltpu.VMEM((Z, 128, 640), BF16),
            pltpu.VMEM((128, 224), F32),
            pltpu.SemaphoreType.DMA((COPIES,)),
            pltpu.SemaphoreType.DMA((COPIES,)),
            pltpu.SemaphoreType.DMA((4,)),
        ],
        compiler_params=pltpu.CompilerParams(
            collective_id=0, has_side_effects=True, vmem_limit_bytes=52 * 2**20
        ),
    )(hv, resid, gain, *wgu, *wo, *wd)


def spread(piece, x):
    got = [piece(x)]
    for s in range(1, X):
        pairs = [(i, (i // Z + s) % X * Z + i % Z) for i in range(X * Z)]
        got.append(lax.ppermute(piece(lax.rem(x + s, X)), "dp", pairs))
    return got


def local(
    q_lat,
    q_rope,
    fresh_lat,
    fresh_rope,
    cache_lat,
    cache_rope,
    page_table,
    hit_len,
    fresh_len,
    w_uv,
    w_o,
    resid,
    norm_gain,
    w_gate,
    w_up,
    w_down,
):
    x = lax.axis_index("dp") // Z

    def expand_piece(at):
        gate = lax.dynamic_slice(w_gate, (0, at * 576), (224, 576))
        up = lax.dynamic_slice(w_up, (0, at * 576), (224, 576))
        pad = ((0, 0), (0, 64))
        return jnp.concatenate([jnp.pad(gate, pad), jnp.pad(up, pad)], axis=1)

    wo = spread(lambda at: lax.dynamic_slice(w_o, (at * 512, 0), (512, 224)), x)
    wgu = spread(expand_piece, x)
    wd = spread(lambda at: lax.dynamic_slice(w_down, (at * 576, 0), (576, 224)), x)
    head_values = attend_local(
        q_lat,
        q_rope,
        fresh_lat,
        fresh_rope,
        cache_lat,
        cache_rope,
        page_table,
        hit_len,
        fresh_len,
        w_uv,
    )
    return layer(head_values, resid, norm_gain.reshape(1, -1), wgu, wo, wd)


def solution(mesh):
    placed = (
        P("dp", "tensor"),
        P("dp", "tensor"),
        P("dp", None),
        P("dp", None),
        P("dp", None, None),
        P("dp", None, None),
        P("dp", None, None),
        P("dp", None),
        P("dp", None),
        P("tensor", None, None),
        P("tensor", "dp"),
        P("tensor", "dp"),
        P("dp"),
        P("dp", "tensor"),
        P("dp", "tensor"),
        P("tensor", "dp"),
    )
    return jax.shard_map(
        local, mesh=mesh, in_specs=placed, out_specs=P("tensor", "dp"), check_vma=False
    )
```

```python
import functools

import jax
import jax.numpy as jnp
from jax import lax
from jax.experimental import pallas as pl
from jax.experimental.pallas import tpu as pltpu
from jax.sharding import PartitionSpec as P

D = 7168
ROPE = 64
VDIM = 128
X, Y, Z = 4, 4, 8
EPS = 1e-06
MESH = pl.DeviceIdType.MESH
F32 = jnp.float32
BF16 = jnp.bfloat16
CHUNK = 512
AHEAD = 3
LOW = -1e30
QUERIES = 384


def attend_kernel(
    table, hit, count, q_lat, q_rope, fresh_lat, fresh_rope, cache_lat, cache_rope, w_uv,
    out,
    q_all, r_all, shuffle, keys, ropes, peak, mass, acc, w_uv_here, sem, uv_sem,
):
    pages = CHUNK // 128
    chunks0 = (hit[0, 0] + CHUNK - 1) // CHUNK
    chunks1 = (hit[0, 1] + CHUNK - 1) // CHUNK
    chunks = chunks0 + chunks1

    def place(i):
        r = (i >= chunks0).astype(jnp.int32)
        return r, i - r * chunks0

    def page_copies(i, j):
        r, k = place(i)
        page = table[0, r, k * pages + j]
        return (
            pltpu.make_async_copy(
                cache_lat.at[page], keys.at[i, pl.ds(128 * j, 128), :], sem.at[0, i, j]
            ),
            pltpu.make_async_copy(
                cache_rope.at[page], ropes.at[i, :, pl.ds(128 * j, 128)], sem.at[1, i, j]
            ),
        )

    def fetch(i):
        @pl.when(i < chunks)
        def _():
            for j in range(pages):
                for copy in page_copies(i, j):
                    copy.start()

    for i in range(AHEAD):
        fetch(jnp.int32(i))
    uv_copy = pltpu.make_async_copy(w_uv, w_uv_here, uv_sem)
    uv_copy.start()

    for h in range(16):
        for j in range(4):
            shuffle[j, pl.ds(h, 32, stride=16), :] = q_lat[
                :, 512 * h + 128 * j : 512 * h + 128 * (j + 1)
            ].astype(F32)
    for j in range(4):
        q_all[:, 128 * j : 128 * (j + 1)] = shuffle[j].astype(BF16)
    for h in range(0, 16, 2):
        pair = q_rope[:, 64 * h : 64 * h + 128].astype(F32)
        shuffle[0, pl.ds(h, 32, stride=16), :] = pair
        shuffle[0, pl.ds(h + 1, 32, stride=16), :] = jnp.concatenate(
            [pair[:, 64:], pair[:, :64]], axis=1
        )
    r_all[...] = shuffle[0, :, 0:64].astype(BF16)

    scale = (VDIM + ROPE) ** -0.5 * 1.4426950408889634
    n0 = count[0, 0]

    def nt(a, b):
        return lax.dot_general(a, b, (((1,), (1,)), ((), ())), preferred_element_type=F32)

    scores = (nt(q_all[...], fresh_lat[...]) + nt(r_all[...], fresh_rope[...])) * scale
    row = lax.broadcasted_iota(jnp.int32, (512, 32), 0) // 16
    key = lax.broadcasted_iota(jnp.int32, (512, 32), 1)
    valid = (key <= row) & ((key >= n0) | (row < n0))
    scores = jnp.where(valid, scores, LOW)
    top = jnp.max(scores, axis=1, keepdims=True)
    weight = jnp.exp2(scores - top)
    peak[...] = top
    mass[...] = jnp.sum(weight, axis=1, keepdims=True)
    product = jnp.dot(weight.astype(BF16), fresh_lat[...], preferred_element_type=F32)
    for j in range(4):
        acc[j] = product[:, 128 * j : 128 * (j + 1)]

    def body(i, _):
        fetch(i + AHEAD)
        r, k = place(i)
        start = pl.multiple_of(r * 128, 128)
        at = pl.ds(start, QUERIES)
        for j in range(pages):
            for copy in page_copies(i, j):
                copy.wait()
        block = keys[i]
        scores = nt(q_all[at, :], block) + jnp.dot(
            r_all[at, :], ropes[i], preferred_element_type=F32
        )
        position = k * CHUNK + lax.broadcasted_iota(jnp.int32, (1, CHUNK), 1)
        query = start + lax.broadcasted_iota(jnp.int32, (QUERIES, 1), 0)
        first = r * n0 * 16
        last = jnp.where(r == 0, n0 * 16, 512)
        column_bias = jnp.where(position < hit[0, r], 0.0, LOW)
        row_bias = jnp.where((query >= first) & (query < last), 0.0, LOW)
        scores = scores * scale + column_bias + row_bias
        before = peak[at, :]
        top = jnp.maximum(before, jnp.max(scores, axis=1, keepdims=True))
        shrink = jnp.exp2(before - top)
        weight = jnp.exp2(scores - top)
        peak[at, :] = top
        mass[at, :] = mass[at, :] * shrink + jnp.sum(weight, axis=1, keepdims=True)
        product = jnp.dot(weight.astype(BF16), block, preferred_element_type=F32)
        for j in range(4):
            acc[j, at, :] = acc[j, at, :] * shrink + product[:, 128 * j : 128 * (j + 1)]
        return 0

    lax.fori_loop(0, chunks, body, 0)

    uv_copy.wait()
    inverse = 1.0 / mass[...]
    for j in range(4):
        acc[j] = acc[j] * inverse
    for h in range(16):
        rows = jnp.concatenate(
            [acc[j, pl.ds(h, 32, stride=16), :] for j in range(4)], axis=1
        ).astype(BF16)
        values = jnp.dot(rows, w_uv_here[h], preferred_element_type=F32).astype(BF16)
        out[h // 4, :, 128 * (h % 4) : 128 * (h % 4 + 1)] = values


def attend(q_lat, q_rope, fresh_lat, fresh_rope, cache_lat, cache_rope, page_table, hit_len, fresh_len, w_uv):
    vmem = pl.BlockSpec(memory_space=pltpu.VMEM)
    smem = pl.BlockSpec(memory_space=pltpu.SMEM)
    hbm = pl.BlockSpec(memory_space=pl.ANY)
    most = 8192 // CHUNK
    return pl.pallas_call(
        attend_kernel,
        out_shape=jax.ShapeDtypeStruct((4, 32, 512), BF16),
        in_specs=[smem] * 3 + [vmem] * 4 + [hbm] * 3,
        out_specs=vmem,
        scratch_shapes=[
            pltpu.VMEM((512, 512), BF16),
            pltpu.VMEM((512, 64), BF16),
            pltpu.VMEM((4, 512, 128), F32),
            pltpu.VMEM((most, CHUNK, 512), BF16),
            pltpu.VMEM((most, 64, CHUNK), BF16),
            pltpu.VMEM((512, 1), F32),
            pltpu.VMEM((512, 1), F32),
            pltpu.VMEM((4, 512, 128), F32),
            pltpu.VMEM((16, 512, 128), BF16),
            pltpu.SemaphoreType.DMA((2, most, CHUNK // 128)),
            pltpu.SemaphoreType.DMA,
        ],
        compiler_params=pltpu.CompilerParams(vmem_limit_bytes=61 * 2**20),
        cost_estimate=pl.CostEstimate(
            flops=20 * 10**9, bytes_accessed=12 * 2**20, transcendentals=2**22
        ),
    )(page_table, hit_len, fresh_len, q_lat, q_rope, fresh_lat, fresh_rope, cache_lat, cache_rope, w_uv)


def layer_kernel(
    hv, resid, gain,
    w_gate, w_up, wgu1, wgu2, wgu3, w_o, w_down,
    out,
    heads, normed, wgu, wo, wd, part_o, part_d, sib_o, sib_d,
    a1_o, b1_o, ra_o, rb_o, a2_o, b2_o,
    a1_d, b1_d, ra_d, rb_d, a2_d, b2_d,
    terms, from_left, from_right, hidden, stream,
    ssem, rsem, wsem,
):
    dp, tensor = lax.axis_index("dp"), lax.axis_index("tensor")
    x, z = dp // Z, lax.rem(dp, Z)
    y, c = tensor // 2, lax.rem(tensor, 2)

    def near(dx=0, dy=0, dz=0, dc=0):
        return (
            lax.rem(x + dx, X) * Z + lax.rem(z + dz, Z),
            lax.rem(y + dy, Y) * 2 + lax.rem(c + dc, 2),
        )

    x_of = [near(dx=k) for k in range(X)]
    y_of = [near(dy=k) for k in range(Y)]
    right, left, sibling = near(dz=1), near(dz=Z - 1), near(dc=1)

    def window(xk):
        return pl.ds(pl.multiple_of((9 * xk) // 2 * 128, 128), 640)

    def block_rows(xk):
        return pl.ds(pl.multiple_of(xk * 256, 256), 224)

    loads = [
        pltpu.make_async_copy(
            w_o.at[:, pl.ds(pl.multiple_of(x * 512, 512), 512)], wo.at[0], wsem.at[0]
        ),
        pltpu.make_async_copy(
            w_gate.at[:, window(x)], wgu.at[block_rows(x), pl.ds(0, 640)], wsem.at[1]
        ),
        pltpu.make_async_copy(
            w_up.at[:, window(x)], wgu.at[block_rows(x), pl.ds(640, 640)], wsem.at[2]
        ),
        pltpu.make_async_copy(w_down.at[:, window(x)], wd.at[0], wsem.at[3]),
    ]
    for s, block in enumerate((wgu1, wgu2, wgu3)):
        loads.append(
            pltpu.make_async_copy(
                block, wgu.at[block_rows(lax.rem(x - s - 1 + X, X)), :], wsem.at[4 + s]
            )
        )
    for load in loads:
        load.start()

    barrier = pltpu.get_barrier_semaphore()
    partners = x_of[1:] + y_of[1:] + [right, left, sibling]
    for device in partners:
        pl.semaphore_signal(barrier, inc=1, device_id=device, device_id_type=MESH)
    pl.semaphore_wait(barrier, len(partners))

    sent = []

    def send(src, dst, device):
        at = len(sent)
        copy = pltpu.make_async_remote_copy(
            src_ref=src, dst_ref=dst, send_sem=ssem.at[at], recv_sem=rsem.at[at],
            device_id=device, device_id_type=MESH,
        )
        copy.start()
        sent.append(copy)
        return copy

    def ring_gather(view, first, arrived):
        got = {}
        for sub in range(4):
            first(sub)
            piece = view(z, sub)
            got["r", 0, sub] = send(piece, piece, right)
            got["l", 0, sub] = send(piece, piece, left)
        for hop in range(1, 4):
            zl, zr = lax.rem(z - hop + Z, Z), lax.rem(z + hop, Z)
            for sub in range(4):
                got["r", hop - 1, sub].wait_recv()
                if hop < 3 or sub < 2:
                    piece = view(zl, sub)
                    got["r", hop, sub] = send(piece, piece, right)
                got["l", hop - 1, sub].wait_recv()
                if hop < 3 or sub >= 2:
                    piece = view(zr, sub)
                    got["l", hop, sub] = send(piece, piece, left)
            arrived(zl)
            arrived(zr)
        for sub in range(4):
            got["r" if sub < 2 else "l", 3, sub].wait_recv()
        arrived(lax.rem(z + 4, Z))

    def reduce_scatter(part, sib, a1, b1, ra, rb, a2, b2):
        swaps = []
        for k in (1, 2, 3, 0):
            yk = lax.rem(y + k, Y)
            swaps.append((k, yk, send(part.at[yk, 1 - c], sib.at[k], sibling)))
        stage_b, stage_a = [], []
        for k, yk, copy in swaps:
            copy.wait_recv()
            part[yk, c] = part[yk, c] + sib[k]
            if k:
                stage_b.append(send(part.at[yk, c, :, pl.ds(64, 64), :], b1.at[k - 1], y_of[k]))
        for k in (1, 2, 3):
            xk = lax.rem(x + k, X)
            stage_a.append(send(part.at[:, c, xk, pl.ds(0, 64), :], a1.at[k - 1], x_of[k]))
        for copy in stage_b:
            copy.wait_recv()
        total = part[y, c, :, 64:128, :].astype(F32)
        for k in range(3):
            total = total + b1[k].astype(F32)
        rb[...] = total.astype(BF16)
        last_b = [
            send(rb.at[lax.rem(x + k, X)], b2.at[k - 1], x_of[k]) for k in (1, 2, 3)
        ]
        for copy in stage_a:
            copy.wait_recv()
        total = part[:, c, x, 0:64, :].astype(F32)
        for k in range(3):
            total = total + a1[k].astype(F32)
        ra[...] = total.astype(BF16)
        last_a = [
            send(ra.at[lax.rem(y + k, Y)], a2.at[k - 1], y_of[k]) for k in (1, 2, 3)
        ]
        for copy in last_a + last_b:
            copy.wait_recv()
        half_a = ra[y].astype(F32)
        half_b = rb[x].astype(F32)
        for k in range(3):
            half_a = half_a + a2[k].astype(F32)
            half_b = half_b + b2[k].astype(F32)
        return half_a[:, :224], half_b[:, :224]

    heads[z, x] = hv[x]
    moved = [None] + [
        send(hv.at[lax.rem(x + k, X)], heads.at[z, x], x_of[k]) for k in (1, 2, 3)
    ]

    wo_moves = [
        send(
            w_o.at[:, pl.ds(pl.multiple_of(lax.rem(x + k, X) * 512, 512), 512)],
            wo.at[k],
            x_of[k],
        )
        for k in (1, 2, 3)
    ]

    def own_heads(sub):
        if sub:
            moved[sub].wait_recv()

    ring_gather(
        lambda zi, sub: heads.at[zi, lax.rem(x - sub + X, X)], own_heads, lambda zi: None
    )

    loads[0].wait()
    for copy in wo_moves:
        copy.wait_recv()

    def nt(a, b):
        return lax.dot_general(a, b, (((1,), (1,)), ((), ())), preferred_element_type=F32)

    def project(j, _):
        rows = heads[:, j].reshape(Z * 32, 512)
        for s in range(X):
            product = nt(rows, wo[s]).astype(BF16)
            part_o[j, :, lax.rem(x - s + X, X), :, 0:224] = product.reshape(2, 128, 224)
        return 0

    lax.fori_loop(0, Y, project, 0)

    halves = reduce_scatter(part_o, sib_o, a1_o, b1_o, ra_o, rb_o, a2_o, b2_o)

    width = pl.ds(pl.multiple_of(x * 256, 256), 256)
    for h, attended in enumerate(halves):
        at = pl.ds(64 * h, 64)
        total = resid[at, :].astype(F32) + attended
        stream[at, :] = total
        squares = jnp.sum(total * total, axis=1, keepdims=True)
        high = squares.astype(BF16).astype(F32)
        low = squares - high
        lane = lax.broadcasted_iota(jnp.int32, (64, 32), 1)
        tail = jnp.where(lane == 0, high, jnp.where(lane == 1, low, 0.0))
        scaled = jnp.concatenate([total * gain[...].astype(F32), tail], axis=1)
        normed[y, c, at, width] = scaled.astype(BF16)

    upper, lower = pl.ds(0, 64), pl.ds(64, 64)

    def columns(xk):
        return pl.ds(pl.multiple_of(xk * 256, 256), 256)

    own_a, own_b = normed.at[y, c, upper, width], normed.at[y, c, lower, width]
    a_y = [send(own_a, own_a, y_of[k]) for k in (1, 2, 3)]
    b_x = [send(own_b, own_b, x_of[k]) for k in (1, 2, 3)]
    a_x = [[send(own_a, own_a, x_of[k]) for k in (1, 2, 3)]]
    b_y = [[send(own_b, own_b, y_of[k]) for k in (1, 2, 3)]]
    for k in (1, 2, 3):
        a_y[k - 1].wait_recv()
        piece = normed.at[lax.rem(y - k + Y, Y), c, upper, width]
        a_x.append([send(piece, piece, x_of[j]) for j in (1, 2, 3)])
        b_x[k - 1].wait_recv()
        piece = normed.at[y, c, lower, columns(lax.rem(x - k + X, X))]
        b_y.append([send(piece, piece, y_of[j]) for j in (1, 2, 3)])
    over = []
    piece = normed.at[:, c, upper, width]
    over.append(send(piece, piece, sibling))
    piece = normed.at[y, c, lower, :]
    over.append(send(piece, piece, sibling))
    for k in (1, 2, 3):
        for group in a_x:
            group[k - 1].wait_recv()
        piece = normed.at[:, c, upper, columns(lax.rem(x - k + X, X))]
        over.append(send(piece, piece, sibling))
        for group in b_y:
            group[k - 1].wait_recv()
        piece = normed.at[lax.rem(y - k + Y, Y), c, lower, :]
        over.append(send(piece, piece, sibling))

    for load in loads[1:]:
        load.wait()
    odd = lax.rem(x, 2)
    edge = pl.multiple_of((1 - odd) * 512, 128)
    lane = lax.broadcasted_iota(jnp.int32, (1, 128), 1)
    mine = (lane >= 64 * odd) & (lane < 64 + 64 * odd)
    for start in (edge, 640 + edge):
        tile = pl.ds(pl.multiple_of(start, 128), 128)
        wgu[:, tile] = jnp.where(mine, wgu[:, tile].astype(F32), 0.0).astype(BF16)
    row = lax.broadcasted_iota(jnp.int32, (32, 1280), 0)
    lane = lax.broadcasted_iota(jnp.int32, (32, 1280), 1)
    tail = jnp.where((row < 2) & (lane == 576 * (1 - odd)), 1.0, 0.0).astype(BF16)
    for q in range(X):
        wgu[256 * q + 224 : 256 * q + 256, :] = tail
    for copy in over:
        copy.wait_recv()

    def expand(b):
        rows = normed[b // 2, lax.rem(b, 2)]
        terms[b] = jnp.dot(rows, wgu[...], preferred_element_type=F32).astype(BF16)

    def block_at(j):
        far = 4 - (j + 1) // 2
        step = jnp.where(lax.rem(j, 2) == 1, far, Z - far)
        return lax.rem(z + step, Z)

    def expand_range(lo, hi):
        def body(j, _):
            expand(block_at(j))
            return 0

        lax.fori_loop(lo, hi, body, 0)

    def sub_rows(sub):
        return pl.ds(32 * sub, 32)

    got = {}
    expand_range(0, 1)
    far = lax.rem(z + 4, Z)
    for sub in (0, 1):
        got["r", 0, sub] = send(
            terms.at[far, sub_rows(sub)], from_left.at[0, sub_rows(sub)], right
        )
        got["l", 0, sub + 2] = send(
            terms.at[far, sub_rows(sub + 2)], from_right.at[0, sub_rows(sub + 2)], left
        )
    expand_range(1, 3)
    for i in (0, 1):
        got["r", 1, i + 2] = send(
            terms.at[lax.rem(z + 3, Z), sub_rows(i + 2)],
            from_left.at[1, sub_rows(i + 2)],
            right,
        )
        got["l", 1, i] = send(
            terms.at[lax.rem(z + 5, Z), sub_rows(i)], from_right.at[1, sub_rows(i)], left
        )
    wd_moves = [
        send(w_down.at[:, window(lax.rem(x + k, X))], wd.at[k], x_of[k]) for k in (1, 2, 3)
    ]
    expand_range(3, 8)

    def pass_on(step, sub, way):
        buffer, device = (from_left, right) if way == "r" else (from_right, left)
        b = lax.rem(z + (4 - step if way == "r" else 4 + step), Z)
        got[way, step - 1, sub].wait_recv()
        at = sub_rows(sub)
        buffer[step - 1, at] = buffer[step - 1, at] + terms[b, at]
        got[way, step, sub] = send(buffer.at[step - 1, at], buffer.at[step, at], device)

    for i in (0, 1):
        pass_on(1, i, "r")
        pass_on(1, i + 2, "l")
    for step in (2, 3):
        for i in range(4):
            pass_on(step, (i + 2) % 4, "r")
            pass_on(step, i, "l")

    def own_hidden(sub):
        at = sub_rows(sub)
        got["r", 3, sub].wait_recv()
        got["l", 3, sub].wait_recv()
        total = (
            terms[z, at].astype(F32) + from_left[3, at].astype(F32) + from_right[3, at].astype(F32)
        )
        squares = jnp.where(odd == 1, total[:, 0:1], total[:, 576:577])
        scale = lax.rsqrt(squares * (1.0 / D) + EPS)
        gate, up = total[:, :640] * scale, total[:, 640:] * scale
        hidden[z, at] = (gate / (1.0 + jnp.exp(-gate)) * up).astype(BF16)

    def contract(b):
        rows = hidden[b]
        for s in range(X):
            product = nt(rows, wd[s]).astype(BF16)
            part_d[b // 2, lax.rem(b, 2), lax.rem(x - s + X, X), :, 0:224] = product

    for copy in wd_moves:
        copy.wait_recv()
    ring_gather(lambda zi, sub: hidden.at[zi, sub_rows(sub)], own_hidden, contract)
    contract(z)

    halves = reduce_scatter(part_d, sib_d, a1_d, b1_d, ra_d, rb_d, a2_d, b2_d)
    for h, mlp in enumerate(halves):
        at = pl.ds(64 * h, 64)
        out[at, :] = (stream[at, :] + mlp).astype(BF16)
    for copy in sent:
        copy.wait_send()


COPIES = 176


def layer(hv, resid, gain, w_gate, w_up, wgu, w_o, w_down):
    vmem = pl.BlockSpec(memory_space=pltpu.VMEM)
    hbm = pl.BlockSpec(memory_space=pl.ANY)
    halves = [
        pltpu.VMEM((3, 4, 64, 256), BF16),
        pltpu.VMEM((3, 4, 64, 256), BF16),
        pltpu.VMEM((4, 64, 256), BF16),
        pltpu.VMEM((4, 64, 256), BF16),
        pltpu.VMEM((3, 64, 256), BF16),
        pltpu.VMEM((3, 64, 256), BF16),
    ]
    return pl.pallas_call(
        layer_kernel,
        out_shape=jax.ShapeDtypeStruct((128, 224), BF16),
        in_specs=[vmem] * 3 + [hbm] * 7,
        out_specs=vmem,
        scratch_shapes=[
            pltpu.VMEM((Z, X, 32, 512), BF16),
            pltpu.VMEM((Y, 2, 128, X * 256), BF16),
            pltpu.VMEM((X * 256, 1280), BF16),
            pltpu.VMEM((X, 224, 512), BF16),
            pltpu.VMEM((X, 224, 640), BF16),
            pltpu.VMEM((Y, 2, X, 128, 256), BF16),
            pltpu.VMEM((Y, 2, X, 128, 256), BF16),
            pltpu.VMEM((Y, X, 128, 256), BF16),
            pltpu.VMEM((Y, X, 128, 256), BF16),
            *halves,
            *halves,
            pltpu.VMEM((Z, 128, 1280), BF16),
            pltpu.VMEM((4, 128, 1280), BF16),
            pltpu.VMEM((4, 128, 1280), BF16),
            pltpu.VMEM((Z, 128, 640), BF16),
            pltpu.VMEM((128, 224), F32),
            pltpu.SemaphoreType.DMA((COPIES,)),
            pltpu.SemaphoreType.DMA((COPIES,)),
            pltpu.SemaphoreType.DMA((7,)),
        ],
        compiler_params=pltpu.CompilerParams(
            collective_id=0, has_side_effects=True, vmem_limit_bytes=52 * 2**20
        ),
    )(hv, resid, gain, w_gate, w_up, *wgu, w_o, w_down)


def cut_kernel(w_gate, w_up, piece1, piece2, piece3, sem):
    x = lax.axis_index("dp") // Z
    copies = []
    for s, piece in enumerate((piece1, piece2, piece3)):
        start = (9 * lax.rem(x + s + 1, X)) // 2 * 128
        window = pl.ds(pl.multiple_of(start, 128), 640)
        for j, w in enumerate((w_gate, w_up)):
            copies.append(
                pltpu.make_async_copy(
                    w.at[:, window], piece.at[:, pl.ds(640 * j, 640)], sem.at[s, j]
                )
            )
    for copy in copies:
        copy.start()
    for copy in copies:
        copy.wait()


def spread(w_gate, w_up):
    hbm = pl.BlockSpec(memory_space=pl.ANY)
    pieces = pl.pallas_call(
        cut_kernel,
        out_shape=[jax.ShapeDtypeStruct((224, 1280), BF16)] * 3,
        in_specs=[hbm] * 2,
        out_specs=[hbm] * 3,
        scratch_shapes=[pltpu.SemaphoreType.DMA((3, 2))],
    )(w_gate, w_up)
    got = []
    for s in range(1, X):
        pairs = [(i, (i // Z + s) % X * Z + i % Z) for i in range(X * Z)]
        got.append(lax.ppermute(pieces[s - 1], "dp", pairs))
    return got


def local(
    q_lat,
    q_rope,
    fresh_lat,
    fresh_rope,
    cache_lat,
    cache_rope,
    page_table,
    hit_len,
    fresh_len,
    w_uv,
    w_o,
    resid,
    norm_gain,
    w_gate,
    w_up,
    w_down,
):
    wgu = spread(w_gate, w_up)
    head_values = attend(
        q_lat,
        q_rope,
        fresh_lat,
        fresh_rope,
        cache_lat,
        cache_rope,
        page_table,
        hit_len,
        fresh_len,
        w_uv,
    )
    return layer(
        head_values, resid, norm_gain.reshape(1, -1), w_gate, w_up, wgu, w_o.T, w_down.T
    )


def solution(mesh):
    placed = (
        P("dp", "tensor"),
        P("dp", "tensor"),
        P("dp", None),
        P("dp", None),
        P("dp", None, None),
        P("dp", None, None),
        P("dp", None, None),
        P("dp", None),
        P("dp", None),
        P("tensor", None, None),
        P("tensor", "dp"),
        P("tensor", "dp"),
        P("dp"),
        P("dp", "tensor"),
        P("dp", "tensor"),
        P("tensor", "dp"),
    )
    return jax.shard_map(
        local, mesh=mesh, in_specs=placed, out_specs=P("tensor", "dp"), check_vma=False
    )
```

```python
import functools

import jax
import jax.numpy as jnp
from jax import lax
from jax.experimental import pallas as pl
from jax.experimental.pallas import tpu as pltpu
from jax.sharding import PartitionSpec as P

D = 7168
ROPE = 64
VDIM = 128
X, Y, Z = 4, 4, 8
EPS = 1e-06
MESH = pl.DeviceIdType.MESH
F32 = jnp.float32
BF16 = jnp.bfloat16
CHUNK = 512
AHEAD = 3
LOW = -1e30
QUERIES = 384


def attend_kernel(
    table, hit, count, q_lat, q_rope, fresh_lat, fresh_rope, cache_lat, cache_rope, w_uv,
    out,
    q_all, r_all, shuffle, keys, ropes, peak, mass, acc, w_uv_here, sem, uv_sem,
):
    pages = CHUNK // 128
    chunks0 = (hit[0, 0] + CHUNK - 1) // CHUNK
    chunks1 = (hit[0, 1] + CHUNK - 1) // CHUNK
    chunks = chunks0 + chunks1

    def place(i):
        r = (i >= chunks0).astype(jnp.int32)
        return r, i - r * chunks0

    def page_copies(i, j):
        r, k = place(i)
        page = table[0, r, k * pages + j]
        return (
            pltpu.make_async_copy(
                cache_lat.at[page], keys.at[i, pl.ds(128 * j, 128), :], sem.at[0, i, j]
            ),
            pltpu.make_async_copy(
                cache_rope.at[page], ropes.at[i, :, pl.ds(128 * j, 128)], sem.at[1, i, j]
            ),
        )

    def fetch(i):
        @pl.when(i < chunks)
        def _():
            for j in range(pages):
                for copy in page_copies(i, j):
                    copy.start()

    for i in range(AHEAD):
        fetch(jnp.int32(i))
    uv_copy = pltpu.make_async_copy(w_uv, w_uv_here, uv_sem)
    uv_copy.start()

    for h in range(16):
        for j in range(4):
            shuffle[j, pl.ds(h, 32, stride=16), :] = q_lat[
                :, 512 * h + 128 * j : 512 * h + 128 * (j + 1)
            ].astype(F32)
    for j in range(4):
        q_all[:, 128 * j : 128 * (j + 1)] = shuffle[j].astype(BF16)
    for h in range(0, 16, 2):
        pair = q_rope[:, 64 * h : 64 * h + 128].astype(F32)
        shuffle[0, pl.ds(h, 32, stride=16), :] = pair
        shuffle[0, pl.ds(h + 1, 32, stride=16), :] = jnp.concatenate(
            [pair[:, 64:], pair[:, :64]], axis=1
        )
    r_all[...] = shuffle[0, :, 0:64].astype(BF16)

    scale = (VDIM + ROPE) ** -0.5 * 1.4426950408889634
    n0 = count[0, 0]

    def nt(a, b):
        return lax.dot_general(a, b, (((1,), (1,)), ((), ())), preferred_element_type=F32)

    scores = (nt(q_all[...], fresh_lat[...]) + nt(r_all[...], fresh_rope[...])) * scale
    row = lax.broadcasted_iota(jnp.int32, (512, 32), 0) // 16
    key = lax.broadcasted_iota(jnp.int32, (512, 32), 1)
    valid = (key <= row) & ((key >= n0) | (row < n0))
    scores = jnp.where(valid, scores, LOW)
    top = jnp.max(scores, axis=1, keepdims=True)
    weight = jnp.exp2(scores - top)
    peak[...] = top
    mass[...] = jnp.sum(weight, axis=1, keepdims=True)
    product = jnp.dot(weight.astype(BF16), fresh_lat[...], preferred_element_type=F32)
    for j in range(4):
        acc[j] = product[:, 128 * j : 128 * (j + 1)]

    def body(i, _):
        fetch(i + AHEAD)
        r, k = place(i)
        start = pl.multiple_of(r * 128, 128)
        at = pl.ds(start, QUERIES)
        for j in range(pages):
            for copy in page_copies(i, j):
                copy.wait()
        block = keys[i]
        scores = nt(q_all[at, :], block) + jnp.dot(
            r_all[at, :], ropes[i], preferred_element_type=F32
        )
        position = k * CHUNK + lax.broadcasted_iota(jnp.int32, (1, CHUNK), 1)
        query = start + lax.broadcasted_iota(jnp.int32, (QUERIES, 1), 0)
        first = r * n0 * 16
        last = jnp.where(r == 0, n0 * 16, 512)
        column_bias = jnp.where(position < hit[0, r], 0.0, LOW)
        row_bias = jnp.where((query >= first) & (query < last), 0.0, LOW)
        scores = scores * scale + column_bias + row_bias
        before = peak[at, :]
        top = jnp.maximum(before, jnp.max(scores, axis=1, keepdims=True))
        shrink = jnp.exp2(before - top)
        weight = jnp.exp2(scores - top)
        peak[at, :] = top
        mass[at, :] = mass[at, :] * shrink + jnp.sum(weight, axis=1, keepdims=True)
        product = jnp.dot(weight.astype(BF16), block, preferred_element_type=F32)
        for j in range(4):
            acc[j, at, :] = acc[j, at, :] * shrink + product[:, 128 * j : 128 * (j + 1)]
        return 0

    lax.fori_loop(0, chunks, body, 0)

    uv_copy.wait()
    inverse = 1.0 / mass[...]
    for j in range(4):
        acc[j] = acc[j] * inverse
    for h in range(16):
        rows = jnp.concatenate(
            [acc[j, pl.ds(h, 32, stride=16), :] for j in range(4)], axis=1
        ).astype(BF16)
        values = jnp.dot(rows, w_uv_here[h], preferred_element_type=F32).astype(BF16)
        out[h // 4, :, 128 * (h % 4) : 128 * (h % 4 + 1)] = values


def attend(q_lat, q_rope, fresh_lat, fresh_rope, cache_lat, cache_rope, page_table, hit_len, fresh_len, w_uv):
    vmem = pl.BlockSpec(memory_space=pltpu.VMEM)
    smem = pl.BlockSpec(memory_space=pltpu.SMEM)
    hbm = pl.BlockSpec(memory_space=pl.ANY)
    most = 8192 // CHUNK
    return pl.pallas_call(
        attend_kernel,
        out_shape=jax.ShapeDtypeStruct((4, 32, 512), BF16),
        in_specs=[smem] * 3 + [vmem] * 4 + [hbm] * 3,
        out_specs=vmem,
        scratch_shapes=[
            pltpu.VMEM((512, 512), BF16),
            pltpu.VMEM((512, 64), BF16),
            pltpu.VMEM((4, 512, 128), F32),
            pltpu.VMEM((most, CHUNK, 512), BF16),
            pltpu.VMEM((most, 64, CHUNK), BF16),
            pltpu.VMEM((512, 1), F32),
            pltpu.VMEM((512, 1), F32),
            pltpu.VMEM((4, 512, 128), F32),
            pltpu.VMEM((16, 512, 128), BF16),
            pltpu.SemaphoreType.DMA((2, most, CHUNK // 128)),
            pltpu.SemaphoreType.DMA,
        ],
        compiler_params=pltpu.CompilerParams(vmem_limit_bytes=61 * 2**20),
        cost_estimate=pl.CostEstimate(
            flops=20 * 10**9, bytes_accessed=12 * 2**20, transcendentals=2**22
        ),
    )(page_table, hit_len, fresh_len, q_lat, q_rope, fresh_lat, fresh_rope, cache_lat, cache_rope, w_uv)


def layer_kernel(
    hv, resid, gain,
    w_gate, w_up, wgu1, wgu2, wgu3, w_o, w_down,
    out,
    heads, normed, wgu, wo, wd, part_o, part_d, sib_o, sib_d,
    a1_o, b1_o, ra_o, rb_o, a2_o, b2_o,
    a1_d, b1_d, ra_d, rb_d, a2_d, b2_d,
    terms, from_left, from_right, hidden, stream,
    ssem, rsem, wsem,
):
    dp, tensor = lax.axis_index("dp"), lax.axis_index("tensor")
    x, z = dp // Z, lax.rem(dp, Z)
    y, c = tensor // 2, lax.rem(tensor, 2)

    def near(dx=0, dy=0, dz=0, dc=0):
        return (
            lax.rem(x + dx, X) * Z + lax.rem(z + dz, Z),
            lax.rem(y + dy, Y) * 2 + lax.rem(c + dc, 2),
        )

    x_of = [near(dx=k) for k in range(X)]
    y_of = [near(dy=k) for k in range(Y)]
    right, left, sibling = near(dz=1), near(dz=Z - 1), near(dc=1)

    def window(xk):
        return pl.ds(pl.multiple_of((9 * xk) // 2 * 128, 128), 640)

    def block_rows(xk):
        return pl.ds(pl.multiple_of(xk * 256, 256), 224)

    loads = [
        pltpu.make_async_copy(
            w_o.at[:, pl.ds(pl.multiple_of(x * 512, 512), 512)], wo.at[0], wsem.at[0]
        ),
        pltpu.make_async_copy(
            w_gate.at[:, window(x)], wgu.at[block_rows(x), pl.ds(0, 640)], wsem.at[1]
        ),
        pltpu.make_async_copy(
            w_up.at[:, window(x)], wgu.at[block_rows(x), pl.ds(640, 640)], wsem.at[2]
        ),
        pltpu.make_async_copy(w_down.at[:, window(x)], wd.at[0], wsem.at[3]),
    ]
    for s, block in enumerate((wgu1, wgu2, wgu3)):
        loads.append(
            pltpu.make_async_copy(
                block, wgu.at[block_rows(lax.rem(x - s - 1 + X, X)), :], wsem.at[4 + s]
            )
        )
    for load in loads:
        load.start()

    barrier = pltpu.get_barrier_semaphore()
    partners = x_of[1:] + y_of[1:] + [right, left, sibling]
    for device in partners:
        pl.semaphore_signal(barrier, inc=1, device_id=device, device_id_type=MESH)
    pl.semaphore_wait(barrier, len(partners))

    sent = []

    def send(src, dst, device):
        at = len(sent)
        copy = pltpu.make_async_remote_copy(
            src_ref=src, dst_ref=dst, send_sem=ssem.at[at], recv_sem=rsem.at[at],
            device_id=device, device_id_type=MESH,
        )
        copy.start()
        sent.append(copy)
        return copy

    def ring_gather(view, first, arrived):
        got = {}
        for sub in range(4):
            first(sub)
            piece = view(z, sub)
            got["r", 0, sub] = send(piece, piece, right)
            got["l", 0, sub] = send(piece, piece, left)
        for hop in range(1, 4):
            zl, zr = lax.rem(z - hop + Z, Z), lax.rem(z + hop, Z)
            for sub in range(4):
                got["r", hop - 1, sub].wait_recv()
                if hop < 3 or sub < 2:
                    piece = view(zl, sub)
                    got["r", hop, sub] = send(piece, piece, right)
                got["l", hop - 1, sub].wait_recv()
                if hop < 3 or sub >= 2:
                    piece = view(zr, sub)
                    got["l", hop, sub] = send(piece, piece, left)
            arrived(zl)
            arrived(zr)
        for sub in range(4):
            got["r" if sub < 2 else "l", 3, sub].wait_recv()
        arrived(lax.rem(z + 4, Z))

    def reduce_scatter(part, sib, a1, b1, ra, rb, a2, b2):
        swaps = []
        for k in (1, 2, 3, 0):
            yk = lax.rem(y + k, Y)
            swaps.append((k, yk, send(part.at[yk, 1 - c], sib.at[k], sibling)))
        stage_b, stage_a = [], []
        for k, yk, copy in swaps:
            copy.wait_recv()
            part[yk, c] = part[yk, c] + sib[k]
            if k:
                stage_b.append(send(part.at[yk, c, :, pl.ds(64, 64), :], b1.at[k - 1], y_of[k]))
        for k in (1, 2, 3):
            xk = lax.rem(x + k, X)
            stage_a.append(send(part.at[:, c, xk, pl.ds(0, 64), :], a1.at[k - 1], x_of[k]))
        for copy in stage_b:
            copy.wait_recv()
        total = part[y, c, :, 64:128, :].astype(F32)
        for k in range(3):
            total = total + b1[k].astype(F32)
        rb[...] = total.astype(BF16)
        last_b = [
            send(rb.at[lax.rem(x + k, X)], b2.at[k - 1], x_of[k]) for k in (1, 2, 3)
        ]
        for copy in stage_a:
            copy.wait_recv()
        total = part[:, c, x, 0:64, :].astype(F32)
        for k in range(3):
            total = total + a1[k].astype(F32)
        ra[...] = total.astype(BF16)
        last_a = [
            send(ra.at[lax.rem(y + k, Y)], a2.at[k - 1], y_of[k]) for k in (1, 2, 3)
        ]
        for copy in last_a + last_b:
            copy.wait_recv()
        half_a = ra[y].astype(F32)
        half_b = rb[x].astype(F32)
        for k in range(3):
            half_a = half_a + a2[k].astype(F32)
            half_b = half_b + b2[k].astype(F32)
        return half_a[:, :224], half_b[:, :224]

    heads[z, x] = hv[x]
    moved = [None] + [
        send(hv.at[lax.rem(x + k, X)], heads.at[z, x], x_of[k]) for k in (1, 2, 3)
    ]

    wo_moves = [
        send(
            w_o.at[:, pl.ds(pl.multiple_of(lax.rem(x + k, X) * 512, 512), 512)],
            wo.at[k],
            x_of[k],
        )
        for k in (1, 2, 3)
    ]

    def own_heads(sub):
        if sub:
            moved[sub].wait_recv()

    ring_gather(
        lambda zi, sub: heads.at[zi, lax.rem(x - sub + X, X)], own_heads, lambda zi: None
    )

    loads[0].wait()
    for copy in wo_moves:
        copy.wait_recv()

    def nt(a, b):
        return lax.dot_general(a, b, (((1,), (1,)), ((), ())), preferred_element_type=F32)

    def project(j, _):
        rows = heads[:, j].reshape(Z * 32, 512)
        for s in range(X):
            product = nt(rows, wo[s]).astype(BF16)
            part_o[j, :, lax.rem(x - s + X, X), :, 0:224] = product.reshape(2, 128, 224)
        return 0

    lax.fori_loop(0, Y, project, 0)

    halves = reduce_scatter(part_o, sib_o, a1_o, b1_o, ra_o, rb_o, a2_o, b2_o)

    width = pl.ds(pl.multiple_of(x * 256, 256), 256)
    for h, attended in enumerate(halves):
        at = pl.ds(64 * h, 64)
        total = resid[at, :].astype(F32) + attended
        stream[at, :] = total
        squares = jnp.sum(total * total, axis=1, keepdims=True)
        high = squares.astype(BF16).astype(F32)
        low = squares - high
        lane = lax.broadcasted_iota(jnp.int32, (64, 32), 1)
        tail = jnp.where(lane == 0, high, jnp.where(lane == 1, low, 0.0))
        scaled = jnp.concatenate([total * gain[...].astype(F32), tail], axis=1)
        normed[y, c, at, width] = scaled.astype(BF16)

    upper, lower = pl.ds(0, 64), pl.ds(64, 64)

    def columns(xk):
        return pl.ds(pl.multiple_of(xk * 256, 256), 256)

    own_a, own_b = normed.at[y, c, upper, width], normed.at[y, c, lower, width]
    a_y = [send(own_a, own_a, y_of[k]) for k in (1, 2, 3)]
    b_x = [send(own_b, own_b, x_of[k]) for k in (1, 2, 3)]
    a_x = [[send(own_a, own_a, x_of[k]) for k in (1, 2, 3)]]
    b_y = [[send(own_b, own_b, y_of[k]) for k in (1, 2, 3)]]
    for k in (1, 2, 3):
        a_y[k - 1].wait_recv()
        piece = normed.at[lax.rem(y - k + Y, Y), c, upper, width]
        a_x.append([send(piece, piece, x_of[j]) for j in (1, 2, 3)])
        b_x[k - 1].wait_recv()
        piece = normed.at[y, c, lower, columns(lax.rem(x - k + X, X))]
        b_y.append([send(piece, piece, y_of[j]) for j in (1, 2, 3)])
    over = []
    piece = normed.at[:, c, upper, width]
    over.append(send(piece, piece, sibling))
    piece = normed.at[y, c, lower, :]
    over.append(send(piece, piece, sibling))
    for k in (1, 2, 3):
        for group in a_x:
            group[k - 1].wait_recv()
        piece = normed.at[:, c, upper, columns(lax.rem(x - k + X, X))]
        over.append(send(piece, piece, sibling))
        for group in b_y:
            group[k - 1].wait_recv()
        piece = normed.at[lax.rem(y - k + Y, Y), c, lower, :]
        over.append(send(piece, piece, sibling))

    for load in loads[1:]:
        load.wait()
    odd = lax.rem(x, 2)
    edge = pl.multiple_of((1 - odd) * 512, 128)
    lane = lax.broadcasted_iota(jnp.int32, (1, 128), 1)
    mine = (lane >= 64 * odd) & (lane < 64 + 64 * odd)
    for start in (edge, 640 + edge):
        tile = pl.ds(pl.multiple_of(start, 128), 128)
        wgu[:, tile] = jnp.where(mine, wgu[:, tile].astype(F32), 0.0).astype(BF16)
    row = lax.broadcasted_iota(jnp.int32, (32, 1280), 0)
    lane = lax.broadcasted_iota(jnp.int32, (32, 1280), 1)
    tail = jnp.where((row < 2) & (lane == 576 * (1 - odd)), 1.0, 0.0).astype(BF16)
    for q in range(X):
        wgu[256 * q + 224 : 256 * q + 256, :] = tail
    for copy in over:
        copy.wait_recv()

    def expand(b):
        rows = normed[b // 2, lax.rem(b, 2)]
        terms[b] = jnp.dot(rows, wgu[...], preferred_element_type=F32).astype(BF16)

    def block_at(j):
        far = 4 - (j + 1) // 2
        step = jnp.where(lax.rem(j, 2) == 1, far, Z - far)
        return lax.rem(z + step, Z)

    def expand_range(lo, hi):
        def body(j, _):
            expand(block_at(j))
            return 0

        lax.fori_loop(lo, hi, body, 0)

    def sub_rows(sub):
        return pl.ds(32 * sub, 32)

    got = {}
    expand_range(0, 1)
    far = lax.rem(z + 4, Z)
    for sub in (0, 1):
        got["r", 0, sub] = send(
            terms.at[far, sub_rows(sub)], from_left.at[0, sub_rows(sub)], right
        )
        got["l", 0, sub + 2] = send(
            terms.at[far, sub_rows(sub + 2)], from_right.at[0, sub_rows(sub + 2)], left
        )
    expand_range(1, 3)
    for i in (0, 1):
        got["r", 1, i + 2] = send(
            terms.at[lax.rem(z + 3, Z), sub_rows(i + 2)],
            from_left.at[1, sub_rows(i + 2)],
            right,
        )
        got["l", 1, i] = send(
            terms.at[lax.rem(z + 5, Z), sub_rows(i)], from_right.at[1, sub_rows(i)], left
        )
    wd_moves = [
        send(w_down.at[:, window(lax.rem(x + k, X))], wd.at[k], x_of[k]) for k in (1, 2, 3)
    ]
    expand_range(3, 8)

    def pass_on(step, sub, way):
        buffer, device = (from_left, right) if way == "r" else (from_right, left)
        b = lax.rem(z + (4 - step if way == "r" else 4 + step), Z)
        got[way, step - 1, sub].wait_recv()
        at = sub_rows(sub)
        buffer[step - 1, at] = buffer[step - 1, at] + terms[b, at]
        got[way, step, sub] = send(buffer.at[step - 1, at], buffer.at[step, at], device)

    for i in (0, 1):
        pass_on(1, i, "r")
        pass_on(1, i + 2, "l")
    for step in (2, 3):
        for i in range(4):
            pass_on(step, (i + 2) % 4, "r")
            pass_on(step, i, "l")

    def own_hidden(sub):
        at = sub_rows(sub)
        got["r", 3, sub].wait_recv()
        got["l", 3, sub].wait_recv()
        total = (
            terms[z, at].astype(F32) + from_left[3, at].astype(F32) + from_right[3, at].astype(F32)
        )
        squares = jnp.where(odd == 1, total[:, 0:1], total[:, 576:577])
        scale = lax.rsqrt(squares * (1.0 / D) + EPS)
        gate, up = total[:, :640] * scale, total[:, 640:] * scale
        hidden[z, at] = (gate / (1.0 + jnp.exp(-gate)) * up).astype(BF16)

    def contract(b):
        rows = hidden[b]
        for s in range(X):
            product = nt(rows, wd[s]).astype(BF16)
            part_d[b // 2, lax.rem(b, 2), lax.rem(x - s + X, X), :, 0:224] = product

    for copy in wd_moves:
        copy.wait_recv()
    ring_gather(lambda zi, sub: hidden.at[zi, sub_rows(sub)], own_hidden, contract)
    contract(z)

    halves = reduce_scatter(part_d, sib_d, a1_d, b1_d, ra_d, rb_d, a2_d, b2_d)
    for h, mlp in enumerate(halves):
        at = pl.ds(64 * h, 64)
        out[at, :] = (stream[at, :] + mlp).astype(BF16)
    for copy in sent:
        copy.wait_send()


COPIES = 176


def layer(hv, resid, gain, w_gate, w_up, wgu, w_o, w_down):
    vmem = pl.BlockSpec(memory_space=pltpu.VMEM)
    hbm = pl.BlockSpec(memory_space=pl.ANY)
    halves = [
        pltpu.VMEM((3, 4, 64, 256), BF16),
        pltpu.VMEM((3, 4, 64, 256), BF16),
        pltpu.VMEM((4, 64, 256), BF16),
        pltpu.VMEM((4, 64, 256), BF16),
        pltpu.VMEM((3, 64, 256), BF16),
        pltpu.VMEM((3, 64, 256), BF16),
    ]
    return pl.pallas_call(
        layer_kernel,
        out_shape=jax.ShapeDtypeStruct((128, 224), BF16),
        in_specs=[vmem] * 3 + [hbm] * 7,
        out_specs=vmem,
        scratch_shapes=[
            pltpu.VMEM((Z, X, 32, 512), BF16),
            pltpu.VMEM((Y, 2, 128, X * 256), BF16),
            pltpu.VMEM((X * 256, 1280), BF16),
            pltpu.VMEM((X, 224, 512), BF16),
            pltpu.VMEM((X, 224, 640), BF16),
            pltpu.VMEM((Y, 2, X, 128, 256), BF16),
            pltpu.VMEM((Y, 2, X, 128, 256), BF16),
            pltpu.VMEM((Y, X, 128, 256), BF16),
            pltpu.VMEM((Y, X, 128, 256), BF16),
            *halves,
            *halves,
            pltpu.VMEM((Z, 128, 1280), BF16),
            pltpu.VMEM((4, 128, 1280), BF16),
            pltpu.VMEM((4, 128, 1280), BF16),
            pltpu.VMEM((Z, 128, 640), BF16),
            pltpu.VMEM((128, 224), F32),
            pltpu.SemaphoreType.DMA((COPIES,)),
            pltpu.SemaphoreType.DMA((COPIES,)),
            pltpu.SemaphoreType.DMA((7,)),
        ],
        compiler_params=pltpu.CompilerParams(
            collective_id=0, has_side_effects=True, vmem_limit_bytes=52 * 2**20
        ),
    )(hv, resid, gain, w_gate, w_up, *wgu, w_o, w_down)


def cut_kernel(w_gate, w_up, piece1, piece2, piece3, sem):
    x = lax.axis_index("dp") // Z
    copies = []
    for s, piece in enumerate((piece1, piece2, piece3)):
        start = (9 * lax.rem(x + s + 1, X)) // 2 * 128
        window = pl.ds(pl.multiple_of(start, 128), 640)
        for j, w in enumerate((w_gate, w_up)):
            copies.append(
                pltpu.make_async_copy(
                    w.at[:, window], piece.at[:, pl.ds(640 * j, 640)], sem.at[s, j]
                )
            )
    for copy in copies:
        copy.start()
    for copy in copies:
        copy.wait()


def spread(w_gate, w_up):
    hbm = pl.BlockSpec(memory_space=pl.ANY)
    pieces = pl.pallas_call(
        cut_kernel,
        out_shape=[jax.ShapeDtypeStruct((224, 1280), BF16)] * 3,
        in_specs=[hbm] * 2,
        out_specs=[pl.BlockSpec(memory_space=pltpu.VMEM)] * 3,
        scratch_shapes=[pltpu.SemaphoreType.DMA((3, 2))],
    )(w_gate, w_up)
    got = []
    for s in range(1, X):
        pairs = [(i, (i // Z + s) % X * Z + i % Z) for i in range(X * Z)]
        got.append(lax.ppermute(pieces[s - 1], "dp", pairs))
    return got


def local(
    q_lat,
    q_rope,
    fresh_lat,
    fresh_rope,
    cache_lat,
    cache_rope,
    page_table,
    hit_len,
    fresh_len,
    w_uv,
    w_o,
    resid,
    norm_gain,
    w_gate,
    w_up,
    w_down,
):
    wgu = spread(w_gate, w_up)
    head_values = attend(
        q_lat,
        q_rope,
        fresh_lat,
        fresh_rope,
        cache_lat,
        cache_rope,
        page_table,
        hit_len,
        fresh_len,
        w_uv,
    )
    return layer(
        head_values, resid, norm_gain.reshape(1, -1), w_gate, w_up, wgu, w_o.T, w_down.T
    )


def solution(mesh):
    placed = (
        P("dp", "tensor"),
        P("dp", "tensor"),
        P("dp", None),
        P("dp", None),
        P("dp", None, None),
        P("dp", None, None),
        P("dp", None, None),
        P("dp", None),
        P("dp", None),
        P("tensor", None, None),
        P("tensor", "dp"),
        P("tensor", "dp"),
        P("dp"),
        P("dp", "tensor"),
        P("dp", "tensor"),
        P("tensor", "dp"),
    )
    return jax.shard_map(
        local, mesh=mesh, in_specs=placed, out_specs=P("tensor", "dp"), check_vma=False
    )
```

```python
import functools

import jax
import jax.numpy as jnp
from jax import lax
from jax.experimental import pallas as pl
from jax.experimental.pallas import tpu as pltpu
from jax.sharding import PartitionSpec as P

D = 7168
ROPE = 64
VDIM = 128
X, Y, Z = 4, 4, 8
EPS = 1e-06
MESH = pl.DeviceIdType.MESH
F32 = jnp.float32
BF16 = jnp.bfloat16
CHUNK = 512
AHEAD = 4
LOW = -1e30
QUERIES = 384


def attend_kernel(
    table, hit, count, q_lat, q_rope, fresh_lat, fresh_rope, cache_lat, cache_rope, w_uv,
    out,
    q_all, r_all, shuffle, keys, ropes, peak, mass, acc, w_uv_here, even, odd, sem, uv_sem,
):
    pages = CHUNK // 128
    chunks0 = (hit[0, 0] + CHUNK - 1) // CHUNK
    chunks1 = (hit[0, 1] + CHUNK - 1) // CHUNK
    chunks = chunks0 + chunks1

    def place(i):
        r = (i >= chunks0).astype(jnp.int32)
        return r, i - r * chunks0

    def page_copies(i, j):
        r, k = place(i)
        page = table[0, r, k * pages + j]
        return (
            pltpu.make_async_copy(
                cache_lat.at[page], keys.at[i, pl.ds(128 * j, 128), :], sem.at[0, i, j]
            ),
            pltpu.make_async_copy(
                cache_rope.at[page], ropes.at[i, :, pl.ds(128 * j, 128)], sem.at[1, i, j]
            ),
        )

    def fetch(i):
        @pl.when(i < chunks)
        def _():
            for j in range(pages):
                for copy in page_copies(i, j):
                    copy.start()

    for i in range(AHEAD):
        fetch(jnp.int32(i))
    uv_copy = pltpu.make_async_copy(w_uv, w_uv_here, uv_sem)
    uv_copy.start()

    for h in range(16):
        for j in range(4):
            shuffle[j, pl.ds(h, 32, stride=16), :] = q_lat[
                :, 512 * h + 128 * j : 512 * h + 128 * (j + 1)
            ].astype(F32)
    for j in range(4):
        q_all[:, 128 * j : 128 * (j + 1)] = shuffle[j].astype(BF16)
    for h in range(0, 16, 2):
        pair = q_rope[:, 64 * h : 64 * h + 128].astype(F32)
        shuffle[0, pl.ds(h, 32, stride=16), :] = pair
        shuffle[0, pl.ds(h + 1, 32, stride=16), :] = jnp.concatenate(
            [pair[:, 64:], pair[:, :64]], axis=1
        )
    r_all[...] = shuffle[0, :, 0:64].astype(BF16)

    scale = (VDIM + ROPE) ** -0.5 * 1.4426950408889634
    n0 = count[0, 0]

    def nt(a, b):
        return lax.dot_general(a, b, (((1,), (1,)), ((), ())), preferred_element_type=F32)

    scores = (nt(q_all[...], fresh_lat[...]) + nt(r_all[...], fresh_rope[...])) * scale
    row = lax.broadcasted_iota(jnp.int32, (512, 32), 0) // 16
    key = lax.broadcasted_iota(jnp.int32, (512, 32), 1)
    valid = (key <= row) & ((key >= n0) | (row < n0))
    scores = jnp.where(valid, scores, LOW)
    top = jnp.max(scores, axis=1, keepdims=True)
    weight = jnp.exp2(scores - top)
    peak[...] = top
    mass[...] = jnp.sum(weight, axis=1, keepdims=True)
    product = jnp.dot(weight.astype(BF16), fresh_lat[...], preferred_element_type=F32)
    for j in range(4):
        acc[j] = product[:, 128 * j : 128 * (j + 1)]

    def ready(i):
        @pl.when(i < chunks)
        def _():
            for j in range(pages):
                for copy in page_copies(i, j):
                    copy.wait()

    def window(i):
        r, k = place(i)
        start = pl.multiple_of(r * 128, 128)
        return r, k, start, pl.ds(start, QUERIES)

    def score(i, held):
        i = jnp.minimum(i, chunks - 1)
        at = window(i)[3]
        held[...] = nt(q_all[at, :], keys[i]) + jnp.dot(
            r_all[at, :], ropes[i], preferred_element_type=F32
        )

    def absorb(i, held):
        own = jnp.minimum(i, chunks - 1)
        r, k, start, at = window(own)
        limit = jnp.where(i < chunks, hit[0, r], 0)
        position = k * CHUNK + lax.broadcasted_iota(jnp.int32, (1, CHUNK), 1)
        query = start + lax.broadcasted_iota(jnp.int32, (QUERIES, 1), 0)
        first = r * n0 * 16
        last = jnp.where(r == 0, n0 * 16, 512)
        column_bias = jnp.where(position < limit, 0.0, LOW)
        row_bias = jnp.where((query >= first) & (query < last), 0.0, LOW)
        scores = held[...] * scale + column_bias + row_bias
        before = peak[at, :]
        top = jnp.maximum(before, jnp.max(scores, axis=1, keepdims=True))
        shrink = jnp.exp2(before - top)
        weight = jnp.exp2(scores - top)
        peak[at, :] = top
        mass[at, :] = mass[at, :] * shrink + jnp.sum(weight, axis=1, keepdims=True)
        product = jnp.dot(weight.astype(BF16), keys[own], preferred_element_type=F32)
        for j in range(4):
            acc[j, at, :] = acc[j, at, :] * shrink + product[:, 128 * j : 128 * (j + 1)]

    ready(0)
    score(0, even)

    def body(t, _):
        i = 2 * t
        fetch(i + AHEAD)
        fetch(i + 1 + AHEAD)
        ready(i + 1)
        ready(i + 2)
        score(i + 1, odd)
        absorb(i, even)
        score(i + 2, even)
        absorb(i + 1, odd)
        return 0

    lax.fori_loop(0, (chunks + 1) // 2, body, 0)

    uv_copy.wait()
    inverse = 1.0 / mass[...]
    for j in range(4):
        acc[j] = acc[j] * inverse
    for h in range(16):
        rows = jnp.concatenate(
            [acc[j, pl.ds(h, 32, stride=16), :] for j in range(4)], axis=1
        ).astype(BF16)
        values = jnp.dot(rows, w_uv_here[h], preferred_element_type=F32).astype(BF16)
        out[h // 4, :, 128 * (h % 4) : 128 * (h % 4 + 1)] = values


def attend(q_lat, q_rope, fresh_lat, fresh_rope, cache_lat, cache_rope, page_table, hit_len, fresh_len, w_uv):
    vmem = pl.BlockSpec(memory_space=pltpu.VMEM)
    smem = pl.BlockSpec(memory_space=pltpu.SMEM)
    hbm = pl.BlockSpec(memory_space=pl.ANY)
    most = 8192 // CHUNK
    return pl.pallas_call(
        attend_kernel,
        out_shape=jax.ShapeDtypeStruct((4, 32, 512), BF16),
        in_specs=[smem] * 3 + [vmem] * 4 + [hbm] * 3,
        out_specs=vmem,
        scratch_shapes=[
            pltpu.VMEM((512, 512), BF16),
            pltpu.VMEM((512, 64), BF16),
            pltpu.VMEM((4, 512, 128), F32),
            pltpu.VMEM((most, CHUNK, 512), BF16),
            pltpu.VMEM((most, 64, CHUNK), BF16),
            pltpu.VMEM((512, 1), F32),
            pltpu.VMEM((512, 1), F32),
            pltpu.VMEM((4, 512, 128), F32),
            pltpu.VMEM((16, 512, 128), BF16),
            pltpu.VMEM((QUERIES, CHUNK), F32),
            pltpu.VMEM((QUERIES, CHUNK), F32),
            pltpu.SemaphoreType.DMA((2, most, CHUNK // 128)),
            pltpu.SemaphoreType.DMA,
        ],
        compiler_params=pltpu.CompilerParams(vmem_limit_bytes=61 * 2**20),
        cost_estimate=pl.CostEstimate(
            flops=20 * 10**9, bytes_accessed=12 * 2**20, transcendentals=2**22
        ),
    )(page_table, hit_len, fresh_len, q_lat, q_rope, fresh_lat, fresh_rope, cache_lat, cache_rope, w_uv)


def layer_kernel(
    hv, resid, gain,
    w_gate, w_up, wgu1, wgu3, w_o, w_down,
    out,
    heads, normed, wgu, wo, wd, part_o, part_d, sib_o, sib_d,
    a1_o, b1_o, ra_o, rb_o, a2_o, b2_o,
    a1_d, b1_d, ra_d, rb_d, a2_d, b2_d,
    terms, from_left, from_right, hidden, stream,
    ssem, rsem, wsem,
):
    dp, tensor = lax.axis_index("dp"), lax.axis_index("tensor")
    x, z = dp // Z, lax.rem(dp, Z)
    y, c = tensor // 2, lax.rem(tensor, 2)

    def near(dx=0, dy=0, dz=0, dc=0):
        return (
            lax.rem(x + dx, X) * Z + lax.rem(z + dz, Z),
            lax.rem(y + dy, Y) * 2 + lax.rem(c + dc, 2),
        )

    x_of = [near(dx=k) for k in range(X)]
    y_of = [near(dy=k) for k in range(Y)]
    right, left, sibling = near(dz=1), near(dz=Z - 1), near(dc=1)

    def window(xk):
        return pl.ds(pl.multiple_of((9 * xk) // 2 * 128, 128), 640)

    def block_rows(xk):
        return pl.ds(pl.multiple_of(xk * 256, 256), 224)

    loads = [
        pltpu.make_async_copy(
            w_o.at[:, pl.ds(pl.multiple_of(x * 512, 512), 512)], wo.at[0], wsem.at[0]
        ),
        pltpu.make_async_copy(
            w_gate.at[:, window(x)], wgu.at[block_rows(x), pl.ds(0, 640)], wsem.at[1]
        ),
        pltpu.make_async_copy(
            w_up.at[:, window(x)], wgu.at[block_rows(x), pl.ds(640, 640)], wsem.at[2]
        ),
        pltpu.make_async_copy(w_down.at[:, window(x)], wd.at[0], wsem.at[3]),
    ]
    for i, (s, block) in enumerate(((1, wgu1), (3, wgu3))):
        loads.append(
            pltpu.make_async_copy(
                block, wgu.at[block_rows(lax.rem(x - s + X, X)), :], wsem.at[4 + i]
            )
        )
    for load in loads:
        load.start()

    barrier = pltpu.get_barrier_semaphore()
    partners = x_of[1:] + y_of[1:] + [right, left, sibling]
    for device in partners:
        pl.semaphore_signal(barrier, inc=1, device_id=device, device_id_type=MESH)
    pl.semaphore_wait(barrier, len(partners))

    sent = []

    def send(src, dst, device):
        at = len(sent)
        copy = pltpu.make_async_remote_copy(
            src_ref=src, dst_ref=dst, send_sem=ssem.at[at], recv_sem=rsem.at[at],
            device_id=device, device_id_type=MESH,
        )
        copy.start()
        sent.append(copy)
        return copy

    def ring_gather(view, first, arrived):
        got = {}
        for sub in range(4):
            first(sub)
            piece = view(z, sub)
            got["r", 0, sub] = send(piece, piece, right)
            got["l", 0, sub] = send(piece, piece, left)
        for hop in range(1, 4):
            zl, zr = lax.rem(z - hop + Z, Z), lax.rem(z + hop, Z)
            for sub in range(4):
                got["r", hop - 1, sub].wait_recv()
                if hop < 3 or sub < 2:
                    piece = view(zl, sub)
                    got["r", hop, sub] = send(piece, piece, right)
                got["l", hop - 1, sub].wait_recv()
                if hop < 3 or sub >= 2:
                    piece = view(zr, sub)
                    got["l", hop, sub] = send(piece, piece, left)
            arrived(zl)
            arrived(zr)
        for sub in range(4):
            got["r" if sub < 2 else "l", 3, sub].wait_recv()
        arrived(lax.rem(z + 4, Z))

    def reduce_scatter(part, sib, a1, b1, ra, rb, a2, b2):
        swaps = []
        for k in (1, 2, 3, 0):
            yk = lax.rem(y + k, Y)
            swaps.append((k, yk, send(part.at[yk, 1 - c], sib.at[k], sibling)))
        stage_b, stage_a = [], []
        for k, yk, copy in swaps:
            copy.wait_recv()
            part[yk, c] = part[yk, c] + sib[k]
            if k:
                stage_b.append(send(part.at[yk, c, :, pl.ds(64, 64), :], b1.at[k - 1], y_of[k]))
        for k in (1, 2, 3):
            xk = lax.rem(x + k, X)
            stage_a.append(send(part.at[:, c, xk, pl.ds(0, 64), :], a1.at[k - 1], x_of[k]))
        for copy in stage_b:
            copy.wait_recv()
        total = part[y, c, :, 64:128, :].astype(F32)
        for k in range(3):
            total = total + b1[k].astype(F32)
        rb[...] = total.astype(BF16)
        last_b = [
            send(rb.at[lax.rem(x + k, X)], b2.at[k - 1], x_of[k]) for k in (1, 2, 3)
        ]
        for copy in stage_a:
            copy.wait_recv()
        total = part[:, c, x, 0:64, :].astype(F32)
        for k in range(3):
            total = total + a1[k].astype(F32)
        ra[...] = total.astype(BF16)
        last_a = [
            send(ra.at[lax.rem(y + k, Y)], a2.at[k - 1], y_of[k]) for k in (1, 2, 3)
        ]
        for copy in last_a + last_b:
            copy.wait_recv()
        half_a = ra[y].astype(F32)
        half_b = rb[x].astype(F32)
        for k in range(3):
            half_a = half_a + a2[k].astype(F32)
            half_b = half_b + b2[k].astype(F32)
        return half_a[:, :224], half_b[:, :224]

    heads[z, x] = hv[x]
    moved = [None] + [
        send(hv.at[lax.rem(x + k, X)], heads.at[z, x], x_of[k]) for k in (1, 2, 3)
    ]

    wo_moves = [
        send(
            w_o.at[:, pl.ds(pl.multiple_of(lax.rem(x + k, X) * 512, 512), 512)],
            wo.at[k],
            x_of[k],
        )
        for k in (1, 2, 3)
    ]

    def own_heads(sub):
        if sub:
            moved[sub].wait_recv()

    unit_moves = []
    seen = []

    def heads_arrived(zi):
        seen.append(zi)
        if len(seen) == 2:
            there = window(lax.rem(x + 2, X))
            for j, w in enumerate((w_gate, w_up)):
                unit_moves.append(
                    send(
                        w.at[:, there], wgu.at[block_rows(x), pl.ds(640 * j, 640)], x_of[2]
                    )
                )

    ring_gather(
        lambda zi, sub: heads.at[zi, lax.rem(x - sub + X, X)], own_heads, heads_arrived
    )

    loads[0].wait()
    for copy in wo_moves:
        copy.wait_recv()

    def nt(a, b):
        return lax.dot_general(a, b, (((1,), (1,)), ((), ())), preferred_element_type=F32)

    def project(j, _):
        rows = heads[:, j].reshape(Z * 32, 512)
        for s in range(X):
            product = nt(rows, wo[s]).astype(BF16)
            part_o[j, :, lax.rem(x - s + X, X), :, 0:224] = product.reshape(2, 128, 224)
        return 0

    lax.fori_loop(0, Y, project, 0)

    halves = reduce_scatter(part_o, sib_o, a1_o, b1_o, ra_o, rb_o, a2_o, b2_o)

    width = pl.ds(pl.multiple_of(x * 256, 256), 256)
    for h, attended in enumerate(halves):
        at = pl.ds(64 * h, 64)
        total = resid[at, :].astype(F32) + attended
        stream[at, :] = total
        squares = jnp.sum(total * total, axis=1, keepdims=True)
        high = squares.astype(BF16).astype(F32)
        low = squares - high
        lane = lax.broadcasted_iota(jnp.int32, (64, 32), 1)
        tail = jnp.where(lane == 0, high, jnp.where(lane == 1, low, 0.0))
        scaled = jnp.concatenate([total * gain[...].astype(F32), tail], axis=1)
        normed[y, c, at, width] = scaled.astype(BF16)

    upper, lower = pl.ds(0, 64), pl.ds(64, 64)

    def columns(xk):
        return pl.ds(pl.multiple_of(xk * 256, 256), 256)

    own_a, own_b = normed.at[y, c, upper, width], normed.at[y, c, lower, width]
    a_y = [send(own_a, own_a, y_of[k]) for k in (1, 2, 3)]
    b_x = [send(own_b, own_b, x_of[k]) for k in (1, 2, 3)]
    a_x = [[send(own_a, own_a, x_of[k]) for k in (1, 2, 3)]]
    b_y = [[send(own_b, own_b, y_of[k]) for k in (1, 2, 3)]]
    for k in (1, 2, 3):
        a_y[k - 1].wait_recv()
        piece = normed.at[lax.rem(y - k + Y, Y), c, upper, width]
        a_x.append([send(piece, piece, x_of[j]) for j in (1, 2, 3)])
        b_x[k - 1].wait_recv()
        piece = normed.at[y, c, lower, columns(lax.rem(x - k + X, X))]
        b_y.append([send(piece, piece, y_of[j]) for j in (1, 2, 3)])
    over = []
    piece = normed.at[:, c, upper, width]
    over.append(send(piece, piece, sibling))
    piece = normed.at[y, c, lower, :]
    over.append(send(piece, piece, sibling))
    for k in (1, 2, 3):
        for group in a_x:
            group[k - 1].wait_recv()
        piece = normed.at[:, c, upper, columns(lax.rem(x - k + X, X))]
        over.append(send(piece, piece, sibling))
        for group in b_y:
            group[k - 1].wait_recv()
        piece = normed.at[lax.rem(y - k + Y, Y), c, lower, :]
        over.append(send(piece, piece, sibling))

    for load in loads[1:]:
        load.wait()
    for copy in unit_moves:
        copy.wait_recv()
    odd = lax.rem(x, 2)
    edge = pl.multiple_of((1 - odd) * 512, 128)
    lane = lax.broadcasted_iota(jnp.int32, (1, 128), 1)
    mine = (lane >= 64 * odd) & (lane < 64 + 64 * odd)
    for start in (edge, 640 + edge):
        tile = pl.ds(pl.multiple_of(start, 128), 128)
        wgu[:, tile] = jnp.where(mine, wgu[:, tile].astype(F32), 0.0).astype(BF16)
    row = lax.broadcasted_iota(jnp.int32, (32, 1280), 0)
    lane = lax.broadcasted_iota(jnp.int32, (32, 1280), 1)
    tail = jnp.where((row < 2) & (lane == 576 * (1 - odd)), 1.0, 0.0).astype(BF16)
    for q in range(X):
        wgu[256 * q + 224 : 256 * q + 256, :] = tail
    for copy in over:
        copy.wait_recv()

    def expand(b):
        rows = normed[b // 2, lax.rem(b, 2)]
        terms[b] = jnp.dot(rows, wgu[...], preferred_element_type=F32).astype(BF16)

    def block_at(j):
        far = 4 - (j + 1) // 2
        step = jnp.where(lax.rem(j, 2) == 1, far, Z - far)
        return lax.rem(z + step, Z)

    def expand_range(lo, hi):
        def body(j, _):
            expand(block_at(j))
            return 0

        lax.fori_loop(lo, hi, body, 0)

    def sub_rows(sub):
        return pl.ds(32 * sub, 32)

    got = {}
    expand_range(0, 1)
    far = lax.rem(z + 4, Z)
    for sub in (0, 1):
        got["r", 0, sub] = send(
            terms.at[far, sub_rows(sub)], from_left.at[0, sub_rows(sub)], right
        )
        got["l", 0, sub + 2] = send(
            terms.at[far, sub_rows(sub + 2)], from_right.at[0, sub_rows(sub + 2)], left
        )
    expand_range(1, 3)
    for i in (0, 1):
        got["r", 1, i + 2] = send(
            terms.at[lax.rem(z + 3, Z), sub_rows(i + 2)],
            from_left.at[1, sub_rows(i + 2)],
            right,
        )
        got["l", 1, i] = send(
            terms.at[lax.rem(z + 5, Z), sub_rows(i)], from_right.at[1, sub_rows(i)], left
        )
    wd_moves = [
        send(w_down.at[:, window(lax.rem(x + k, X))], wd.at[k], x_of[k]) for k in (1, 2, 3)
    ]
    expand_range(3, 8)

    def pass_on(step, sub, way):
        buffer, device = (from_left, right) if way == "r" else (from_right, left)
        b = lax.rem(z + (4 - step if way == "r" else 4 + step), Z)
        got[way, step - 1, sub].wait_recv()
        at = sub_rows(sub)
        buffer[step - 1, at] = buffer[step - 1, at] + terms[b, at]
        got[way, step, sub] = send(buffer.at[step - 1, at], buffer.at[step, at], device)

    for i in (0, 1):
        pass_on(1, i, "r")
        pass_on(1, i + 2, "l")
    for step in (2, 3):
        for i in range(4):
            pass_on(step, (i + 2) % 4, "r")
            pass_on(step, i, "l")

    def own_hidden(sub):
        at = sub_rows(sub)
        got["r", 3, sub].wait_recv()
        got["l", 3, sub].wait_recv()
        total = (
            terms[z, at].astype(F32) + from_left[3, at].astype(F32) + from_right[3, at].astype(F32)
        )
        squares = jnp.where(odd == 1, total[:, 0:1], total[:, 576:577])
        scale = lax.rsqrt(squares * (1.0 / D) + EPS)
        gate, up = total[:, :640] * scale, total[:, 640:] * scale
        hidden[z, at] = (gate / (1.0 + jnp.exp(-gate)) * up).astype(BF16)

    def contract(b):
        rows = hidden[b]
        for s in range(X):
            product = nt(rows, wd[s]).astype(BF16)
            part_d[b // 2, lax.rem(b, 2), lax.rem(x - s + X, X), :, 0:224] = product

    for copy in wd_moves:
        copy.wait_recv()
    ring_gather(lambda zi, sub: hidden.at[zi, sub_rows(sub)], own_hidden, contract)
    contract(z)

    halves = reduce_scatter(part_d, sib_d, a1_d, b1_d, ra_d, rb_d, a2_d, b2_d)
    for h, mlp in enumerate(halves):
        at = pl.ds(64 * h, 64)
        out[at, :] = (stream[at, :] + mlp).astype(BF16)
    for copy in sent:
        copy.wait_send()


COPIES = 176


def layer(hv, resid, gain, w_gate, w_up, wgu, w_o, w_down):
    vmem = pl.BlockSpec(memory_space=pltpu.VMEM)
    hbm = pl.BlockSpec(memory_space=pl.ANY)
    halves = [
        pltpu.VMEM((3, 4, 64, 256), BF16),
        pltpu.VMEM((3, 4, 64, 256), BF16),
        pltpu.VMEM((4, 64, 256), BF16),
        pltpu.VMEM((4, 64, 256), BF16),
        pltpu.VMEM((3, 64, 256), BF16),
        pltpu.VMEM((3, 64, 256), BF16),
    ]
    return pl.pallas_call(
        layer_kernel,
        out_shape=jax.ShapeDtypeStruct((128, 224), BF16),
        in_specs=[vmem] * 3 + [hbm] * 6,
        out_specs=vmem,
        scratch_shapes=[
            pltpu.VMEM((Z, X, 32, 512), BF16),
            pltpu.VMEM((Y, 2, 128, X * 256), BF16),
            pltpu.VMEM((X * 256, 1280), BF16),
            pltpu.VMEM((X, 224, 512), BF16),
            pltpu.VMEM((X, 224, 640), BF16),
            pltpu.VMEM((Y, 2, X, 128, 256), BF16),
            pltpu.VMEM((Y, 2, X, 128, 256), BF16),
            pltpu.VMEM((Y, X, 128, 256), BF16),
            pltpu.VMEM((Y, X, 128, 256), BF16),
            *halves,
            *halves,
            pltpu.VMEM((Z, 128, 1280), BF16),
            pltpu.VMEM((4, 128, 1280), BF16),
            pltpu.VMEM((4, 128, 1280), BF16),
            pltpu.VMEM((Z, 128, 640), BF16),
            pltpu.VMEM((128, 224), F32),
            pltpu.SemaphoreType.DMA((COPIES,)),
            pltpu.SemaphoreType.DMA((COPIES,)),
            pltpu.SemaphoreType.DMA((6,)),
        ],
        compiler_params=pltpu.CompilerParams(
            collective_id=0, has_side_effects=True, vmem_limit_bytes=52 * 2**20
        ),
    )(hv, resid, gain, w_gate, w_up, *wgu, w_o, w_down)


def cut_kernel(w_gate, w_up, piece1, piece3, sem):
    x = lax.axis_index("dp") // Z
    copies = []
    for i, (s, piece) in enumerate(((1, piece1), (3, piece3))):
        start = (9 * lax.rem(x + s, X)) // 2 * 128
        window = pl.ds(pl.multiple_of(start, 128), 640)
        for j, w in enumerate((w_gate, w_up)):
            copies.append(
                pltpu.make_async_copy(
                    w.at[:, window], piece.at[:, pl.ds(640 * j, 640)], sem.at[i, j]
                )
            )
    for copy in copies:
        copy.start()
    for copy in copies:
        copy.wait()


def spread(w_gate, w_up):
    hbm = pl.BlockSpec(memory_space=pl.ANY)
    pieces = pl.pallas_call(
        cut_kernel,
        out_shape=[jax.ShapeDtypeStruct((224, 1280), BF16)] * 2,
        in_specs=[hbm] * 2,
        out_specs=[pl.BlockSpec(memory_space=pltpu.VMEM)] * 2,
        scratch_shapes=[pltpu.SemaphoreType.DMA((2, 2))],
    )(w_gate, w_up)
    got = []
    for s, piece in zip((1, 3), pieces):
        pairs = [(i, (i // Z + s) % X * Z + i % Z) for i in range(X * Z)]
        got.append(lax.ppermute(piece, "dp", pairs))
    return got


def local(
    q_lat,
    q_rope,
    fresh_lat,
    fresh_rope,
    cache_lat,
    cache_rope,
    page_table,
    hit_len,
    fresh_len,
    w_uv,
    w_o,
    resid,
    norm_gain,
    w_gate,
    w_up,
    w_down,
):
    wgu = spread(w_gate, w_up)
    head_values = attend(
        q_lat,
        q_rope,
        fresh_lat,
        fresh_rope,
        cache_lat,
        cache_rope,
        page_table,
        hit_len,
        fresh_len,
        w_uv,
    )
    return layer(
        head_values, resid, norm_gain.reshape(1, -1), w_gate, w_up, wgu, w_o.T, w_down.T
    )


def solution(mesh):
    placed = (
        P("dp", "tensor"),
        P("dp", "tensor"),
        P("dp", None),
        P("dp", None),
        P("dp", None, None),
        P("dp", None, None),
        P("dp", None, None),
        P("dp", None),
        P("dp", None),
        P("tensor", None, None),
        P("tensor", "dp"),
        P("tensor", "dp"),
        P("dp"),
        P("dp", "tensor"),
        P("dp", "tensor"),
        P("tensor", "dp"),
    )
    return jax.shard_map(
        local, mesh=mesh, in_specs=placed, out_specs=P("tensor", "dp"), check_vma=False
    )
```

```python
import functools

import jax
import jax.numpy as jnp
from jax import lax
from jax.experimental import pallas as pl
from jax.experimental.pallas import tpu as pltpu
from jax.sharding import PartitionSpec as P

D = 7168
ROPE = 64
VDIM = 128
X, Y, Z = 4, 4, 8
EPS = 1e-06
MESH = pl.DeviceIdType.MESH
F32 = jnp.float32
BF16 = jnp.bfloat16
CHUNK = 512
AHEAD = 4
LOW = -1e30
QUERIES = 384


def attend_kernel(
    table, hit, count, q_lat, q_rope, fresh_lat, fresh_rope, cache_lat, cache_rope, w_uv,
    out,
    q_all, r_all, shuffle, keys, ropes, peak, mass, acc, w_uv_here, even, odd, sem, uv_sem,
):
    pages = CHUNK // 128
    chunks0 = (hit[0, 0] + CHUNK - 1) // CHUNK
    chunks1 = (hit[0, 1] + CHUNK - 1) // CHUNK
    chunks = chunks0 + chunks1

    def place(i):
        r = (i >= chunks0).astype(jnp.int32)
        return r, i - r * chunks0

    def page_copies(i, j):
        r, k = place(i)
        page = table[0, r, k * pages + j]
        return (
            pltpu.make_async_copy(
                cache_lat.at[page], keys.at[i, pl.ds(128 * j, 128), :], sem.at[0, i, j]
            ),
            pltpu.make_async_copy(
                cache_rope.at[page], ropes.at[i, :, pl.ds(128 * j, 128)], sem.at[1, i, j]
            ),
        )

    def fetch(i):
        @pl.when(i < chunks)
        def _():
            for j in range(pages):
                for copy in page_copies(i, j):
                    copy.start()

    for i in range(AHEAD):
        fetch(jnp.int32(i))
    uv_copy = pltpu.make_async_copy(w_uv, w_uv_here, uv_sem)
    uv_copy.start()

    for h in range(16):
        for j in range(4):
            shuffle[j, pl.ds(h, 32, stride=16), :] = q_lat[
                :, 512 * h + 128 * j : 512 * h + 128 * (j + 1)
            ].astype(F32)
    for j in range(4):
        q_all[:, 128 * j : 128 * (j + 1)] = shuffle[j].astype(BF16)
    for h in range(0, 16, 2):
        pair = q_rope[:, 64 * h : 64 * h + 128].astype(F32)
        shuffle[0, pl.ds(h, 32, stride=16), :] = pair
        shuffle[0, pl.ds(h + 1, 32, stride=16), :] = jnp.concatenate(
            [pair[:, 64:], pair[:, :64]], axis=1
        )
    r_all[...] = shuffle[0, :, 0:64].astype(BF16)

    scale = (VDIM + ROPE) ** -0.5 * 1.4426950408889634
    n0 = count[0, 0]

    def nt(a, b):
        return lax.dot_general(a, b, (((1,), (1,)), ((), ())), preferred_element_type=F32)

    scores = (nt(q_all[...], fresh_lat[...]) + nt(r_all[...], fresh_rope[...])) * scale
    row = lax.broadcasted_iota(jnp.int32, (512, 32), 0) // 16
    key = lax.broadcasted_iota(jnp.int32, (512, 32), 1)
    valid = (key <= row) & ((key >= n0) | (row < n0))
    scores = jnp.where(valid, scores, LOW)
    top = jnp.max(scores, axis=1, keepdims=True)
    weight = jnp.exp2(scores - top)
    peak[...] = top
    mass[...] = jnp.sum(weight, axis=1, keepdims=True)
    product = jnp.dot(weight.astype(BF16), fresh_lat[...], preferred_element_type=F32)
    for j in range(4):
        acc[j] = product[:, 128 * j : 128 * (j + 1)]

    def ready(i):
        @pl.when(i < chunks)
        def _():
            for j in range(pages):
                for copy in page_copies(i, j):
                    copy.wait()

    def window(i):
        r, k = place(i)
        start = pl.multiple_of(r * 128, 128)
        return r, k, start, pl.ds(start, QUERIES)

    def score(i, held):
        i = jnp.minimum(i, chunks - 1)
        at = window(i)[3]
        held[...] = nt(q_all[at, :], keys[i]) + jnp.dot(
            r_all[at, :], ropes[i], preferred_element_type=F32
        )

    def absorb(i, held):
        own = jnp.minimum(i, chunks - 1)
        r, k, start, at = window(own)
        limit = jnp.where(i < chunks, hit[0, r], 0)
        position = k * CHUNK + lax.broadcasted_iota(jnp.int32, (1, CHUNK), 1)
        query = start + lax.broadcasted_iota(jnp.int32, (QUERIES, 1), 0)
        first = r * n0 * 16
        last = jnp.where(r == 0, n0 * 16, 512)
        column_bias = jnp.where(position < limit, 0.0, LOW)
        row_bias = jnp.where((query >= first) & (query < last), 0.0, LOW)
        scores = held[...] * scale + column_bias + row_bias
        before = peak[at, :]
        top = jnp.maximum(before, jnp.max(scores, axis=1, keepdims=True))
        shrink = jnp.exp2(before - top)
        weight = jnp.exp2(scores - top)
        peak[at, :] = top
        mass[at, :] = mass[at, :] * shrink + jnp.sum(weight, axis=1, keepdims=True)
        product = jnp.dot(weight.astype(BF16), keys[own], preferred_element_type=F32)
        for j in range(4):
            acc[j, at, :] = acc[j, at, :] * shrink + product[:, 128 * j : 128 * (j + 1)]

    ready(0)
    score(0, even)

    def body(t, _):
        i = 2 * t
        fetch(i + AHEAD)
        fetch(i + 1 + AHEAD)
        ready(i + 1)
        ready(i + 2)
        score(i + 1, odd)
        absorb(i, even)
        score(i + 2, even)
        absorb(i + 1, odd)
        return 0

    lax.fori_loop(0, (chunks + 1) // 2, body, 0)

    uv_copy.wait()
    inverse = 1.0 / mass[...]
    for j in range(4):
        acc[j] = acc[j] * inverse
    for h in range(16):
        rows = jnp.concatenate(
            [acc[j, pl.ds(h, 32, stride=16), :] for j in range(4)], axis=1
        ).astype(BF16)
        values = jnp.dot(rows, w_uv_here[h], preferred_element_type=F32).astype(BF16)
        out[h // 4, :, 128 * (h % 4) : 128 * (h % 4 + 1)] = values


def attend(q_lat, q_rope, fresh_lat, fresh_rope, cache_lat, cache_rope, page_table, hit_len, fresh_len, w_uv):
    vmem = pl.BlockSpec(memory_space=pltpu.VMEM)
    smem = pl.BlockSpec(memory_space=pltpu.SMEM)
    hbm = pl.BlockSpec(memory_space=pl.ANY)
    most = 8192 // CHUNK
    return pl.pallas_call(
        attend_kernel,
        out_shape=jax.ShapeDtypeStruct((4, 32, 512), BF16),
        in_specs=[smem] * 3 + [vmem] * 4 + [hbm] * 3,
        out_specs=vmem,
        scratch_shapes=[
            pltpu.VMEM((512, 512), BF16),
            pltpu.VMEM((512, 64), BF16),
            pltpu.VMEM((4, 512, 128), F32),
            pltpu.VMEM((most, CHUNK, 512), BF16),
            pltpu.VMEM((most, 64, CHUNK), BF16),
            pltpu.VMEM((512, 1), F32),
            pltpu.VMEM((512, 1), F32),
            pltpu.VMEM((4, 512, 128), F32),
            pltpu.VMEM((16, 512, 128), BF16),
            pltpu.VMEM((QUERIES, CHUNK), F32),
            pltpu.VMEM((QUERIES, CHUNK), F32),
            pltpu.SemaphoreType.DMA((2, most, CHUNK // 128)),
            pltpu.SemaphoreType.DMA,
        ],
        compiler_params=pltpu.CompilerParams(vmem_limit_bytes=61 * 2**20),
        cost_estimate=pl.CostEstimate(
            flops=20 * 10**9, bytes_accessed=12 * 2**20, transcendentals=2**22
        ),
    )(page_table, hit_len, fresh_len, q_lat, q_rope, fresh_lat, fresh_rope, cache_lat, cache_rope, w_uv)


def layer_kernel(
    hv, resid, gain,
    w_gate, w_up, wgu1, wgu3, w_o, w_down,
    out,
    heads, normed, wgu, wo, wd, part_o, part_d, sib_o, sib_d,
    a1_o, b1_o, ra_o, rb_o, a2_o, b2_o,
    a1_d, b1_d, ra_d, rb_d, a2_d, b2_d,
    terms, from_left, from_right, hidden, stream,
    ssem, rsem, wsem,
):
    dp, tensor = lax.axis_index("dp"), lax.axis_index("tensor")
    x, z = dp // Z, lax.rem(dp, Z)
    y, c = tensor // 2, lax.rem(tensor, 2)

    def near(dx=0, dy=0, dz=0, dc=0):
        return (
            lax.rem(x + dx, X) * Z + lax.rem(z + dz, Z),
            lax.rem(y + dy, Y) * 2 + lax.rem(c + dc, 2),
        )

    x_of = [near(dx=k) for k in range(X)]
    y_of = [near(dy=k) for k in range(Y)]
    right, left, sibling = near(dz=1), near(dz=Z - 1), near(dc=1)

    def window(xk):
        return pl.ds(pl.multiple_of((9 * xk) // 2 * 128, 128), 640)

    def block_rows(xk):
        return pl.ds(pl.multiple_of(xk * 256, 256), 224)

    loads = [
        pltpu.make_async_copy(
            w_o.at[:, pl.ds(pl.multiple_of(x * 512, 512), 512)], wo.at[0], wsem.at[0]
        ),
        pltpu.make_async_copy(
            w_gate.at[:, window(x)], wgu.at[block_rows(x), pl.ds(0, 640)], wsem.at[1]
        ),
        pltpu.make_async_copy(
            w_up.at[:, window(x)], wgu.at[block_rows(x), pl.ds(640, 640)], wsem.at[2]
        ),
        pltpu.make_async_copy(w_down.at[:, window(x)], wd.at[0], wsem.at[3]),
    ]
    for i, (s, block) in enumerate(((1, wgu1), (3, wgu3))):
        loads.append(
            pltpu.make_async_copy(
                block, wgu.at[block_rows(lax.rem(x - s + X, X)), :], wsem.at[4 + i]
            )
        )
    for load in loads:
        load.start()

    barrier = pltpu.get_barrier_semaphore()
    partners = x_of[1:] + y_of[1:] + [right, left, sibling]
    for device in partners:
        pl.semaphore_signal(barrier, inc=1, device_id=device, device_id_type=MESH)
    pl.semaphore_wait(barrier, len(partners))

    sent = []

    def send(src, dst, device):
        at = len(sent)
        copy = pltpu.make_async_remote_copy(
            src_ref=src, dst_ref=dst, send_sem=ssem.at[at], recv_sem=rsem.at[at],
            device_id=device, device_id_type=MESH,
        )
        copy.start()
        sent.append(copy)
        return copy

    def ring_gather(view, first, arrived):
        got = {}
        for sub in range(4):
            first(sub)
            piece = view(z, sub)
            got["r", 0, sub] = send(piece, piece, right)
            got["l", 0, sub] = send(piece, piece, left)
        for hop in range(1, 4):
            zl, zr = lax.rem(z - hop + Z, Z), lax.rem(z + hop, Z)
            for sub in range(4):
                got["r", hop - 1, sub].wait_recv()
                if hop < 3 or sub < 2:
                    piece = view(zl, sub)
                    got["r", hop, sub] = send(piece, piece, right)
                got["l", hop - 1, sub].wait_recv()
                if hop < 3 or sub >= 2:
                    piece = view(zr, sub)
                    got["l", hop, sub] = send(piece, piece, left)
            arrived(zl)
            arrived(zr)
        for sub in range(4):
            got["r" if sub < 2 else "l", 3, sub].wait_recv()
        arrived(lax.rem(z + 4, Z))

    def nt(a, b):
        return lax.dot_general(a, b, (((1,), (1,)), ((), ())), preferred_element_type=F32)

    def scatter(part, a1, b1, ra, rb, a2, b2, in_turn):
        stage_a = []
        base = len(sent)

        def to_row(k, yk):
            return pltpu.make_async_remote_copy(
                src_ref=part.at[yk, c, :, pl.ds(64, 64), :],
                dst_ref=b1.at[k - 1],
                send_sem=ssem.at[base + k - 1],
                recv_sem=rsem.at[base + k - 1],
                device_id=(dp, yk * 2 + c),
                device_id_type=MESH,
            )

        stage_b = [to_row(k, lax.rem(y + k, Y)) for k in (1, 2, 3)]
        sent.extend(stage_b)

        def first(yk):
            k = lax.rem(yk - y + Y, Y)

            @pl.when(k != 0)
            def _():
                to_row(k, yk).start()

            for j in (1, 2, 3):
                stage_a.append(
                    send(
                        part.at[yk, c, lax.rem(x + j, X), pl.ds(0, 64), :],
                        a1.at[j - 1, yk],
                        x_of[j],
                    )
                )

        def second_a(k):
            yk = lax.rem(y + k, Y)
            total = part[yk, c, x, 0:64, :].astype(F32)
            for j in (1, 2, 3):
                if in_turn:
                    stage_a[3 * ((k - 1) % Y) + j - 1].wait_recv()
                total = total + a1[j - 1, yk].astype(F32)
            if k == 0:
                return total
            ra[k] = total.astype(BF16)
            return send(ra.at[k], a2.at[k - 1], y_of[k])

        def second_b(j):
            xj = lax.rem(x + j, X)
            total = part[y, c, xj, 64:128, :].astype(F32)
            for k in range(3):
                total = total + b1[k, xj].astype(F32)
            if j == 0:
                return total
            rb[j] = total.astype(BF16)
            return send(rb.at[j], b2.at[j - 1], x_of[j])

        def finish():
            if not in_turn:
                for copy in stage_a:
                    copy.wait_recv()
            last_a = [second_a(k) for k in (1, 2, 3)]
            for copy in stage_b:
                copy.wait_recv()
            last_b = [second_b(j) for j in (1, 2, 3)]
            half_b = second_b(0)
            half_a = second_a(0)
            for k in range(3):
                last_a[k].wait_recv()
                half_a = half_a + a2[k].astype(F32)
            for k in range(3):
                last_b[k].wait_recv()
                half_b = half_b + b2[k].astype(F32)
            return half_a[:, :224], half_b[:, :224]

        return first, finish

    own_heads_copy = pltpu.make_async_copy(hv.at[x], heads.at[z, x], wsem.at[6])
    own_heads_copy.start()
    moved = [None] + [
        send(hv.at[lax.rem(x + k, X)], heads.at[z, x], x_of[k]) for k in (1, 2, 3)
    ]

    wo_moves = [
        send(
            w_o.at[:, pl.ds(pl.multiple_of(lax.rem(x + k, X) * 512, 512), 512)],
            wo.at[k],
            x_of[k],
        )
        for k in (1, 2, 3)
    ]

    def own_heads(sub):
        if sub:
            moved[sub].wait_recv()
        else:
            own_heads_copy.wait()

    unit_moves = []
    seen = []

    def heads_arrived(zi):
        seen.append(zi)
        if len(seen) == 2:
            there = window(lax.rem(x + 2, X))
            for j, w in enumerate((w_gate, w_up)):
                unit_moves.append(
                    send(
                        w.at[:, there], wgu.at[block_rows(x), pl.ds(640 * j, 640)], x_of[2]
                    )
                )

    ring_gather(
        lambda zi, sub: heads.at[zi, lax.rem(x - sub + X, X)], own_heads, heads_arrived
    )

    loads[0].wait()
    for copy in wo_moves:
        copy.wait_recv()

    swaps = []
    for k in (1, 2, 3, 0):
        yk = lax.rem(y + k, Y)
        rows = heads[:, yk].reshape(Z * 32, 512)
        for s in range(X):
            product = nt(rows, wo[s]).astype(BF16)
            part_o[yk, :, lax.rem(x - s + X, X), :, 0:224] = product.reshape(2, 128, 224)
        swaps.append((k, yk, send(part_o.at[yk, 1 - c], sib_o.at[k], sibling)))
    first, finish = scatter(part_o, a1_o, b1_o, ra_o, rb_o, a2_o, b2_o, True)
    for k, yk, copy in swaps:
        copy.wait_recv()
        part_o[yk, c] = part_o[yk, c] + sib_o[k]
        first(yk)
    halves = finish()

    width = pl.ds(pl.multiple_of(x * 256, 256), 256)
    for h, attended in enumerate(halves):
        at = pl.ds(64 * h, 64)
        total = resid[at, :].astype(F32) + attended
        stream[at, :] = total
        squares = jnp.sum(total * total, axis=1, keepdims=True)
        high = squares.astype(BF16).astype(F32)
        low = squares - high
        lane = lax.broadcasted_iota(jnp.int32, (64, 32), 1)
        tail = jnp.where(lane == 0, high, jnp.where(lane == 1, low, 0.0))
        scaled = jnp.concatenate([total * gain[...].astype(F32), tail], axis=1)
        normed[y, c, at, width] = scaled.astype(BF16)

    upper, lower = pl.ds(0, 64), pl.ds(64, 64)

    def columns(xk):
        return pl.ds(pl.multiple_of(xk * 256, 256), 256)

    own_a, own_b = normed.at[y, c, upper, width], normed.at[y, c, lower, width]
    a_y = [send(own_a, own_a, y_of[k]) for k in (1, 2, 3)]
    b_x = [send(own_b, own_b, x_of[k]) for k in (1, 2, 3)]
    a_x = [[send(own_a, own_a, x_of[k]) for k in (1, 2, 3)]]
    b_y = [[send(own_b, own_b, y_of[k]) for k in (1, 2, 3)]]
    for k in (1, 2, 3):
        a_y[k - 1].wait_recv()
        piece = normed.at[lax.rem(y - k + Y, Y), c, upper, width]
        a_x.append([send(piece, piece, x_of[j]) for j in (1, 2, 3)])
        b_x[k - 1].wait_recv()
        piece = normed.at[y, c, lower, columns(lax.rem(x - k + X, X))]
        b_y.append([send(piece, piece, y_of[j]) for j in (1, 2, 3)])
    over = []
    piece = normed.at[:, c, upper, width]
    over.append(send(piece, piece, sibling))
    piece = normed.at[y, c, lower, :]
    over.append(send(piece, piece, sibling))
    for k in (1, 2, 3):
        for group in a_x:
            group[k - 1].wait_recv()
        piece = normed.at[:, c, upper, columns(lax.rem(x - k + X, X))]
        over.append(send(piece, piece, sibling))
        for group in b_y:
            group[k - 1].wait_recv()
        piece = normed.at[lax.rem(y - k + Y, Y), c, lower, :]
        over.append(send(piece, piece, sibling))

    for load in loads[1:]:
        load.wait()
    for copy in unit_moves:
        copy.wait_recv()
    odd = lax.rem(x, 2)
    edge = pl.multiple_of((1 - odd) * 512, 128)
    lane = lax.broadcasted_iota(jnp.int32, (1, 128), 1)
    mine = (lane >= 64 * odd) & (lane < 64 + 64 * odd)
    for start in (edge, 640 + edge):
        tile = pl.ds(pl.multiple_of(start, 128), 128)
        wgu[:, tile] = jnp.where(mine, wgu[:, tile].astype(F32), 0.0).astype(BF16)
    row = lax.broadcasted_iota(jnp.int32, (32, 1280), 0)
    lane = lax.broadcasted_iota(jnp.int32, (32, 1280), 1)
    tail = jnp.where((row < 2) & (lane == 576 * (1 - odd)), 1.0, 0.0).astype(BF16)
    for q in range(X):
        wgu[256 * q + 224 : 256 * q + 256, :] = tail
    for copy in over:
        copy.wait_recv()

    def expand(b):
        rows = normed[b // 2, lax.rem(b, 2)]
        terms[b] = jnp.dot(rows, wgu[...], preferred_element_type=F32).astype(BF16)

    def block_at(j):
        far = 4 - (j + 1) // 2
        step = jnp.where(lax.rem(j, 2) == 1, far, Z - far)
        return lax.rem(z + step, Z)

    def expand_range(lo, hi):
        def body(j, _):
            expand(block_at(j))
            return 0

        lax.fori_loop(lo, hi, body, 0)

    def sub_rows(sub):
        return pl.ds(32 * sub, 32)

    got = {}
    expand_range(0, 1)
    far = lax.rem(z + 4, Z)
    for sub in (0, 1):
        got["r", 0, sub] = send(
            terms.at[far, sub_rows(sub)], from_left.at[0, sub_rows(sub)], right
        )
        got["l", 0, sub + 2] = send(
            terms.at[far, sub_rows(sub + 2)], from_right.at[0, sub_rows(sub + 2)], left
        )
    expand_range(1, 3)
    for i in (0, 1):
        got["r", 1, i + 2] = send(
            terms.at[lax.rem(z + 3, Z), sub_rows(i + 2)],
            from_left.at[1, sub_rows(i + 2)],
            right,
        )
        got["l", 1, i] = send(
            terms.at[lax.rem(z + 5, Z), sub_rows(i)], from_right.at[1, sub_rows(i)], left
        )
    wd_moves = [
        send(w_down.at[:, window(lax.rem(x + k, X))], wd.at[k], x_of[k]) for k in (1, 2, 3)
    ]
    expand_range(3, 8)

    def pass_on(step, sub, way):
        buffer, device = (from_left, right) if way == "r" else (from_right, left)
        b = lax.rem(z + (4 - step if way == "r" else 4 + step), Z)
        got[way, step - 1, sub].wait_recv()
        at = sub_rows(sub)
        buffer[step - 1, at] = buffer[step - 1, at] + terms[b, at]
        got[way, step, sub] = send(buffer.at[step - 1, at], buffer.at[step, at], device)

    for i in (0, 1):
        pass_on(1, i, "r")
        pass_on(1, i + 2, "l")
    for step in (2, 3):
        for i in range(4):
            pass_on(step, (i + 2) % 4, "r")
            pass_on(step, i, "l")

    def own_hidden(sub):
        at = sub_rows(sub)
        got["r", 3, sub].wait_recv()
        got["l", 3, sub].wait_recv()
        total = (
            terms[z, at].astype(F32) + from_left[3, at].astype(F32) + from_right[3, at].astype(F32)
        )
        squares = jnp.where(odd == 1, total[:, 0:1], total[:, 576:577])
        scale = lax.rsqrt(squares * (1.0 / D) + EPS)
        gate, up = total[:, :640] * scale, total[:, 640:] * scale
        hidden[z, at] = (gate / (1.0 + jnp.exp(-gate)) * up).astype(BF16)

    def contract(b):
        rows = hidden[b]
        for s in range(X):
            product = nt(rows, wd[s]).astype(BF16)
            part_d[b // 2, lax.rem(b, 2), lax.rem(x - s + X, X), :, 0:224] = product

    for copy in wd_moves:
        copy.wait_recv()
    first, finish = scatter(part_d, a1_d, b1_d, ra_d, rb_d, a2_d, b2_d, False)

    def in_order(parity):
        odd_hops = lax.rem(z + 1 + parity, 2) == 0
        steps = ((1, 0), (Z - 1, 2), (3, Z - 2), (Z - 3, 4))
        return [lax.rem(z + jnp.where(odd_hops, a, b), Z) // 2 for a, b in steps]

    to_sibling, from_sibling = in_order(1 - c), in_order(c)
    swaps = []
    met = []

    def swap(slot):
        swaps.append(send(part_d.at[to_sibling[slot], 1 - c], sib_d.at[slot], sibling))

    def add_swapped(slot):
        swaps[slot].wait_recv()
        at = from_sibling[slot]
        part_d[at, c] = part_d[at, c] + sib_d[slot]
        first(at)

    def hidden_arrived(zi):
        if not met:
            contract(z)
        contract(zi)
        met.append(zi)
        if len(met) == 4:
            swap(0)
            swap(1)
        elif len(met) == 6:
            swap(2)
            add_swapped(0)
            add_swapped(1)
        elif len(met) == 7:
            swap(3)
            add_swapped(2)

    ring_gather(lambda zi, sub: hidden.at[zi, sub_rows(sub)], own_hidden, hidden_arrived)
    add_swapped(3)
    halves = finish()
    for h, mlp in enumerate(halves):
        at = pl.ds(64 * h, 64)
        out[at, :] = (stream[at, :] + mlp).astype(BF16)
    for copy in sent:
        copy.wait_send()


COPIES = 200


def layer(hv, resid, gain, w_gate, w_up, wgu, w_o, w_down):
    vmem = pl.BlockSpec(memory_space=pltpu.VMEM)
    hbm = pl.BlockSpec(memory_space=pl.ANY)
    halves = [
        pltpu.VMEM((3, 4, 64, 256), BF16),
        pltpu.VMEM((3, 4, 64, 256), BF16),
        pltpu.VMEM((4, 64, 256), BF16),
        pltpu.VMEM((4, 64, 256), BF16),
        pltpu.VMEM((3, 64, 256), BF16),
        pltpu.VMEM((3, 64, 256), BF16),
    ]
    return pl.pallas_call(
        layer_kernel,
        out_shape=jax.ShapeDtypeStruct((128, 224), BF16),
        in_specs=[hbm] + [vmem] * 2 + [hbm] * 6,
        out_specs=vmem,
        scratch_shapes=[
            pltpu.VMEM((Z, X, 32, 512), BF16),
            pltpu.VMEM((Y, 2, 128, X * 256), BF16),
            pltpu.VMEM((X * 256, 1280), BF16),
            pltpu.VMEM((X, 224, 512), BF16),
            pltpu.VMEM((X, 224, 640), BF16),
            pltpu.VMEM((Y, 2, X, 128, 256), BF16),
            pltpu.VMEM((Y, 2, X, 128, 256), BF16),
            pltpu.VMEM((Y, X, 128, 256), BF16),
            pltpu.VMEM((Y, X, 128, 256), BF16),
            *halves,
            *halves,
            pltpu.VMEM((Z, 128, 1280), BF16),
            pltpu.VMEM((4, 128, 1280), BF16),
            pltpu.VMEM((4, 128, 1280), BF16),
            pltpu.VMEM((Z, 128, 640), BF16),
            pltpu.VMEM((128, 224), F32),
            pltpu.SemaphoreType.DMA((COPIES,)),
            pltpu.SemaphoreType.DMA((COPIES,)),
            pltpu.SemaphoreType.DMA((7,)),
        ],
        compiler_params=pltpu.CompilerParams(
            collective_id=0, has_side_effects=True, vmem_limit_bytes=52 * 2**20
        ),
    )(hv, resid, gain, w_gate, w_up, *wgu, w_o, w_down)


def cut_kernel(w_gate, w_up, piece1, piece3, sem):
    x = lax.axis_index("dp") // Z
    copies = []
    for i, (s, piece) in enumerate(((1, piece1), (3, piece3))):
        start = (9 * lax.rem(x + s, X)) // 2 * 128
        window = pl.ds(pl.multiple_of(start, 128), 640)
        for j, w in enumerate((w_gate, w_up)):
            copies.append(
                pltpu.make_async_copy(
                    w.at[:, window], piece.at[:, pl.ds(640 * j, 640)], sem.at[i, j]
                )
            )
    for copy in copies:
        copy.start()
    for copy in copies:
        copy.wait()


def spread(w_gate, w_up):
    hbm = pl.BlockSpec(memory_space=pl.ANY)
    pieces = pl.pallas_call(
        cut_kernel,
        out_shape=[jax.ShapeDtypeStruct((224, 1280), BF16)] * 2,
        in_specs=[hbm] * 2,
        out_specs=[pl.BlockSpec(memory_space=pltpu.VMEM)] * 2,
        scratch_shapes=[pltpu.SemaphoreType.DMA((2, 2))],
    )(w_gate, w_up)
    got = []
    for s, piece in zip((1, 3), pieces):
        pairs = [(i, (i // Z + s) % X * Z + i % Z) for i in range(X * Z)]
        got.append(lax.ppermute(piece, "dp", pairs))
    return got


def local(
    q_lat,
    q_rope,
    fresh_lat,
    fresh_rope,
    cache_lat,
    cache_rope,
    page_table,
    hit_len,
    fresh_len,
    w_uv,
    w_o,
    resid,
    norm_gain,
    w_gate,
    w_up,
    w_down,
):
    wgu = spread(w_gate, w_up)
    head_values = attend(
        q_lat,
        q_rope,
        fresh_lat,
        fresh_rope,
        cache_lat,
        cache_rope,
        page_table,
        hit_len,
        fresh_len,
        w_uv,
    )
    return layer(
        head_values, resid, norm_gain.reshape(1, -1), w_gate, w_up, wgu, w_o.T, w_down.T
    )


def solution(mesh):
    placed = (
        P("dp", "tensor"),
        P("dp", "tensor"),
        P("dp", None),
        P("dp", None),
        P("dp", None, None),
        P("dp", None, None),
        P("dp", None, None),
        P("dp", None),
        P("dp", None),
        P("tensor", None, None),
        P("tensor", "dp"),
        P("tensor", "dp"),
        P("dp"),
        P("dp", "tensor"),
        P("dp", "tensor"),
        P("tensor", "dp"),
    )
    return jax.shard_map(
        local, mesh=mesh, in_specs=placed, out_specs=P("tensor", "dp"), check_vma=False
    )
```

```python
import functools

import jax
import jax.numpy as jnp
from jax import lax
from jax.experimental import pallas as pl
from jax.experimental.pallas import tpu as pltpu
from jax.sharding import PartitionSpec as P

D = 7168
ROPE = 64
VDIM = 128
X, Y, Z = 4, 4, 8
EPS = 1e-06
MESH = pl.DeviceIdType.MESH
F32 = jnp.float32
BF16 = jnp.bfloat16
CHUNK = 512
AHEAD = 4
LOW = -1e30
QUERIES = 384


def attend_kernel(
    table, hit, count, q_lat, q_rope, fresh_lat, fresh_rope, cache_lat, cache_rope, w_uv,
    out,
    q_all, r_all, shuffle, keys, ropes, peak, mass, acc, w_uv_here, even, odd, sem, uv_sem,
):
    pages = CHUNK // 128
    chunks0 = (hit[0, 0] + CHUNK - 1) // CHUNK
    chunks1 = (hit[0, 1] + CHUNK - 1) // CHUNK
    chunks = chunks0 + chunks1

    def place(i):
        r = (i >= chunks0).astype(jnp.int32)
        return r, i - r * chunks0

    def page_copies(i, j):
        r, k = place(i)
        page = table[0, r, k * pages + j]
        return (
            pltpu.make_async_copy(
                cache_lat.at[page], keys.at[i, pl.ds(128 * j, 128), :], sem.at[0, i, j]
            ),
            pltpu.make_async_copy(
                cache_rope.at[page], ropes.at[i, :, pl.ds(128 * j, 128)], sem.at[1, i, j]
            ),
        )

    def fetch(i):
        @pl.when(i < chunks)
        def _():
            for j in range(pages):
                for copy in page_copies(i, j):
                    copy.start()

    for i in range(AHEAD):
        fetch(jnp.int32(i))
    uv_copy = pltpu.make_async_copy(w_uv, w_uv_here, uv_sem)
    uv_copy.start()

    for h in range(16):
        for j in range(4):
            shuffle[j, pl.ds(h, 32, stride=16), :] = q_lat[
                :, 512 * h + 128 * j : 512 * h + 128 * (j + 1)
            ].astype(F32)
    for j in range(4):
        q_all[:, 128 * j : 128 * (j + 1)] = shuffle[j].astype(BF16)
    for h in range(0, 16, 2):
        pair = q_rope[:, 64 * h : 64 * h + 128].astype(F32)
        shuffle[0, pl.ds(h, 32, stride=16), :] = pair
        shuffle[0, pl.ds(h + 1, 32, stride=16), :] = jnp.concatenate(
            [pair[:, 64:], pair[:, :64]], axis=1
        )
    r_all[...] = shuffle[0, :, 0:64].astype(BF16)

    scale = (VDIM + ROPE) ** -0.5 * 1.4426950408889634
    n0 = count[0, 0]

    def nt(a, b):
        return lax.dot_general(a, b, (((1,), (1,)), ((), ())), preferred_element_type=F32)

    scores = (nt(q_all[...], fresh_lat[...]) + nt(r_all[...], fresh_rope[...])) * scale
    row = lax.broadcasted_iota(jnp.int32, (512, 32), 0) // 16
    key = lax.broadcasted_iota(jnp.int32, (512, 32), 1)
    valid = (key <= row) & ((key >= n0) | (row < n0))
    scores = jnp.where(valid, scores, LOW)
    top = jnp.max(scores, axis=1, keepdims=True)
    weight = jnp.exp2(scores - top)
    peak[...] = top
    mass[...] = jnp.sum(weight, axis=1, keepdims=True)
    product = jnp.dot(weight.astype(BF16), fresh_lat[...], preferred_element_type=F32)
    for j in range(4):
        acc[j] = product[:, 128 * j : 128 * (j + 1)]

    def ready(i):
        @pl.when(i < chunks)
        def _():
            for j in range(pages):
                for copy in page_copies(i, j):
                    copy.wait()

    def window(i):
        r, k = place(i)
        start = pl.multiple_of(r * 128, 128)
        return r, k, start, pl.ds(start, QUERIES)

    def score(i, held):
        i = jnp.minimum(i, chunks - 1)
        at = window(i)[3]
        held[...] = nt(q_all[at, :], keys[i]) + jnp.dot(
            r_all[at, :], ropes[i], preferred_element_type=F32
        )

    def absorb(i, held):
        own = jnp.minimum(i, chunks - 1)
        r, k, start, at = window(own)
        limit = jnp.where(i < chunks, hit[0, r], 0)
        position = k * CHUNK + lax.broadcasted_iota(jnp.int32, (1, CHUNK), 1)
        query = start + lax.broadcasted_iota(jnp.int32, (QUERIES, 1), 0)
        first = r * n0 * 16
        last = jnp.where(r == 0, n0 * 16, 512)
        column_bias = jnp.where(position < limit, 0.0, LOW)
        row_bias = jnp.where((query >= first) & (query < last), 0.0, LOW)
        scores = held[...] * scale + column_bias + row_bias
        before = peak[at, :]
        top = jnp.maximum(before, jnp.max(scores, axis=1, keepdims=True))
        shrink = jnp.exp2(before - top)
        weight = jnp.exp2(scores - top)
        peak[at, :] = top
        mass[at, :] = mass[at, :] * shrink + jnp.sum(weight, axis=1, keepdims=True)
        product = jnp.dot(weight.astype(BF16), keys[own], preferred_element_type=F32)
        for j in range(4):
            acc[j, at, :] = acc[j, at, :] * shrink + product[:, 128 * j : 128 * (j + 1)]

    ready(0)
    score(0, even)

    def body(t, _):
        i = 2 * t
        fetch(i + AHEAD)
        fetch(i + 1 + AHEAD)
        ready(i + 1)
        ready(i + 2)
        score(i + 1, odd)
        absorb(i, even)
        score(i + 2, even)
        absorb(i + 1, odd)
        return 0

    lax.fori_loop(0, (chunks + 1) // 2, body, 0)

    uv_copy.wait()
    inverse = 1.0 / mass[...]
    for j in range(4):
        acc[j] = acc[j] * inverse
    for h in range(16):
        rows = jnp.concatenate(
            [acc[j, pl.ds(h, 32, stride=16), :] for j in range(4)], axis=1
        ).astype(BF16)
        values = jnp.dot(rows, w_uv_here[h], preferred_element_type=F32).astype(BF16)
        out[h // 4, :, 128 * (h % 4) : 128 * (h % 4 + 1)] = values


def attend(q_lat, q_rope, fresh_lat, fresh_rope, cache_lat, cache_rope, page_table, hit_len, fresh_len, w_uv):
    vmem = pl.BlockSpec(memory_space=pltpu.VMEM)
    smem = pl.BlockSpec(memory_space=pltpu.SMEM)
    hbm = pl.BlockSpec(memory_space=pl.ANY)
    most = 8192 // CHUNK
    return pl.pallas_call(
        attend_kernel,
        out_shape=jax.ShapeDtypeStruct((4, 32, 512), BF16),
        in_specs=[smem] * 3 + [vmem] * 4 + [hbm] * 3,
        out_specs=vmem,
        scratch_shapes=[
            pltpu.VMEM((512, 512), BF16),
            pltpu.VMEM((512, 64), BF16),
            pltpu.VMEM((4, 512, 128), F32),
            pltpu.VMEM((most, CHUNK, 512), BF16),
            pltpu.VMEM((most, 64, CHUNK), BF16),
            pltpu.VMEM((512, 1), F32),
            pltpu.VMEM((512, 1), F32),
            pltpu.VMEM((4, 512, 128), F32),
            pltpu.VMEM((16, 512, 128), BF16),
            pltpu.VMEM((QUERIES, CHUNK), F32),
            pltpu.VMEM((QUERIES, CHUNK), F32),
            pltpu.SemaphoreType.DMA((2, most, CHUNK // 128)),
            pltpu.SemaphoreType.DMA,
        ],
        compiler_params=pltpu.CompilerParams(vmem_limit_bytes=61 * 2**20),
        cost_estimate=pl.CostEstimate(
            flops=20 * 10**9, bytes_accessed=12 * 2**20, transcendentals=2**22
        ),
    )(page_table, hit_len, fresh_len, q_lat, q_rope, fresh_lat, fresh_rope, cache_lat, cache_rope, w_uv)


def layer_kernel(
    hv, resid, gain,
    w_gate, w_up, wgu1, wgu3, w_o, w_down,
    out,
    heads, normed, wgu, wo, wd, part_o, part_d, sib_o, sib_d,
    a1_o, b1_o, ra_o, rb_o, a2_o, b2_o,
    a1_d, b1_d, ra_d, rb_d, a2_d, b2_d,
    terms, from_left, from_right, hidden, stream, squares_out, squares_in, scale,
    ssem, rsem, wsem,
):
    dp, tensor = lax.axis_index("dp"), lax.axis_index("tensor")
    x, z = dp // Z, lax.rem(dp, Z)
    y, c = tensor // 2, lax.rem(tensor, 2)

    def near(dx=0, dy=0, dz=0, dc=0):
        return (
            lax.rem(x + dx, X) * Z + lax.rem(z + dz, Z),
            lax.rem(y + dy, Y) * 2 + lax.rem(c + dc, 2),
        )

    x_of = [near(dx=k) for k in range(X)]
    y_of = [near(dy=k) for k in range(Y)]
    right, left, sibling = near(dz=1), near(dz=Z - 1), near(dc=1)

    def whole_tiles(xk):
        start = ((9 * xk) // 2 + lax.rem(xk, 2)) * 128
        return pl.ds(pl.multiple_of(start, 128), 512)

    def half_tile(xk):
        start = ((9 * xk) // 2 + 4 * (1 - lax.rem(xk, 2))) * 128
        return pl.ds(pl.multiple_of(start, 128), 128)

    def block_rows(xk):
        return pl.ds(pl.multiple_of(xk * 256, 256), 224)

    def unit_blocks(xk):
        for j, w in enumerate((w_gate, w_up)):
            yield w.at[:, whole_tiles(xk)], wgu.at[block_rows(x), pl.ds(512 * j, 512)]
            yield w.at[:, half_tile(xk)], wgu.at[block_rows(x), pl.ds(1024 + 128 * j, 128)]

    def down_blocks(xk, at):
        yield w_down.at[:, whole_tiles(xk)], wd.at[at, :, pl.ds(0, 512)]
        yield w_down.at[:, half_tile(xk)], wd.at[at, :, pl.ds(512, 128)]

    pairs = [(w_o.at[:, pl.ds(pl.multiple_of(x * 512, 512), 512)], wo.at[0])]
    pairs += [*unit_blocks(x), *down_blocks(x, 0)]
    for s, block in ((1, wgu1), (3, wgu3)):
        pairs.append((block, wgu.at[block_rows(lax.rem(x - s + X, X)), :]))
    loads = [
        pltpu.make_async_copy(src, dst, wsem.at[i]) for i, (src, dst) in enumerate(pairs)
    ]
    for load in loads:
        load.start()

    barrier = pltpu.get_barrier_semaphore()
    z_of = [near(dz=k) for k in range(Z)]
    partners = x_of[1:] + y_of[1:] + z_of[1:] + [sibling]
    for device in partners:
        pl.semaphore_signal(barrier, inc=1, device_id=device, device_id_type=MESH)
    pl.semaphore_wait(barrier, len(partners))

    sent = []

    def send(src, dst, device):
        at = len(sent)
        copy = pltpu.make_async_remote_copy(
            src_ref=src, dst_ref=dst, send_sem=ssem.at[at], recv_sem=rsem.at[at],
            device_id=device, device_id_type=MESH,
        )
        copy.start()
        sent.append(copy)
        return copy

    def ring_gather(view, first, arrived):
        got = {}
        for sub in range(4):
            first(sub)
            piece = view(z, sub)
            got["r", 0, sub] = send(piece, piece, right)
            got["l", 0, sub] = send(piece, piece, left)
        for hop in range(1, 4):
            zl, zr = lax.rem(z - hop + Z, Z), lax.rem(z + hop, Z)
            for sub in range(4):
                got["r", hop - 1, sub].wait_recv()
                if hop < 3 or sub < 2:
                    piece = view(zl, sub)
                    got["r", hop, sub] = send(piece, piece, right)
                got["l", hop - 1, sub].wait_recv()
                if hop < 3 or sub >= 2:
                    piece = view(zr, sub)
                    got["l", hop, sub] = send(piece, piece, left)
            arrived(zl)
            arrived(zr)
        for sub in range(4):
            got["r" if sub < 2 else "l", 3, sub].wait_recv()
        arrived(lax.rem(z + 4, Z))

    def nt(a, b):
        return lax.dot_general(a, b, (((1,), (1,)), ((), ())), preferred_element_type=F32)

    def scatter(part, a1, b1, ra, rb, a2, b2, in_turn):
        stage_a = []
        base = len(sent)

        def to_row(k, yk):
            return pltpu.make_async_remote_copy(
                src_ref=part.at[yk, c, :, pl.ds(64, 64), :],
                dst_ref=b1.at[k - 1],
                send_sem=ssem.at[base + k - 1],
                recv_sem=rsem.at[base + k - 1],
                device_id=(dp, yk * 2 + c),
                device_id_type=MESH,
            )

        stage_b = [to_row(k, lax.rem(y + k, Y)) for k in (1, 2, 3)]
        sent.extend(stage_b)

        def first(yk):
            k = lax.rem(yk - y + Y, Y)

            @pl.when(k != 0)
            def _():
                to_row(k, yk).start()

            for j in (1, 2, 3):
                stage_a.append(
                    send(
                        part.at[yk, c, lax.rem(x + j, X), pl.ds(0, 64), :],
                        a1.at[j - 1, yk],
                        x_of[j],
                    )
                )

        def second_a(k):
            yk = lax.rem(y + k, Y)
            total = part[yk, c, x, 0:64, :].astype(F32)
            for j in (1, 2, 3):
                if in_turn:
                    stage_a[3 * ((k - 1) % Y) + j - 1].wait_recv()
                total = total + a1[j - 1, yk].astype(F32)
            if k == 0:
                return total
            ra[k] = total.astype(BF16)
            return send(ra.at[k], a2.at[k - 1], y_of[k])

        def second_b(j):
            xj = lax.rem(x + j, X)
            total = part[y, c, xj, 64:128, :].astype(F32)
            for k in range(3):
                total = total + b1[k, xj].astype(F32)
            if j == 0:
                return total
            rb[j] = total.astype(BF16)
            return send(rb.at[j], b2.at[j - 1], x_of[j])

        def finish():
            if not in_turn:
                for copy in stage_a:
                    copy.wait_recv()
            last_a = [second_a(k) for k in (1, 2, 3)]
            for copy in stage_b:
                copy.wait_recv()
            last_b = [second_b(j) for j in (1, 2, 3)]
            half_b = second_b(0)
            half_a = second_a(0)
            for k in range(3):
                last_a[k].wait_recv()
                half_a = half_a + a2[k].astype(F32)
            for k in range(3):
                last_b[k].wait_recv()
                half_b = half_b + b2[k].astype(F32)
            return half_a[:, :224], half_b[:, :224]

        return first, finish

    own_heads_copy = pltpu.make_async_copy(hv.at[x], heads.at[z, x], wsem.at[9])
    own_heads_copy.start()
    moved = [None] + [
        send(hv.at[lax.rem(x + k, X)], heads.at[z, x], x_of[k]) for k in (1, 2, 3)
    ]

    wo_moves = [
        send(
            w_o.at[:, pl.ds(pl.multiple_of(lax.rem(x + k, X) * 512, 512), 512)],
            wo.at[k],
            x_of[k],
        )
        for k in (1, 2, 3)
    ]

    def own_heads(sub):
        if sub:
            moved[sub].wait_recv()
        else:
            own_heads_copy.wait()

    unit_moves = []
    seen = []

    def heads_arrived(zi):
        seen.append(zi)
        if len(seen) == 2:
            for src, dst in unit_blocks(lax.rem(x + 2, X)):
                unit_moves.append(send(src, dst, x_of[2]))

    ring_gather(
        lambda zi, sub: heads.at[zi, lax.rem(x - sub + X, X)], own_heads, heads_arrived
    )

    loads[0].wait()
    for copy in wo_moves:
        copy.wait_recv()

    swaps = []
    for k in (1, 2, 3, 0):
        yk = lax.rem(y + k, Y)
        rows = heads[:, yk].reshape(Z * 32, 512)
        for s in range(X):
            product = nt(rows, wo[s]).astype(BF16)
            part_o[yk, :, lax.rem(x - s + X, X), :, 0:224] = product.reshape(2, 128, 224)
        swaps.append((k, yk, send(part_o.at[yk, 1 - c], sib_o.at[k], sibling)))
    first, finish = scatter(part_o, a1_o, b1_o, ra_o, rb_o, a2_o, b2_o, True)
    for k, yk, copy in swaps:
        copy.wait_recv()
        part_o[yk, c] = part_o[yk, c] + sib_o[k]
        first(yk)
    halves = finish()

    width = pl.ds(pl.multiple_of(x * 256, 256), 256)
    for h, attended in enumerate(halves):
        at = pl.ds(64 * h, 64)
        total = resid[at, :].astype(F32) + attended
        stream[at, :] = total
        squares = jnp.sum(total * total, axis=1, keepdims=True)
        high = squares.astype(BF16).astype(F32)
        low = squares - high
        lane = lax.broadcasted_iota(jnp.int32, (64, 32), 1)
        tail = jnp.where(lane == 0, high, jnp.where(lane == 1, low, 0.0))
        scaled = jnp.concatenate([total * gain[...].astype(F32), tail], axis=1)
        normed[y, c, at, width] = scaled.astype(BF16)

    upper, lower = pl.ds(0, 64), pl.ds(64, 64)

    def columns(xk):
        return pl.ds(pl.multiple_of(xk * 256, 256), 256)

    own_a, own_b = normed.at[y, c, upper, width], normed.at[y, c, lower, width]
    a_y = [send(own_a, own_a, y_of[k]) for k in (1, 2, 3)]
    b_x = [send(own_b, own_b, x_of[k]) for k in (1, 2, 3)]
    a_x = [[send(own_a, own_a, x_of[k]) for k in (1, 2, 3)]]
    b_y = [[send(own_b, own_b, y_of[k]) for k in (1, 2, 3)]]
    for k in (1, 2, 3):
        a_y[k - 1].wait_recv()
        piece = normed.at[lax.rem(y - k + Y, Y), c, upper, width]
        a_x.append([send(piece, piece, x_of[j]) for j in (1, 2, 3)])
        b_x[k - 1].wait_recv()
        piece = normed.at[y, c, lower, columns(lax.rem(x - k + X, X))]
        b_y.append([send(piece, piece, y_of[j]) for j in (1, 2, 3)])
    over = []
    piece = normed.at[:, c, upper, width]
    over.append(send(piece, piece, sibling))
    piece = normed.at[y, c, lower, :]
    over.append(send(piece, piece, sibling))
    for k in (1, 2, 3):
        for group in a_x:
            group[k - 1].wait_recv()
        piece = normed.at[:, c, upper, columns(lax.rem(x - k + X, X))]
        over.append(send(piece, piece, sibling))
        for group in b_y:
            group[k - 1].wait_recv()
        piece = normed.at[lax.rem(y - k + Y, Y), c, lower, :]
        over.append(send(piece, piece, sibling))

    for load in loads[1:]:
        load.wait()
    for copy in unit_moves:
        copy.wait_recv()
    odd = lax.rem(x, 2)
    low = lax.broadcasted_iota(jnp.int32, (1, 128), 1) < 64
    for q in range(X):
        at = pl.ds(256 * q, 256)
        gate_half = wgu[at, 1024:1152].astype(F32)
        up_half = wgu[at, 1152:1280].astype(F32)
        even_mix = jnp.where(low, gate_half, pltpu.roll(up_half, 64, 1))
        odd_mix = jnp.where(low, pltpu.roll(gate_half, 64, 1), up_half)
        wgu[at, 1024:1152] = jnp.where(odd == 1, odd_mix, even_mix).astype(BF16)
        wgu[256 * q + 224 : 256 * q + 256, :] = jnp.zeros((32, 1280), BF16)
    for copy in over:
        copy.wait_recv()

    lane = lax.broadcasted_iota(jnp.int32, (8, X * 256), 1)
    pick = jnp.where(lax.rem(lane, 256) // 2 == 112, 1.0, 0.0).astype(BF16)
    for b in range(Z):
        squares_out[b] = nt(pick, normed[b // 2, b % 2])
    square_moves = [
        send(squares_out.at[lax.rem(z + k, Z)], squares_in.at[k], z_of[k]) for k in range(1, Z)
    ]

    def expand(b):
        rows = normed[b // 2, lax.rem(b, 2)]
        terms[b] = jnp.dot(rows, wgu[:, 0:1152], preferred_element_type=F32).astype(BF16)

    def block_at(j):
        far = 4 - (j + 1) // 2
        step = jnp.where(lax.rem(j, 2) == 1, far, Z - far)
        return lax.rem(z + step, Z)

    def expand_range(lo, hi):
        def body(j, _):
            expand(block_at(j))
            return 0

        lax.fori_loop(lo, hi, body, 0)

    def sub_rows(sub):
        return pl.ds(32 * sub, 32)

    got = {}
    expand_range(0, 1)
    far = lax.rem(z + 4, Z)
    for sub in (0, 1):
        got["r", 0, sub] = send(
            terms.at[far, sub_rows(sub)], from_left.at[0, sub_rows(sub)], right
        )
        got["l", 0, sub + 2] = send(
            terms.at[far, sub_rows(sub + 2)], from_right.at[0, sub_rows(sub + 2)], left
        )
    expand_range(1, 3)
    for i in (0, 1):
        got["r", 1, i + 2] = send(
            terms.at[lax.rem(z + 3, Z), sub_rows(i + 2)],
            from_left.at[1, sub_rows(i + 2)],
            right,
        )
        got["l", 1, i] = send(
            terms.at[lax.rem(z + 5, Z), sub_rows(i)], from_right.at[1, sub_rows(i)], left
        )
    wd_moves = []
    for k in (1, 2, 3):
        for src, dst in down_blocks(lax.rem(x + k, X), k):
            wd_moves.append(send(src, dst, x_of[k]))
    expand_range(3, 8)

    def pass_on(step, sub, way):
        buffer, device = (from_left, right) if way == "r" else (from_right, left)
        b = lax.rem(z + (4 - step if way == "r" else 4 + step), Z)
        got[way, step - 1, sub].wait_recv()
        at = sub_rows(sub)
        buffer[step - 1, at] = buffer[step - 1, at] + terms[b, at]
        got[way, step, sub] = send(buffer.at[step - 1, at], buffer.at[step, at], device)

    for i in (0, 1):
        pass_on(1, i, "r")
        pass_on(1, i + 2, "l")
    for step in (2, 3):
        for i in range(4):
            pass_on(step, (i + 2) % 4, "r")
            pass_on(step, i, "l")

    squares = squares_out[z]
    for k, copy in enumerate(square_moves):
        copy.wait_recv()
        squares = squares + squares_in[k + 1]
    row = lax.broadcasted_iota(jnp.int32, (128, 128), 0)
    lane = lax.broadcasted_iota(jnp.int32, (128, 128), 1)
    diagonal = jnp.where(row == lane, jnp.broadcast_to(squares[0:1, :], (128, 128)), 0.0)
    scale[...] = lax.rsqrt(jnp.sum(diagonal, axis=1, keepdims=True) * (1.0 / D) + EPS)

    def own_hidden(sub):
        at = sub_rows(sub)
        got["r", 3, sub].wait_recv()
        got["l", 3, sub].wait_recv()
        total = (
            terms[z, at].astype(F32) + from_left[3, at].astype(F32) + from_right[3, at].astype(F32)
        )
        factor = scale[at, :]
        gate, up = total[:, :512] * factor, total[:, 512:1024] * factor
        mixed = total[:, 1024:] * factor
        half = mixed / (1.0 + jnp.exp(-mixed)) * pltpu.roll(mixed, 64, 1)
        half = jnp.where(low, half, 0.0)
        half = jnp.where(odd == 1, pltpu.roll(half, 64, 1), half)
        hidden[z, at, 0:512] = (gate / (1.0 + jnp.exp(-gate)) * up).astype(BF16)
        hidden[z, at, 512:640] = half.astype(BF16)

    def contract(b):
        rows = hidden[b]
        for s in range(X):
            product = nt(rows, wd[s]).astype(BF16)
            part_d[b // 2, lax.rem(b, 2), lax.rem(x - s + X, X), :, 0:224] = product

    for copy in wd_moves:
        copy.wait_recv()
    first, finish = scatter(part_d, a1_d, b1_d, ra_d, rb_d, a2_d, b2_d, False)

    def in_order(parity):
        odd_hops = lax.rem(z + 1 + parity, 2) == 0
        steps = ((1, 0), (Z - 1, 2), (3, Z - 2), (Z - 3, 4))
        return [lax.rem(z + jnp.where(odd_hops, a, b), Z) // 2 for a, b in steps]

    to_sibling, from_sibling = in_order(1 - c), in_order(c)
    swaps = []
    met = []

    def swap(slot):
        swaps.append(send(part_d.at[to_sibling[slot], 1 - c], sib_d.at[slot], sibling))

    def add_swapped(slot):
        swaps[slot].wait_recv()
        at = from_sibling[slot]
        part_d[at, c] = part_d[at, c] + sib_d[slot]
        first(at)

    def hidden_arrived(zi):
        if not met:
            contract(z)
        contract(zi)
        met.append(zi)
        if len(met) == 4:
            swap(0)
            swap(1)
        elif len(met) == 6:
            swap(2)
            add_swapped(0)
            add_swapped(1)
        elif len(met) == 7:
            swap(3)
            add_swapped(2)

    ring_gather(lambda zi, sub: hidden.at[zi, sub_rows(sub)], own_hidden, hidden_arrived)
    add_swapped(3)
    halves = finish()
    for h, mlp in enumerate(halves):
        at = pl.ds(64 * h, 64)
        out[at, :] = (stream[at, :] + mlp).astype(BF16)
    for copy in sent:
        copy.wait_send()


COPIES = 240


def layer(hv, resid, gain, w_gate, w_up, wgu, w_o, w_down):
    vmem = pl.BlockSpec(memory_space=pltpu.VMEM)
    hbm = pl.BlockSpec(memory_space=pl.ANY)
    halves = [
        pltpu.VMEM((3, 4, 64, 256), BF16),
        pltpu.VMEM((3, 4, 64, 256), BF16),
        pltpu.VMEM((4, 64, 256), BF16),
        pltpu.VMEM((4, 64, 256), BF16),
        pltpu.VMEM((3, 64, 256), BF16),
        pltpu.VMEM((3, 64, 256), BF16),
    ]
    return pl.pallas_call(
        layer_kernel,
        out_shape=jax.ShapeDtypeStruct((128, 224), BF16),
        in_specs=[pl.BlockSpec(memory_space=pltpu.HBM)] + [vmem] * 2 + [hbm] * 6,
        out_specs=vmem,
        scratch_shapes=[
            pltpu.VMEM((Z, X, 32, 512), BF16),
            pltpu.VMEM((Y, 2, 128, X * 256), BF16),
            pltpu.VMEM((X * 256, 1280), BF16),
            pltpu.VMEM((X, 224, 512), BF16),
            pltpu.VMEM((X, 224, 640), BF16),
            pltpu.VMEM((Y, 2, X, 128, 256), BF16),
            pltpu.VMEM((Y, 2, X, 128, 256), BF16),
            pltpu.VMEM((Y, X, 128, 256), BF16),
            pltpu.VMEM((Y, X, 128, 256), BF16),
            *halves,
            *halves,
            pltpu.VMEM((Z, 128, 1152), BF16),
            pltpu.VMEM((4, 128, 1152), BF16),
            pltpu.VMEM((4, 128, 1152), BF16),
            pltpu.VMEM((Z, 128, 640), BF16),
            pltpu.VMEM((128, 224), F32),
            pltpu.VMEM((Z, 8, 128), F32),
            pltpu.VMEM((Z, 8, 128), F32),
            pltpu.VMEM((128, 1), F32),
            pltpu.SemaphoreType.DMA((COPIES,)),
            pltpu.SemaphoreType.DMA((COPIES,)),
            pltpu.SemaphoreType.DMA((11,)),
        ],
        compiler_params=pltpu.CompilerParams(
            collective_id=0, has_side_effects=True, vmem_limit_bytes=52 * 2**20
        ),
    )(hv, resid, gain, w_gate, w_up, *wgu, w_o, w_down)


def cut_kernel(w_gate, w_up, piece1, piece3, sem):
    x = lax.axis_index("dp") // Z
    copies = []
    for i, (s, piece) in enumerate(((1, piece1), (3, piece3))):
        there = lax.rem(x + s, X)
        first, odd = (9 * there) // 2, lax.rem(there, 2)
        whole = pl.ds(pl.multiple_of((first + odd) * 128, 128), 512)
        half = pl.ds(pl.multiple_of((first + 4 * (1 - odd)) * 128, 128), 128)
        for j, w in enumerate((w_gate, w_up)):
            copies.append(
                pltpu.make_async_copy(
                    w.at[:, whole], piece.at[:, pl.ds(512 * j, 512)], sem.at[i, 2 * j]
                )
            )
            copies.append(
                pltpu.make_async_copy(
                    w.at[:, half], piece.at[:, pl.ds(1024 + 128 * j, 128)], sem.at[i, 2 * j + 1]
                )
            )
    for copy in copies:
        copy.start()
    for copy in copies:
        copy.wait()


def spread(w_gate, w_up):
    hbm = pl.BlockSpec(memory_space=pl.ANY)
    pieces = pl.pallas_call(
        cut_kernel,
        out_shape=[jax.ShapeDtypeStruct((224, 1280), BF16)] * 2,
        in_specs=[hbm] * 2,
        out_specs=[pl.BlockSpec(memory_space=pltpu.VMEM)] * 2,
        scratch_shapes=[pltpu.SemaphoreType.DMA((2, 4))],
    )(w_gate, w_up)
    got = []
    for s, piece in zip((1, 3), pieces):
        pairs = [(i, (i // Z + s) % X * Z + i % Z) for i in range(X * Z)]
        got.append(lax.ppermute(piece, "dp", pairs))
    return got


def local(
    q_lat,
    q_rope,
    fresh_lat,
    fresh_rope,
    cache_lat,
    cache_rope,
    page_table,
    hit_len,
    fresh_len,
    w_uv,
    w_o,
    resid,
    norm_gain,
    w_gate,
    w_up,
    w_down,
):
    wgu = spread(w_gate, w_up)
    head_values = attend(
        q_lat,
        q_rope,
        fresh_lat,
        fresh_rope,
        cache_lat,
        cache_rope,
        page_table,
        hit_len,
        fresh_len,
        w_uv,
    )
    return layer(
        head_values, resid, norm_gain.reshape(1, -1), w_gate, w_up, wgu, w_o.T, w_down.T
    )


def solution(mesh):
    placed = (
        P("dp", "tensor"),
        P("dp", "tensor"),
        P("dp", None),
        P("dp", None),
        P("dp", None, None),
        P("dp", None, None),
        P("dp", None, None),
        P("dp", None),
        P("dp", None),
        P("tensor", None, None),
        P("tensor", "dp"),
        P("tensor", "dp"),
        P("dp"),
        P("dp", "tensor"),
        P("dp", "tensor"),
        P("tensor", "dp"),
    )
    return jax.shard_map(
        local, mesh=mesh, in_specs=placed, out_specs=P("tensor", "dp"), check_vma=False
    )
```

```python
import functools

import jax
import jax.numpy as jnp
from jax import lax
from jax.experimental import pallas as pl
from jax.experimental.pallas import tpu as pltpu
from jax.sharding import PartitionSpec as P

D = 7168
ROPE = 64
VDIM = 128
X, Y, Z = 4, 4, 8
EPS = 1e-06
MESH = pl.DeviceIdType.MESH
F32 = jnp.float32
BF16 = jnp.bfloat16
CHUNK = 512
AHEAD = 4
LOW = -1e30
QUERIES = 384


def attend_kernel(
    table, hit, count, q_lat, q_rope, fresh_lat, fresh_rope, cache_lat, cache_rope, w_uv,
    out,
    q_all, r_all, shuffle, keys, ropes, peak, mass, acc, w_uv_here, even, odd, sem, uv_sem,
):
    pages = CHUNK // 128
    chunks0 = (hit[0, 0] + CHUNK - 1) // CHUNK
    chunks1 = (hit[0, 1] + CHUNK - 1) // CHUNK
    chunks = chunks0 + chunks1

    def place(i):
        r = (i >= chunks0).astype(jnp.int32)
        return r, i - r * chunks0

    def page_copies(i, j):
        r, k = place(i)
        page = table[0, r, k * pages + j]
        return (
            pltpu.make_async_copy(
                cache_lat.at[page], keys.at[i, pl.ds(128 * j, 128), :], sem.at[0, i, j]
            ),
            pltpu.make_async_copy(
                cache_rope.at[page], ropes.at[i, :, pl.ds(128 * j, 128)], sem.at[1, i, j]
            ),
        )

    def fetch(i):
        @pl.when(i < chunks)
        def _():
            for j in range(pages):
                for copy in page_copies(i, j):
                    copy.start()

    for i in range(AHEAD):
        fetch(jnp.int32(i))
    uv_copy = pltpu.make_async_copy(w_uv, w_uv_here, uv_sem)
    uv_copy.start()

    for h in range(16):
        for j in range(4):
            shuffle[j, pl.ds(h, 32, stride=16), :] = q_lat[
                :, 512 * h + 128 * j : 512 * h + 128 * (j + 1)
            ].astype(F32)
    for j in range(4):
        q_all[:, 128 * j : 128 * (j + 1)] = shuffle[j].astype(BF16)
    for h in range(0, 16, 2):
        pair = q_rope[:, 64 * h : 64 * h + 128].astype(F32)
        shuffle[0, pl.ds(h, 32, stride=16), :] = pair
        shuffle[0, pl.ds(h + 1, 32, stride=16), :] = jnp.concatenate(
            [pair[:, 64:], pair[:, :64]], axis=1
        )
    r_all[...] = shuffle[0, :, 0:64].astype(BF16)

    scale = (VDIM + ROPE) ** -0.5 * 1.4426950408889634
    n0 = count[0, 0]

    def nt(a, b):
        return lax.dot_general(a, b, (((1,), (1,)), ((), ())), preferred_element_type=F32)

    scores = (nt(q_all[...], fresh_lat[...]) + nt(r_all[...], fresh_rope[...])) * scale
    row = lax.broadcasted_iota(jnp.int32, (512, 32), 0) // 16
    key = lax.broadcasted_iota(jnp.int32, (512, 32), 1)
    valid = (key <= row) & ((key >= n0) | (row < n0))
    scores = jnp.where(valid, scores, LOW)
    top = jnp.max(scores, axis=1, keepdims=True)
    weight = jnp.exp2(scores - top)
    peak[...] = top
    mass[...] = jnp.sum(weight, axis=1, keepdims=True)
    product = jnp.dot(weight.astype(BF16), fresh_lat[...], preferred_element_type=F32)
    for j in range(4):
        acc[j] = product[:, 128 * j : 128 * (j + 1)]

    def ready(i):
        @pl.when(i < chunks)
        def _():
            for j in range(pages):
                for copy in page_copies(i, j):
                    copy.wait()

    def window(i):
        r, k = place(i)
        start = pl.multiple_of(r * 128, 128)
        return r, k, start, pl.ds(start, QUERIES)

    def score(i, held):
        i = jnp.minimum(i, chunks - 1)
        at = window(i)[3]
        held[...] = nt(q_all[at, :], keys[i]) + jnp.dot(
            r_all[at, :], ropes[i], preferred_element_type=F32
        )

    def absorb(i, held):
        own = jnp.minimum(i, chunks - 1)
        r, k, start, at = window(own)
        limit = jnp.where(i < chunks, hit[0, r], 0)
        position = k * CHUNK + lax.broadcasted_iota(jnp.int32, (1, CHUNK), 1)
        query = start + lax.broadcasted_iota(jnp.int32, (QUERIES, 1), 0)
        first = r * n0 * 16
        last = jnp.where(r == 0, n0 * 16, 512)
        column_bias = jnp.where(position < limit, 0.0, LOW)
        row_bias = jnp.where((query >= first) & (query < last), 0.0, LOW)
        scores = held[...] * scale + column_bias + row_bias
        before = peak[at, :]
        top = jnp.maximum(before, jnp.max(scores, axis=1, keepdims=True))
        shrink = jnp.exp2(before - top)
        weight = jnp.exp2(scores - top)
        peak[at, :] = top
        mass[at, :] = mass[at, :] * shrink + jnp.sum(weight, axis=1, keepdims=True)
        product = jnp.dot(weight.astype(BF16), keys[own], preferred_element_type=F32)
        for j in range(4):
            acc[j, at, :] = acc[j, at, :] * shrink + product[:, 128 * j : 128 * (j + 1)]

    ready(0)
    score(0, even)

    def body(t, _):
        i = 2 * t
        fetch(i + AHEAD)
        fetch(i + 1 + AHEAD)
        ready(i + 1)
        ready(i + 2)
        score(i + 1, odd)
        absorb(i, even)
        score(i + 2, even)
        absorb(i + 1, odd)
        return 0

    lax.fori_loop(0, (chunks + 1) // 2, body, 0)

    uv_copy.wait()
    inverse = 1.0 / mass[...]
    for j in range(4):
        acc[j] = acc[j] * inverse
    for h in range(16):
        rows = jnp.concatenate(
            [acc[j, pl.ds(h, 32, stride=16), :] for j in range(4)], axis=1
        ).astype(BF16)
        values = jnp.dot(rows, w_uv_here[h], preferred_element_type=F32).astype(BF16)
        out[h // 4, :, 128 * (h % 4) : 128 * (h % 4 + 1)] = values


def attend(q_lat, q_rope, fresh_lat, fresh_rope, cache_lat, cache_rope, page_table, hit_len, fresh_len, w_uv):
    vmem = pl.BlockSpec(memory_space=pltpu.VMEM)
    smem = pl.BlockSpec(memory_space=pltpu.SMEM)
    hbm = pl.BlockSpec(memory_space=pl.ANY)
    most = 8192 // CHUNK
    return pl.pallas_call(
        attend_kernel,
        out_shape=jax.ShapeDtypeStruct((4, 32, 512), BF16),
        in_specs=[smem] * 3 + [vmem] * 4 + [hbm] * 3,
        out_specs=vmem,
        scratch_shapes=[
            pltpu.VMEM((512, 512), BF16),
            pltpu.VMEM((512, 64), BF16),
            pltpu.VMEM((4, 512, 128), F32),
            pltpu.VMEM((most, CHUNK, 512), BF16),
            pltpu.VMEM((most, 64, CHUNK), BF16),
            pltpu.VMEM((512, 1), F32),
            pltpu.VMEM((512, 1), F32),
            pltpu.VMEM((4, 512, 128), F32),
            pltpu.VMEM((16, 512, 128), BF16),
            pltpu.VMEM((QUERIES, CHUNK), F32),
            pltpu.VMEM((QUERIES, CHUNK), F32),
            pltpu.SemaphoreType.DMA((2, most, CHUNK // 128)),
            pltpu.SemaphoreType.DMA,
        ],
        compiler_params=pltpu.CompilerParams(vmem_limit_bytes=61 * 2**20),
        cost_estimate=pl.CostEstimate(
            flops=20 * 10**9, bytes_accessed=12 * 2**20, transcendentals=2**22
        ),
    )(page_table, hit_len, fresh_len, q_lat, q_rope, fresh_lat, fresh_rope, cache_lat, cache_rope, w_uv)


def layer_kernel(
    hv, resid, gain,
    w_gate, w_up, wgu1, wgu3, w_o, w_down,
    out,
    heads, normed, wgu, wo, wd, part_o, part_d, sib_o, sib_d,
    a1_o, b1_o, ra_o, rb_o, a2_o, b2_o,
    a1_d, b1_d, ra_d, rb_d, a2_d, b2_d,
    terms, from_left, from_right, hidden, stream, squares_out, squares_in, scale,
    ssem, rsem, wsem,
):
    dp, tensor = lax.axis_index("dp"), lax.axis_index("tensor")
    x, z = dp // Z, lax.rem(dp, Z)
    y, c = tensor // 2, lax.rem(tensor, 2)

    def near(dx=0, dy=0, dz=0, dc=0):
        return (
            lax.rem(x + dx, X) * Z + lax.rem(z + dz, Z),
            lax.rem(y + dy, Y) * 2 + lax.rem(c + dc, 2),
        )

    x_of = [near(dx=k) for k in range(X)]
    y_of = [near(dy=k) for k in range(Y)]
    right, left, sibling = near(dz=1), near(dz=Z - 1), near(dc=1)

    def whole_tiles(xk):
        start = ((9 * xk) // 2 + lax.rem(xk, 2)) * 128
        return pl.ds(pl.multiple_of(start, 128), 512)

    def half_tile(xk):
        start = ((9 * xk) // 2 + 4 * (1 - lax.rem(xk, 2))) * 128
        return pl.ds(pl.multiple_of(start, 128), 128)

    def block_rows(xk):
        return pl.ds(pl.multiple_of(xk * 256, 256), 224)

    def unit_blocks(xk):
        for j, w in enumerate((w_gate, w_up)):
            yield w.at[:, whole_tiles(xk)], wgu.at[block_rows(x), pl.ds(512 * j, 512)]
            yield w.at[:, half_tile(xk)], wgu.at[block_rows(x), pl.ds(1024 + 128 * j, 128)]

    def down_blocks(xk, at):
        yield w_down.at[:, whole_tiles(xk)], wd.at[at, :, pl.ds(0, 512)]
        yield w_down.at[:, half_tile(xk)], wd.at[at, :, pl.ds(512, 128)]

    pairs = [(w_o.at[:, pl.ds(pl.multiple_of(x * 512, 512), 512)], wo.at[0])]
    pairs += [*unit_blocks(x), *down_blocks(x, 0)]
    for s, block in ((1, wgu1), (3, wgu3)):
        pairs.append((block, wgu.at[block_rows(lax.rem(x - s + X, X)), :]))
    loads = [
        pltpu.make_async_copy(src, dst, wsem.at[i]) for i, (src, dst) in enumerate(pairs)
    ]
    for load in loads:
        load.start()

    barrier = pltpu.get_barrier_semaphore()
    z_of = [near(dz=k) for k in range(Z)]
    partners = x_of[1:] + y_of[1:] + z_of[1:] + [sibling]
    for device in partners:
        pl.semaphore_signal(barrier, inc=1, device_id=device, device_id_type=MESH)
    pl.semaphore_wait(barrier, len(partners))

    sent = []

    def send(src, dst, device):
        at = len(sent)
        copy = pltpu.make_async_remote_copy(
            src_ref=src, dst_ref=dst, send_sem=ssem.at[at], recv_sem=rsem.at[at],
            device_id=device, device_id_type=MESH,
        )
        copy.start()
        sent.append(copy)
        return copy

    def ring_gather(view, first, arrived):
        got = {}
        for sub in range(4):
            first(sub)
            piece = view(z, sub)
            got["r", 0, sub] = send(piece, piece, right)
            got["l", 0, sub] = send(piece, piece, left)
        for hop in range(1, 4):
            zl, zr = lax.rem(z - hop + Z, Z), lax.rem(z + hop, Z)
            for sub in range(4):
                got["r", hop - 1, sub].wait_recv()
                if hop < 3 or sub < 2:
                    piece = view(zl, sub)
                    got["r", hop, sub] = send(piece, piece, right)
                got["l", hop - 1, sub].wait_recv()
                if hop < 3 or sub >= 2:
                    piece = view(zr, sub)
                    got["l", hop, sub] = send(piece, piece, left)
            arrived(zl)
            arrived(zr)
        for sub in range(4):
            got["r" if sub < 2 else "l", 3, sub].wait_recv()
        arrived(lax.rem(z + 4, Z))

    def nt(a, b):
        return lax.dot_general(a, b, (((1,), (1,)), ((), ())), preferred_element_type=F32)

    def scatter(part, a1, b1, ra, rb, a2, b2, in_turn):
        stage_a = []
        base = len(sent)

        def to_row(k, yk):
            return pltpu.make_async_remote_copy(
                src_ref=part.at[yk, c, :, pl.ds(64, 64), :],
                dst_ref=b1.at[k - 1],
                send_sem=ssem.at[base + k - 1],
                recv_sem=rsem.at[base + k - 1],
                device_id=(dp, yk * 2 + c),
                device_id_type=MESH,
            )

        stage_b = [to_row(k, lax.rem(y + k, Y)) for k in (1, 2, 3)]
        sent.extend(stage_b)

        def first(yk):
            k = lax.rem(yk - y + Y, Y)

            @pl.when(k != 0)
            def _():
                to_row(k, yk).start()

            for j in (1, 2, 3):
                stage_a.append(
                    send(
                        part.at[yk, c, lax.rem(x + j, X), pl.ds(0, 64), :],
                        a1.at[j - 1, yk],
                        x_of[j],
                    )
                )

        def second_a(k):
            yk = lax.rem(y + k, Y)
            total = part[yk, c, x, 0:64, :].astype(F32)
            for j in (1, 2, 3):
                if in_turn:
                    stage_a[3 * ((k - 1) % Y) + j - 1].wait_recv()
                total = total + a1[j - 1, yk].astype(F32)
            if k == 0:
                return total
            ra[k] = total.astype(BF16)
            return send(ra.at[k], a2.at[k - 1], y_of[k])

        def second_b(j):
            xj = lax.rem(x + j, X)
            total = part[y, c, xj, 64:128, :].astype(F32)
            for k in range(3):
                total = total + b1[k, xj].astype(F32)
            if j == 0:
                return total
            rb[j] = total.astype(BF16)
            return send(rb.at[j], b2.at[j - 1], x_of[j])

        def finish():
            if not in_turn:
                for copy in stage_a:
                    copy.wait_recv()
            last_a = [second_a(k) for k in (1, 2, 3)]
            for copy in stage_b:
                copy.wait_recv()
            last_b = [second_b(j) for j in (1, 2, 3)]
            half_b = second_b(0)
            half_a = second_a(0)
            for k in range(3):
                last_a[k].wait_recv()
                half_a = half_a + a2[k].astype(F32)
            for k in range(3):
                last_b[k].wait_recv()
                half_b = half_b + b2[k].astype(F32)
            return half_a[:, :224], half_b[:, :224]

        return first, finish

    own_heads_copy = pltpu.make_async_copy(hv.at[x], heads.at[z, x], wsem.at[9])
    own_heads_copy.start()
    moved = [None] + [
        send(hv.at[lax.rem(x + k, X)], heads.at[z, x], x_of[k]) for k in (1, 2, 3)
    ]

    wo_moves = []

    def move_heads(k):
        there = pl.ds(pl.multiple_of(lax.rem(x + k, X) * 512, 512), 512)
        wo_moves.append(send(w_o.at[:, there], wo.at[k], x_of[k]))

    def own_heads(sub):
        if sub:
            moved[sub].wait_recv()
        else:
            own_heads_copy.wait()
        if sub == 0:
            for k in (1, 2, 3):
                move_heads(k)

    unit_moves = []
    seen = []

    def heads_arrived(zi):
        seen.append(zi)
        if len(seen) == 4:
            for src, dst in unit_blocks(lax.rem(x + 2, X)):
                unit_moves.append(send(src, dst, x_of[2]))

    ring_gather(
        lambda zi, sub: heads.at[zi, lax.rem(x - sub + X, X)], own_heads, heads_arrived
    )

    loads[0].wait()
    for copy in wo_moves:
        copy.wait_recv()

    swaps = []
    for k in (1, 2, 3, 0):
        yk = lax.rem(y + k, Y)
        rows = heads[:, yk].reshape(Z * 32, 512)
        for s in range(X):
            product = nt(rows, wo[s]).astype(BF16)
            part_o[yk, :, lax.rem(x - s + X, X), :, 0:224] = product.reshape(2, 128, 224)
        swaps.append((k, yk, send(part_o.at[yk, 1 - c], sib_o.at[k], sibling)))
    first, finish = scatter(part_o, a1_o, b1_o, ra_o, rb_o, a2_o, b2_o, True)
    for k, yk, copy in swaps:
        copy.wait_recv()
        part_o[yk, c] = part_o[yk, c] + sib_o[k]
        first(yk)
    halves = finish()

    width = pl.ds(pl.multiple_of(x * 256, 256), 256)
    for h, attended in enumerate(halves):
        at = pl.ds(64 * h, 64)
        total = resid[at, :].astype(F32) + attended
        stream[at, :] = total
        squares = jnp.sum(total * total, axis=1, keepdims=True)
        high = squares.astype(BF16).astype(F32)
        low = squares - high
        lane = lax.broadcasted_iota(jnp.int32, (64, 32), 1)
        tail = jnp.where(lane == 0, high, jnp.where(lane == 1, low, 0.0))
        scaled = jnp.concatenate([total * gain[...].astype(F32), tail], axis=1)
        normed[y, c, at, width] = scaled.astype(BF16)

    upper, lower = pl.ds(0, 64), pl.ds(64, 64)

    def columns(xk):
        return pl.ds(pl.multiple_of(xk * 256, 256), 256)

    own_a, own_b = normed.at[y, c, upper, width], normed.at[y, c, lower, width]
    a_y = [send(own_a, own_a, y_of[k]) for k in (1, 2, 3)]
    b_x = [send(own_b, own_b, x_of[k]) for k in (1, 2, 3)]
    a_x = [[send(own_a, own_a, x_of[k]) for k in (1, 2, 3)]]
    b_y = [[send(own_b, own_b, y_of[k]) for k in (1, 2, 3)]]
    for k in (1, 2, 3):
        a_y[k - 1].wait_recv()
        piece = normed.at[lax.rem(y - k + Y, Y), c, upper, width]
        a_x.append([send(piece, piece, x_of[j]) for j in (1, 2, 3)])
        b_x[k - 1].wait_recv()
        piece = normed.at[y, c, lower, columns(lax.rem(x - k + X, X))]
        b_y.append([send(piece, piece, y_of[j]) for j in (1, 2, 3)])
    over = []
    piece = normed.at[:, c, upper, width]
    over.append(send(piece, piece, sibling))
    piece = normed.at[y, c, lower, :]
    over.append(send(piece, piece, sibling))
    for k in (1, 2, 3):
        for group in a_x:
            group[k - 1].wait_recv()
        piece = normed.at[:, c, upper, columns(lax.rem(x - k + X, X))]
        over.append(send(piece, piece, sibling))
        for group in b_y:
            group[k - 1].wait_recv()
        piece = normed.at[lax.rem(y - k + Y, Y), c, lower, :]
        over.append(send(piece, piece, sibling))

    for load in loads[1:]:
        load.wait()
    for copy in unit_moves:
        copy.wait_recv()
    odd = lax.rem(x, 2)
    low = lax.broadcasted_iota(jnp.int32, (1, 128), 1) < 64
    for q in range(X):
        at = pl.ds(256 * q, 256)
        gate_half = wgu[at, 1024:1152].astype(F32)
        up_half = wgu[at, 1152:1280].astype(F32)
        even_mix = jnp.where(low, gate_half, pltpu.roll(up_half, 64, 1))
        odd_mix = jnp.where(low, pltpu.roll(gate_half, 64, 1), up_half)
        wgu[at, 1024:1152] = jnp.where(odd == 1, odd_mix, even_mix).astype(BF16)
        wgu[256 * q + 224 : 256 * q + 256, :] = jnp.zeros((32, 1280), BF16)
    for copy in over:
        copy.wait_recv()

    lane = lax.broadcasted_iota(jnp.int32, (8, X * 256), 1)
    pick = jnp.where(lax.rem(lane, 256) // 2 == 112, 1.0, 0.0).astype(BF16)
    for b in range(Z):
        squares_out[b] = nt(pick, normed[b // 2, b % 2])
    square_moves = [
        send(squares_out.at[lax.rem(z + k, Z)], squares_in.at[k], z_of[k]) for k in range(1, Z)
    ]

    def expand(b):
        rows = normed[b // 2, lax.rem(b, 2)]
        terms[b] = jnp.dot(rows, wgu[:, 0:1152], preferred_element_type=F32).astype(BF16)

    def block_at(j):
        far = 4 - (j + 1) // 2
        step = jnp.where(lax.rem(j, 2) == 1, far, Z - far)
        return lax.rem(z + step, Z)

    def expand_range(lo, hi):
        def body(j, _):
            expand(block_at(j))
            return 0

        lax.fori_loop(lo, hi, body, 0)

    def sub_rows(sub):
        return pl.ds(32 * sub, 32)

    got = {}
    expand_range(0, 1)
    far = lax.rem(z + 4, Z)
    for sub in (0, 1):
        got["r", 0, sub] = send(
            terms.at[far, sub_rows(sub)], from_left.at[0, sub_rows(sub)], right
        )
        got["l", 0, sub + 2] = send(
            terms.at[far, sub_rows(sub + 2)], from_right.at[0, sub_rows(sub + 2)], left
        )
    expand_range(1, 3)
    for i in (0, 1):
        got["r", 1, i + 2] = send(
            terms.at[lax.rem(z + 3, Z), sub_rows(i + 2)],
            from_left.at[1, sub_rows(i + 2)],
            right,
        )
        got["l", 1, i] = send(
            terms.at[lax.rem(z + 5, Z), sub_rows(i)], from_right.at[1, sub_rows(i)], left
        )
    wd_moves = []
    for k in (1, 2, 3):
        for src, dst in down_blocks(lax.rem(x + k, X), k):
            wd_moves.append(send(src, dst, x_of[k]))
    expand_range(3, 8)

    def pass_on(step, sub, way):
        buffer, device = (from_left, right) if way == "r" else (from_right, left)
        b = lax.rem(z + (4 - step if way == "r" else 4 + step), Z)
        got[way, step - 1, sub].wait_recv()
        at = sub_rows(sub)
        buffer[step - 1, at] = buffer[step - 1, at] + terms[b, at]
        got[way, step, sub] = send(buffer.at[step - 1, at], buffer.at[step, at], device)

    for i in (0, 1):
        pass_on(1, i, "r")
        pass_on(1, i + 2, "l")
    for step in (2, 3):
        for i in range(4):
            pass_on(step, (i + 2) % 4, "r")
            pass_on(step, i, "l")

    squares = squares_out[z]
    for k, copy in enumerate(square_moves):
        copy.wait_recv()
        squares = squares + squares_in[k + 1]
    row = lax.broadcasted_iota(jnp.int32, (128, 128), 0)
    lane = lax.broadcasted_iota(jnp.int32, (128, 128), 1)
    diagonal = jnp.where(row == lane, jnp.broadcast_to(squares[0:1, :], (128, 128)), 0.0)
    scale[...] = lax.rsqrt(jnp.sum(diagonal, axis=1, keepdims=True) * (1.0 / D) + EPS)

    def own_hidden(sub):
        at = sub_rows(sub)
        got["r", 3, sub].wait_recv()
        got["l", 3, sub].wait_recv()
        total = (
            terms[z, at].astype(F32) + from_left[3, at].astype(F32) + from_right[3, at].astype(F32)
        )
        factor = scale[at, :]
        gate, up = total[:, :512] * factor, total[:, 512:1024] * factor
        mixed = total[:, 1024:] * factor
        half = mixed / (1.0 + jnp.exp(-mixed)) * pltpu.roll(mixed, 64, 1)
        half = jnp.where(low, half, 0.0)
        half = jnp.where(odd == 1, pltpu.roll(half, 64, 1), half)
        hidden[z, at, 0:512] = (gate / (1.0 + jnp.exp(-gate)) * up).astype(BF16)
        hidden[z, at, 512:640] = half.astype(BF16)

    def contract(b):
        rows = hidden[b]
        for s in range(X):
            product = nt(rows, wd[s]).astype(BF16)
            part_d[b // 2, lax.rem(b, 2), lax.rem(x - s + X, X), :, 0:224] = product

    for copy in wd_moves:
        copy.wait_recv()
    first, finish = scatter(part_d, a1_d, b1_d, ra_d, rb_d, a2_d, b2_d, False)

    def in_order(parity):
        odd_hops = lax.rem(z + 1 + parity, 2) == 0
        steps = ((1, 0), (Z - 1, 2), (3, Z - 2), (Z - 3, 4))
        return [lax.rem(z + jnp.where(odd_hops, a, b), Z) // 2 for a, b in steps]

    to_sibling, from_sibling = in_order(1 - c), in_order(c)
    swaps = []
    met = []

    def swap(slot):
        swaps.append(send(part_d.at[to_sibling[slot], 1 - c], sib_d.at[slot], sibling))

    def add_swapped(slot):
        swaps[slot].wait_recv()
        at = from_sibling[slot]
        part_d[at, c] = part_d[at, c] + sib_d[slot]
        first(at)

    def hidden_arrived(zi):
        if not met:
            contract(z)
        contract(zi)
        met.append(zi)
        if len(met) == 4:
            swap(0)
            swap(1)
        elif len(met) == 6:
            swap(2)
            add_swapped(0)
            add_swapped(1)
        elif len(met) == 7:
            swap(3)
            add_swapped(2)

    ring_gather(lambda zi, sub: hidden.at[zi, sub_rows(sub)], own_hidden, hidden_arrived)
    add_swapped(3)
    halves = finish()
    for h, mlp in enumerate(halves):
        at = pl.ds(64 * h, 64)
        out[at, :] = (stream[at, :] + mlp).astype(BF16)
    for copy in sent:
        copy.wait_send()


COPIES = 240


def layer(hv, resid, gain, w_gate, w_up, wgu, w_o, w_down):
    vmem = pl.BlockSpec(memory_space=pltpu.VMEM)
    hbm = pl.BlockSpec(memory_space=pl.ANY)
    halves = [
        pltpu.VMEM((3, 4, 64, 256), BF16),
        pltpu.VMEM((3, 4, 64, 256), BF16),
        pltpu.VMEM((4, 64, 256), BF16),
        pltpu.VMEM((4, 64, 256), BF16),
        pltpu.VMEM((3, 64, 256), BF16),
        pltpu.VMEM((3, 64, 256), BF16),
    ]
    return pl.pallas_call(
        layer_kernel,
        out_shape=jax.ShapeDtypeStruct((128, 224), BF16),
        in_specs=[pl.BlockSpec(memory_space=pltpu.HBM)] + [vmem] * 2 + [hbm] * 6,
        out_specs=vmem,
        scratch_shapes=[
            pltpu.VMEM((Z, X, 32, 512), BF16),
            pltpu.VMEM((Y, 2, 128, X * 256), BF16),
            pltpu.VMEM((X * 256, 1280), BF16),
            pltpu.VMEM((X, 224, 512), BF16),
            pltpu.VMEM((X, 224, 640), BF16),
            pltpu.VMEM((Y, 2, X, 128, 256), BF16),
            pltpu.VMEM((Y, 2, X, 128, 256), BF16),
            pltpu.VMEM((Y, X, 128, 256), BF16),
            pltpu.VMEM((Y, X, 128, 256), BF16),
            *halves,
            *halves,
            pltpu.VMEM((Z, 128, 1152), BF16),
            pltpu.VMEM((4, 128, 1152), BF16),
            pltpu.VMEM((4, 128, 1152), BF16),
            pltpu.VMEM((Z, 128, 640), BF16),
            pltpu.VMEM((128, 224), F32),
            pltpu.VMEM((Z, 8, 128), F32),
            pltpu.VMEM((Z, 8, 128), F32),
            pltpu.VMEM((128, 1), F32),
            pltpu.SemaphoreType.DMA((COPIES,)),
            pltpu.SemaphoreType.DMA((COPIES,)),
            pltpu.SemaphoreType.DMA((11,)),
        ],
        compiler_params=pltpu.CompilerParams(
            collective_id=0, has_side_effects=True, vmem_limit_bytes=52 * 2**20
        ),
    )(hv, resid, gain, w_gate, w_up, *wgu, w_o, w_down)


def cut_kernel(w_gate, w_up, piece1, piece3, sem):
    x = lax.axis_index("dp") // Z
    copies = []
    for i, (s, piece) in enumerate(((1, piece1), (3, piece3))):
        there = lax.rem(x + s, X)
        first, odd = (9 * there) // 2, lax.rem(there, 2)
        whole = pl.ds(pl.multiple_of((first + odd) * 128, 128), 512)
        half = pl.ds(pl.multiple_of((first + 4 * (1 - odd)) * 128, 128), 128)
        for j, w in enumerate((w_gate, w_up)):
            copies.append(
                pltpu.make_async_copy(
                    w.at[:, whole], piece.at[:, pl.ds(512 * j, 512)], sem.at[i, 2 * j]
                )
            )
            copies.append(
                pltpu.make_async_copy(
                    w.at[:, half], piece.at[:, pl.ds(1024 + 128 * j, 128)], sem.at[i, 2 * j + 1]
                )
            )
    for copy in copies:
        copy.start()
    for copy in copies:
        copy.wait()


def spread(w_gate, w_up):
    hbm = pl.BlockSpec(memory_space=pl.ANY)
    pieces = pl.pallas_call(
        cut_kernel,
        out_shape=[jax.ShapeDtypeStruct((224, 1280), BF16)] * 2,
        in_specs=[hbm] * 2,
        out_specs=[pl.BlockSpec(memory_space=pltpu.VMEM)] * 2,
        scratch_shapes=[pltpu.SemaphoreType.DMA((2, 4))],
    )(w_gate, w_up)
    got = []
    for s, piece in zip((1, 3), pieces):
        pairs = [(i, (i // Z + s) % X * Z + i % Z) for i in range(X * Z)]
        got.append(lax.ppermute(piece, "dp", pairs))
    return got


def local(
    q_lat,
    q_rope,
    fresh_lat,
    fresh_rope,
    cache_lat,
    cache_rope,
    page_table,
    hit_len,
    fresh_len,
    w_uv,
    w_o,
    resid,
    norm_gain,
    w_gate,
    w_up,
    w_down,
):
    wgu = spread(w_gate, w_up)
    head_values = attend(
        q_lat,
        q_rope,
        fresh_lat,
        fresh_rope,
        cache_lat,
        cache_rope,
        page_table,
        hit_len,
        fresh_len,
        w_uv,
    )
    return layer(
        head_values, resid, norm_gain.reshape(1, -1), w_gate, w_up, wgu, w_o.T, w_down.T
    )


def solution(mesh):
    placed = (
        P("dp", "tensor"),
        P("dp", "tensor"),
        P("dp", None),
        P("dp", None),
        P("dp", None, None),
        P("dp", None, None),
        P("dp", None, None),
        P("dp", None),
        P("dp", None),
        P("tensor", None, None),
        P("tensor", "dp"),
        P("tensor", "dp"),
        P("dp"),
        P("dp", "tensor"),
        P("dp", "tensor"),
        P("tensor", "dp"),
    )
    return jax.shard_map(
        local, mesh=mesh, in_specs=placed, out_specs=P("tensor", "dp"), check_vma=False
    )
```

```python
import functools

import jax
import jax.numpy as jnp
from jax import lax
from jax.experimental import pallas as pl
from jax.experimental.pallas import tpu as pltpu
from jax.sharding import PartitionSpec as P

D = 7168
ROPE = 64
VDIM = 128
X, Y, Z = 4, 4, 8
EPS = 1e-06
MESH = pl.DeviceIdType.MESH
F32 = jnp.float32
BF16 = jnp.bfloat16
CHUNK = 512
AHEAD = 4
LOW = -1e30
QUERIES = 384


def attend_kernel(
    table, hit, count, q_lat, q_rope, fresh_lat, fresh_rope, cache_lat, cache_rope, w_uv,
    out,
    q_all, r_all, shuffle, keys, ropes, peak, mass, acc, w_uv_here, even, odd, sem, uv_sem,
):
    pages = CHUNK // 128
    chunks0 = (hit[0, 0] + CHUNK - 1) // CHUNK
    chunks1 = (hit[0, 1] + CHUNK - 1) // CHUNK
    chunks = chunks0 + chunks1

    def place(i):
        r = (i >= chunks0).astype(jnp.int32)
        return r, i - r * chunks0

    def page_copies(i, j):
        r, k = place(i)
        page = table[0, r, k * pages + j]
        return (
            pltpu.make_async_copy(
                cache_lat.at[page], keys.at[i, pl.ds(128 * j, 128), :], sem.at[0, i, j]
            ),
            pltpu.make_async_copy(
                cache_rope.at[page], ropes.at[i, :, pl.ds(128 * j, 128)], sem.at[1, i, j]
            ),
        )

    def fetch(i):
        @pl.when(i < chunks)
        def _():
            for j in range(pages):
                for copy in page_copies(i, j):
                    copy.start()

    for i in range(AHEAD):
        fetch(jnp.int32(i))
    uv_copy = pltpu.make_async_copy(w_uv, w_uv_here, uv_sem)
    uv_copy.start()

    for h in range(16):
        for j in range(4):
            shuffle[j, pl.ds(h, 32, stride=16), :] = q_lat[
                :, 512 * h + 128 * j : 512 * h + 128 * (j + 1)
            ].astype(F32)
    for j in range(4):
        q_all[:, 128 * j : 128 * (j + 1)] = shuffle[j].astype(BF16)
    for h in range(0, 16, 2):
        pair = q_rope[:, 64 * h : 64 * h + 128].astype(F32)
        shuffle[0, pl.ds(h, 32, stride=16), :] = pair
        shuffle[0, pl.ds(h + 1, 32, stride=16), :] = jnp.concatenate(
            [pair[:, 64:], pair[:, :64]], axis=1
        )
    r_all[...] = shuffle[0, :, 0:64].astype(BF16)

    scale = (VDIM + ROPE) ** -0.5 * 1.4426950408889634
    n0 = count[0, 0]

    def nt(a, b):
        return lax.dot_general(a, b, (((1,), (1,)), ((), ())), preferred_element_type=F32)

    scores = (nt(q_all[...], fresh_lat[...]) + nt(r_all[...], fresh_rope[...])) * scale
    row = lax.broadcasted_iota(jnp.int32, (512, 32), 0) // 16
    key = lax.broadcasted_iota(jnp.int32, (512, 32), 1)
    valid = (key <= row) & ((key >= n0) | (row < n0))
    scores = jnp.where(valid, scores, LOW)
    top = jnp.max(scores, axis=1, keepdims=True)
    weight = jnp.exp2(scores - top)
    peak[...] = top
    mass[...] = jnp.sum(weight, axis=1, keepdims=True)
    product = jnp.dot(weight.astype(BF16), fresh_lat[...], preferred_element_type=F32)
    for j in range(4):
        acc[j] = product[:, 128 * j : 128 * (j + 1)]

    def ready(i):
        @pl.when(i < chunks)
        def _():
            for j in range(pages):
                for copy in page_copies(i, j):
                    copy.wait()

    def window(i):
        r, k = place(i)
        start = pl.multiple_of(r * 128, 128)
        return r, k, start, pl.ds(start, QUERIES)

    def score(i, held):
        i = jnp.minimum(i, chunks - 1)
        at = window(i)[3]
        held[...] = nt(q_all[at, :], keys[i]) + jnp.dot(
            r_all[at, :], ropes[i], preferred_element_type=F32
        )

    def absorb(i, held):
        own = jnp.minimum(i, chunks - 1)
        r, k, start, at = window(own)
        limit = jnp.where(i < chunks, hit[0, r], 0)
        position = k * CHUNK + lax.broadcasted_iota(jnp.int32, (1, CHUNK), 1)
        query = start + lax.broadcasted_iota(jnp.int32, (QUERIES, 1), 0)
        first = r * n0 * 16
        last = jnp.where(r == 0, n0 * 16, 512)
        column_bias = jnp.where(position < limit, 0.0, LOW)
        row_bias = jnp.where((query >= first) & (query < last), 0.0, LOW)
        scores = held[...] * scale + column_bias + row_bias
        before = peak[at, :]
        top = jnp.maximum(before, jnp.max(scores, axis=1, keepdims=True))
        shrink = jnp.exp2(before - top)
        weight = jnp.exp2(scores - top)
        peak[at, :] = top
        mass[at, :] = mass[at, :] * shrink + jnp.sum(weight, axis=1, keepdims=True)
        product = jnp.dot(weight.astype(BF16), keys[own], preferred_element_type=F32)
        for j in range(4):
            acc[j, at, :] = acc[j, at, :] * shrink + product[:, 128 * j : 128 * (j + 1)]

    ready(0)
    score(0, even)

    def body(t, _):
        i = 2 * t
        fetch(i + AHEAD)
        fetch(i + 1 + AHEAD)
        ready(i + 1)
        ready(i + 2)
        score(i + 1, odd)
        absorb(i, even)
        score(i + 2, even)
        absorb(i + 1, odd)
        return 0

    lax.fori_loop(0, (chunks + 1) // 2, body, 0)

    uv_copy.wait()
    inverse = 1.0 / mass[...]
    for j in range(4):
        acc[j] = acc[j] * inverse
    for h in range(16):
        rows = jnp.concatenate(
            [acc[j, pl.ds(h, 32, stride=16), :] for j in range(4)], axis=1
        ).astype(BF16)
        values = jnp.dot(rows, w_uv_here[h], preferred_element_type=F32).astype(BF16)
        out[h // 4, :, 128 * (h % 4) : 128 * (h % 4 + 1)] = values


def attend(q_lat, q_rope, fresh_lat, fresh_rope, cache_lat, cache_rope, page_table, hit_len, fresh_len, w_uv):
    vmem = pl.BlockSpec(memory_space=pltpu.VMEM)
    smem = pl.BlockSpec(memory_space=pltpu.SMEM)
    hbm = pl.BlockSpec(memory_space=pl.ANY)
    most = 8192 // CHUNK
    return pl.pallas_call(
        attend_kernel,
        out_shape=jax.ShapeDtypeStruct((4, 32, 512), BF16),
        in_specs=[smem] * 3 + [vmem] * 4 + [hbm] * 3,
        out_specs=vmem,
        scratch_shapes=[
            pltpu.VMEM((512, 512), BF16),
            pltpu.VMEM((512, 64), BF16),
            pltpu.VMEM((4, 512, 128), F32),
            pltpu.VMEM((most, CHUNK, 512), BF16),
            pltpu.VMEM((most, 64, CHUNK), BF16),
            pltpu.VMEM((512, 1), F32),
            pltpu.VMEM((512, 1), F32),
            pltpu.VMEM((4, 512, 128), F32),
            pltpu.VMEM((16, 512, 128), BF16),
            pltpu.VMEM((QUERIES, CHUNK), F32),
            pltpu.VMEM((QUERIES, CHUNK), F32),
            pltpu.SemaphoreType.DMA((2, most, CHUNK // 128)),
            pltpu.SemaphoreType.DMA,
        ],
        compiler_params=pltpu.CompilerParams(vmem_limit_bytes=61 * 2**20),
        cost_estimate=pl.CostEstimate(
            flops=20 * 10**9, bytes_accessed=12 * 2**20, transcendentals=2**22
        ),
    )(page_table, hit_len, fresh_len, q_lat, q_rope, fresh_lat, fresh_rope, cache_lat, cache_rope, w_uv)


def layer_kernel(
    hv, resid, gain,
    w_gate, w_up, wgu1, wgu3, w_o, w_down,
    out,
    heads, normed, wgu, wo, wd, part_o, part_d, sib_o, sib_d,
    a1_o, b1_o, ra_o, rb_o, a2_o, b2_o,
    a1_d, b1_d, ra_d, rb_d, a2_d, b2_d,
    terms, from_left, from_right, hidden, stream, squares_out, squares_in, scale,
    ssem, rsem, wsem,
):
    dp, tensor = lax.axis_index("dp"), lax.axis_index("tensor")
    x, z = dp // Z, lax.rem(dp, Z)
    y, c = tensor // 2, lax.rem(tensor, 2)

    def near(dx=0, dy=0, dz=0, dc=0):
        return (
            lax.rem(x + dx, X) * Z + lax.rem(z + dz, Z),
            lax.rem(y + dy, Y) * 2 + lax.rem(c + dc, 2),
        )

    x_of = [near(dx=k) for k in range(X)]
    y_of = [near(dy=k) for k in range(Y)]
    right, left, sibling = near(dz=1), near(dz=Z - 1), near(dc=1)

    def whole_tiles(xk):
        start = ((9 * xk) // 2 + lax.rem(xk, 2)) * 128
        return pl.ds(pl.multiple_of(start, 128), 512)

    def half_tile(xk):
        start = ((9 * xk) // 2 + 4 * (1 - lax.rem(xk, 2))) * 128
        return pl.ds(pl.multiple_of(start, 128), 128)

    def block_rows(xk):
        return pl.ds(pl.multiple_of(xk * 256, 256), 224)

    def unit_blocks(xk):
        for j, w in enumerate((w_gate, w_up)):
            yield w.at[:, whole_tiles(xk)], wgu.at[block_rows(x), pl.ds(512 * j, 512)]
            yield w.at[:, half_tile(xk)], wgu.at[block_rows(x), pl.ds(1024 + 128 * j, 128)]

    def down_blocks(xk, at):
        yield w_down.at[:, whole_tiles(xk)], wd.at[at, :, pl.ds(0, 512)]
        yield w_down.at[:, half_tile(xk)], wd.at[at, :, pl.ds(512, 128)]

    pairs = [(w_o.at[:, pl.ds(pl.multiple_of(x * 512, 512), 512)], wo.at[0])]
    pairs += [*unit_blocks(x), *down_blocks(x, 0)]
    for s, block in ((1, wgu1), (3, wgu3)):
        pairs.append((block, wgu.at[block_rows(lax.rem(x - s + X, X)), :]))
    loads = [
        pltpu.make_async_copy(src, dst, wsem.at[i]) for i, (src, dst) in enumerate(pairs)
    ]
    for load in loads:
        load.start()

    barrier = pltpu.get_barrier_semaphore()
    z_of = [near(dz=k) for k in range(Z)]
    partners = x_of[1:] + y_of[1:] + z_of[1:] + [sibling]
    for device in partners:
        pl.semaphore_signal(barrier, inc=1, device_id=device, device_id_type=MESH)
    pl.semaphore_wait(barrier, len(partners))

    sent = []

    def send(src, dst, device):
        at = len(sent)
        copy = pltpu.make_async_remote_copy(
            src_ref=src, dst_ref=dst, send_sem=ssem.at[at], recv_sem=rsem.at[at],
            device_id=device, device_id_type=MESH,
        )
        copy.start()
        sent.append(copy)
        return copy

    def ring_gather(view, first, arrived, order=(0, 1, 2, 3)):
        got = {}
        for sub in order:
            first(sub)
            piece = view(z, sub)
            got["r", 0, sub] = send(piece, piece, right)
            got["l", 0, sub] = send(piece, piece, left)
        for hop in range(1, 4):
            zl, zr = lax.rem(z - hop + Z, Z), lax.rem(z + hop, Z)
            for sub in order:
                got["r", hop - 1, sub].wait_recv()
                if hop < 3 or sub < 2:
                    piece = view(zl, sub)
                    got["r", hop, sub] = send(piece, piece, right)
                got["l", hop - 1, sub].wait_recv()
                if hop < 3 or sub >= 2:
                    piece = view(zr, sub)
                    got["l", hop, sub] = send(piece, piece, left)
            arrived(zl)
            arrived(zr)
        for sub in order:
            got["r" if sub < 2 else "l", 3, sub].wait_recv()
        arrived(lax.rem(z + 4, Z))

    def nt(a, b):
        return lax.dot_general(a, b, (((1,), (1,)), ((), ())), preferred_element_type=F32)

    def scatter(part, a1, b1, ra, rb, a2, b2, in_turn):
        stage_a = []
        base = len(sent)

        def to_row(k, yk):
            return pltpu.make_async_remote_copy(
                src_ref=part.at[yk, c, :, pl.ds(64, 64), :],
                dst_ref=b1.at[k - 1],
                send_sem=ssem.at[base + k - 1],
                recv_sem=rsem.at[base + k - 1],
                device_id=(dp, yk * 2 + c),
                device_id_type=MESH,
            )

        stage_b = [to_row(k, lax.rem(y + k, Y)) for k in (1, 2, 3)]
        sent.extend(stage_b)

        def first(yk):
            k = lax.rem(yk - y + Y, Y)

            @pl.when(k != 0)
            def _():
                to_row(k, yk).start()

            for j in (1, 2, 3):
                stage_a.append(
                    send(
                        part.at[yk, c, lax.rem(x + j, X), pl.ds(0, 64), :],
                        a1.at[j - 1, yk],
                        x_of[j],
                    )
                )

        def second_a(k):
            yk = lax.rem(y + k, Y)
            total = part[yk, c, x, 0:64, :].astype(F32)
            for j in (1, 2, 3):
                if in_turn:
                    stage_a[3 * ((k - 1) % Y) + j - 1].wait_recv()
                total = total + a1[j - 1, yk].astype(F32)
            if k == 0:
                return total
            ra[k] = total.astype(BF16)
            return send(ra.at[k], a2.at[k - 1], y_of[k])

        def second_b(j):
            xj = lax.rem(x + j, X)
            total = part[y, c, xj, 64:128, :].astype(F32)
            for k in range(3):
                total = total + b1[k, xj].astype(F32)
            if j == 0:
                return total
            rb[j] = total.astype(BF16)
            return send(rb.at[j], b2.at[j - 1], x_of[j])

        def finish():
            if not in_turn:
                for copy in stage_a:
                    copy.wait_recv()
            last_a = [second_a(k) for k in (1, 2, 3)]
            for copy in stage_b:
                copy.wait_recv()
            last_b = [second_b(j) for j in (1, 2, 3)]
            half_b = second_b(0)
            half_a = second_a(0)
            for k in range(3):
                last_a[k].wait_recv()
                half_a = half_a + a2[k].astype(F32)
            for k in range(3):
                last_b[k].wait_recv()
                half_b = half_b + b2[k].astype(F32)
            return half_a[:, :224], half_b[:, :224]

        return first, finish

    own_heads_copy = pltpu.make_async_copy(hv.at[x], heads.at[z, x], wsem.at[9])
    own_heads_copy.start()
    moved = [None] + [
        send(hv.at[lax.rem(x + k, X)], heads.at[z, x], x_of[k]) for k in (1, 2, 3)
    ]

    wo_moves = []

    def move_heads(k):
        there = pl.ds(pl.multiple_of(lax.rem(x + k, X) * 512, 512), 512)
        wo_moves.append(send(w_o.at[:, there], wo.at[k], x_of[k]))

    def own_heads(sub):
        if sub:
            moved[sub].wait_recv()
        else:
            own_heads_copy.wait()
        if sub == 0:
            for k in (1, 2, 3):
                move_heads(k)

    unit_moves = []
    seen = []

    def heads_arrived(zi):
        seen.append(zi)
        if len(seen) == 4:
            for src, dst in unit_blocks(lax.rem(x + 2, X)):
                unit_moves.append(send(src, dst, x_of[2]))

    ring_gather(
        lambda zi, sub: heads.at[zi, lax.rem(x - sub + X, X)], own_heads, heads_arrived
    )

    loads[0].wait()
    for copy in wo_moves:
        copy.wait_recv()

    swaps = []
    for k in (1, 2, 3, 0):
        yk = lax.rem(y + k, Y)
        rows = heads[:, yk].reshape(Z * 32, 512)
        for s in range(X):
            product = nt(rows, wo[s]).astype(BF16)
            part_o[yk, :, lax.rem(x - s + X, X), :, 0:224] = product.reshape(2, 128, 224)
        swaps.append((k, yk, send(part_o.at[yk, 1 - c], sib_o.at[k], sibling)))
    first, finish = scatter(part_o, a1_o, b1_o, ra_o, rb_o, a2_o, b2_o, True)
    for k, yk, copy in swaps:
        copy.wait_recv()
        part_o[yk, c] = part_o[yk, c] + sib_o[k]
        first(yk)
    halves = finish()

    width = pl.ds(pl.multiple_of(x * 256, 256), 256)
    for h, attended in enumerate(halves):
        at = pl.ds(64 * h, 64)
        total = resid[at, :].astype(F32) + attended
        stream[at, :] = total
        squares = jnp.sum(total * total, axis=1, keepdims=True)
        high = squares.astype(BF16).astype(F32)
        low = squares - high
        lane = lax.broadcasted_iota(jnp.int32, (64, 32), 1)
        tail = jnp.where(lane == 0, high, jnp.where(lane == 1, low, 0.0))
        scaled = jnp.concatenate([total * gain[...].astype(F32), tail], axis=1)
        normed[y, c, at, width] = scaled.astype(BF16)

    upper, lower = pl.ds(0, 64), pl.ds(64, 64)

    def columns(xk):
        return pl.ds(pl.multiple_of(xk * 256, 256), 256)

    own_a, own_b = normed.at[y, c, upper, width], normed.at[y, c, lower, width]
    a_y = [send(own_a, own_a, y_of[k]) for k in (1, 2, 3)]
    b_x = [send(own_b, own_b, x_of[k]) for k in (1, 2, 3)]
    a_x = [[send(own_a, own_a, x_of[k]) for k in (1, 2, 3)]]
    b_y = [[send(own_b, own_b, y_of[k]) for k in (1, 2, 3)]]
    for k in (1, 2, 3):
        a_y[k - 1].wait_recv()
        piece = normed.at[lax.rem(y - k + Y, Y), c, upper, width]
        a_x.append([send(piece, piece, x_of[j]) for j in (1, 2, 3)])
        b_x[k - 1].wait_recv()
        piece = normed.at[y, c, lower, columns(lax.rem(x - k + X, X))]
        b_y.append([send(piece, piece, y_of[j]) for j in (1, 2, 3)])
    over = []
    piece = normed.at[:, c, upper, width]
    over.append(send(piece, piece, sibling))
    piece = normed.at[y, c, lower, :]
    over.append(send(piece, piece, sibling))
    for k in (1, 2, 3):
        for group in a_x:
            group[k - 1].wait_recv()
        piece = normed.at[:, c, upper, columns(lax.rem(x - k + X, X))]
        over.append(send(piece, piece, sibling))
        for group in b_y:
            group[k - 1].wait_recv()
        piece = normed.at[lax.rem(y - k + Y, Y), c, lower, :]
        over.append(send(piece, piece, sibling))

    for load in loads[1:]:
        load.wait()
    for copy in unit_moves:
        copy.wait_recv()
    odd = lax.rem(x, 2)
    low = lax.broadcasted_iota(jnp.int32, (1, 128), 1) < 64
    for q in range(X):
        at = pl.ds(256 * q, 256)
        gate_half = wgu[at, 1024:1152].astype(F32)
        up_half = wgu[at, 1152:1280].astype(F32)
        even_mix = jnp.where(low, gate_half, pltpu.roll(up_half, 64, 1))
        odd_mix = jnp.where(low, pltpu.roll(gate_half, 64, 1), up_half)
        wgu[at, 1024:1152] = jnp.where(odd == 1, odd_mix, even_mix).astype(BF16)
        wgu[256 * q + 224 : 256 * q + 256, :] = jnp.zeros((32, 1280), BF16)
    for copy in over:
        copy.wait_recv()

    lane = lax.broadcasted_iota(jnp.int32, (8, X * 256), 1)
    pick = jnp.where(lax.rem(lane, 256) // 2 == 112, 1.0, 0.0).astype(BF16)
    for b in range(Z):
        squares_out[b] = nt(pick, normed[b // 2, b % 2])
    square_moves = [
        send(squares_out.at[lax.rem(z + k, Z)], squares_in.at[k], z_of[k]) for k in range(1, Z)
    ]

    def expand(b):
        rows = normed[b // 2, lax.rem(b, 2)]
        terms[b] = jnp.dot(rows, wgu[:, 0:1152], preferred_element_type=F32).astype(BF16)

    def block_at(j):
        far = 4 - (j + 1) // 2
        step = jnp.where(lax.rem(j, 2) == 1, far, Z - far)
        return lax.rem(z + step, Z)

    def expand_range(lo, hi):
        def body(j, _):
            expand(block_at(j))
            return 0

        lax.fori_loop(lo, hi, body, 0)

    def sub_rows(sub):
        return pl.ds(32 * sub, 32)

    got = {}
    expand_range(0, 1)
    far = lax.rem(z + 4, Z)
    for sub in (0, 1):
        got["r", 0, sub] = send(
            terms.at[far, sub_rows(sub)], from_left.at[0, sub_rows(sub)], right
        )
        got["l", 0, sub + 2] = send(
            terms.at[far, sub_rows(sub + 2)], from_right.at[0, sub_rows(sub + 2)], left
        )
    expand_range(1, 3)
    for i in (0, 1):
        got["r", 1, i + 2] = send(
            terms.at[lax.rem(z + 3, Z), sub_rows(i + 2)],
            from_left.at[1, sub_rows(i + 2)],
            right,
        )
        got["l", 1, i] = send(
            terms.at[lax.rem(z + 5, Z), sub_rows(i)], from_right.at[1, sub_rows(i)], left
        )
    wd_moves = []
    for k in (1, 2, 3):
        for src, dst in down_blocks(lax.rem(x + k, X), k):
            wd_moves.append(send(src, dst, x_of[k]))
    expand_range(3, 8)

    def pass_on(step, sub, way):
        buffer, device = (from_left, right) if way == "r" else (from_right, left)
        b = lax.rem(z + (4 - step if way == "r" else 4 + step), Z)
        got[way, step - 1, sub].wait_recv()
        at = sub_rows(sub)
        buffer[step - 1, at] = buffer[step - 1, at] + terms[b, at]
        got[way, step, sub] = send(buffer.at[step - 1, at], buffer.at[step, at], device)

    for i in (0, 1):
        pass_on(1, i, "r")
        pass_on(1, i + 2, "l")
    for step in (2, 3):
        for i in range(4):
            pass_on(step, (i + 2) % 4, "r")
            pass_on(step, i, "l")

    squares = squares_out[z]
    for k, copy in enumerate(square_moves):
        copy.wait_recv()
        squares = squares + squares_in[k + 1]
    row = lax.broadcasted_iota(jnp.int32, (128, 128), 0)
    lane = lax.broadcasted_iota(jnp.int32, (128, 128), 1)
    diagonal = jnp.where(row == lane, jnp.broadcast_to(squares[0:1, :], (128, 128)), 0.0)
    scale[...] = lax.rsqrt(jnp.sum(diagonal, axis=1, keepdims=True) * (1.0 / D) + EPS)

    def own_hidden(sub):
        at = sub_rows(sub)
        got["r", 3, sub].wait_recv()
        got["l", 3, sub].wait_recv()
        total = (
            terms[z, at].astype(F32) + from_left[3, at].astype(F32) + from_right[3, at].astype(F32)
        )
        factor = scale[at, :]
        gate, up = total[:, :512] * factor, total[:, 512:1024] * factor
        mixed = total[:, 1024:] * factor
        half = mixed / (1.0 + jnp.exp(-mixed)) * pltpu.roll(mixed, 64, 1)
        half = jnp.where(low, half, 0.0)
        half = jnp.where(odd == 1, pltpu.roll(half, 64, 1), half)
        hidden[z, at, 0:512] = (gate / (1.0 + jnp.exp(-gate)) * up).astype(BF16)
        hidden[z, at, 512:640] = half.astype(BF16)

    def contract(b):
        rows = hidden[b]
        for s in range(X):
            product = nt(rows, wd[s]).astype(BF16)
            part_d[b // 2, lax.rem(b, 2), lax.rem(x - s + X, X), :, 0:224] = product

    for copy in wd_moves:
        copy.wait_recv()
    first, finish = scatter(part_d, a1_d, b1_d, ra_d, rb_d, a2_d, b2_d, False)

    def in_order(parity):
        odd_hops = lax.rem(z + 1 + parity, 2) == 0
        steps = ((1, 0), (Z - 1, 2), (3, Z - 2), (Z - 3, 4))
        return [lax.rem(z + jnp.where(odd_hops, a, b), Z) // 2 for a, b in steps]

    to_sibling, from_sibling = in_order(1 - c), in_order(c)
    swaps = []
    met = []

    def swap(slot):
        swaps.append(send(part_d.at[to_sibling[slot], 1 - c], sib_d.at[slot], sibling))

    def add_swapped(slot):
        swaps[slot].wait_recv()
        at = from_sibling[slot]
        part_d[at, c] = part_d[at, c] + sib_d[slot]
        first(at)

    def hidden_arrived(zi):
        if not met:
            contract(z)
        contract(zi)
        met.append(zi)
        if len(met) == 4:
            swap(0)
            swap(1)
        elif len(met) == 6:
            swap(2)
            add_swapped(0)
            add_swapped(1)
        elif len(met) == 7:
            swap(3)
            add_swapped(2)

    ring_gather(lambda zi, sub: hidden.at[zi, sub_rows(sub)], own_hidden, hidden_arrived, (0, 2, 1, 3))
    add_swapped(3)
    halves = finish()
    for h, mlp in enumerate(halves):
        at = pl.ds(64 * h, 64)
        out[at, :] = (stream[at, :] + mlp).astype(BF16)
    for copy in sent:
        copy.wait_send()


COPIES = 240


def layer(hv, resid, gain, w_gate, w_up, wgu, w_o, w_down):
    vmem = pl.BlockSpec(memory_space=pltpu.VMEM)
    hbm = pl.BlockSpec(memory_space=pl.ANY)
    halves = [
        pltpu.VMEM((3, 4, 64, 256), BF16),
        pltpu.VMEM((3, 4, 64, 256), BF16),
        pltpu.VMEM((4, 64, 256), BF16),
        pltpu.VMEM((4, 64, 256), BF16),
        pltpu.VMEM((3, 64, 256), BF16),
        pltpu.VMEM((3, 64, 256), BF16),
    ]
    return pl.pallas_call(
        layer_kernel,
        out_shape=jax.ShapeDtypeStruct((128, 224), BF16),
        in_specs=[pl.BlockSpec(memory_space=pltpu.HBM)] + [vmem] * 2 + [hbm] * 6,
        out_specs=vmem,
        scratch_shapes=[
            pltpu.VMEM((Z, X, 32, 512), BF16),
            pltpu.VMEM((Y, 2, 128, X * 256), BF16),
            pltpu.VMEM((X * 256, 1280), BF16),
            pltpu.VMEM((X, 224, 512), BF16),
            pltpu.VMEM((X, 224, 640), BF16),
            pltpu.VMEM((Y, 2, X, 128, 256), BF16),
            pltpu.VMEM((Y, 2, X, 128, 256), BF16),
            pltpu.VMEM((Y, X, 128, 256), BF16),
            pltpu.VMEM((Y, X, 128, 256), BF16),
            *halves,
            *halves,
            pltpu.VMEM((Z, 128, 1152), BF16),
            pltpu.VMEM((4, 128, 1152), BF16),
            pltpu.VMEM((4, 128, 1152), BF16),
            pltpu.VMEM((Z, 128, 640), BF16),
            pltpu.VMEM((128, 224), F32),
            pltpu.VMEM((Z, 8, 128), F32),
            pltpu.VMEM((Z, 8, 128), F32),
            pltpu.VMEM((128, 1), F32),
            pltpu.SemaphoreType.DMA((COPIES,)),
            pltpu.SemaphoreType.DMA((COPIES,)),
            pltpu.SemaphoreType.DMA((11,)),
        ],
        compiler_params=pltpu.CompilerParams(
            collective_id=0, has_side_effects=True, vmem_limit_bytes=52 * 2**20
        ),
    )(hv, resid, gain, w_gate, w_up, *wgu, w_o, w_down)


def cut_kernel(w_gate, w_up, piece1, piece3, sem):
    x = lax.axis_index("dp") // Z
    copies = []
    for i, (s, piece) in enumerate(((1, piece1), (3, piece3))):
        there = lax.rem(x + s, X)
        first, odd = (9 * there) // 2, lax.rem(there, 2)
        whole = pl.ds(pl.multiple_of((first + odd) * 128, 128), 512)
        half = pl.ds(pl.multiple_of((first + 4 * (1 - odd)) * 128, 128), 128)
        for j, w in enumerate((w_gate, w_up)):
            copies.append(
                pltpu.make_async_copy(
                    w.at[:, whole], piece.at[:, pl.ds(512 * j, 512)], sem.at[i, 2 * j]
                )
            )
            copies.append(
                pltpu.make_async_copy(
                    w.at[:, half], piece.at[:, pl.ds(1024 + 128 * j, 128)], sem.at[i, 2 * j + 1]
                )
            )
    for copy in copies:
        copy.start()
    for copy in copies:
        copy.wait()


def spread(w_gate, w_up):
    hbm = pl.BlockSpec(memory_space=pl.ANY)
    pieces = pl.pallas_call(
        cut_kernel,
        out_shape=[jax.ShapeDtypeStruct((224, 1280), BF16)] * 2,
        in_specs=[hbm] * 2,
        out_specs=[pl.BlockSpec(memory_space=pltpu.VMEM)] * 2,
        scratch_shapes=[pltpu.SemaphoreType.DMA((2, 4))],
    )(w_gate, w_up)
    got = []
    for s, piece in zip((1, 3), pieces):
        pairs = [(i, (i // Z + s) % X * Z + i % Z) for i in range(X * Z)]
        got.append(lax.ppermute(piece, "dp", pairs))
    return got


def local(
    q_lat,
    q_rope,
    fresh_lat,
    fresh_rope,
    cache_lat,
    cache_rope,
    page_table,
    hit_len,
    fresh_len,
    w_uv,
    w_o,
    resid,
    norm_gain,
    w_gate,
    w_up,
    w_down,
):
    wgu = spread(w_gate, w_up)
    head_values = attend(
        q_lat,
        q_rope,
        fresh_lat,
        fresh_rope,
        cache_lat,
        cache_rope,
        page_table,
        hit_len,
        fresh_len,
        w_uv,
    )
    return layer(
        head_values, resid, norm_gain.reshape(1, -1), w_gate, w_up, wgu, w_o.T, w_down.T
    )


def solution(mesh):
    placed = (
        P("dp", "tensor"),
        P("dp", "tensor"),
        P("dp", None),
        P("dp", None),
        P("dp", None, None),
        P("dp", None, None),
        P("dp", None, None),
        P("dp", None),
        P("dp", None),
        P("tensor", None, None),
        P("tensor", "dp"),
        P("tensor", "dp"),
        P("dp"),
        P("dp", "tensor"),
        P("dp", "tensor"),
        P("tensor", "dp"),
    )
    return jax.shard_map(
        local, mesh=mesh, in_specs=placed, out_specs=P("tensor", "dp"), check_vma=False
    )
```
